256 devices in a mesh: blk: 32 (over z, y_lo, core), tp: 8 (over x, y_hi).
Axes of the slice: x: 4, y: 4 (y_hi: 2, y_lo: 2; y = y_hi * 2 + y_lo), z: 8, core: 2. Of those that a mesh axis runs over, the one named last changes fastest.
Arguments:
- scan_input: bfloat16 [16384, 8192], P('blk', 'tp'), may hold values from -6 to 6
- gate_input: bfloat16 [16384, 8192], P('blk', 'tp'), may hold values from -20 to 20
- state_proj: bfloat16 [16384, 2, 2048], P('blk', None, 'tp'), may hold values from -4 to 4
- step_raw: bfloat16 [16384, 128], P('blk', 'tp')
- log_rate: float32 [128], P('tp'), may hold values from -9 to -2
- step_bias: float32 [128], P('tp'), may hold values from -0.5 to 0.5
- skip_gain: float32 [128], P('tp'), may hold values from 0.5 to 2
- norm_gain: float32 [8192], P('tp'), may hold values from 0.1 to 1.9
- out_proj: bfloat16 [4096, 8192], P('blk', 'tp'), may hold values from -0.0625 to 0.0625
- out_cotangent: bfloat16 [16384, 4096], P('blk', 'tp'), may hold values from -6 to 6
Outputs:
- input_grad: bfloat16 [16384, 8192], P('blk', 'tp')
- gate_grad: bfloat16 [16384, 8192], P('blk', 'tp')
- state_proj_grad: bfloat16 [16384, 2, 2048], P('blk', None, 'tp')
- step_grad: float32 [16384, 128], P('blk', 'tp')
- out_proj_grad: float32 [4096, 8192], P('blk', 'tp')
- log_rate_grad: float32 [128], P('tp')
- step_bias_grad: float32 [128], P('tp')
- skip_grad: float32 [128], P('tp')
- norm_gain_grad: float32 [8192], P('tp')
The draws below stay inside these ranges and needn't reach their ends.
All inputs are finite; a program needn't handle non-finite values.
Results may differ from the reference program's by a relative error of at most 0.009.
Values may be sent and summed in bfloat16 or wider, within the bound.
No kernel may reach another device: no remote copies, remote signals or barrier semaphores. Data moves between devices by JAX's collectives and lax.ppermute only.
A program may use at most 128 MiB of HBM per device.

```python
import math
from functools import partial
import jax
import jax.numpy as jnp
from jax import lax

D = 4096
HEADS = 128
STATE = 256
GROUPS = 8
LOCAL_POSITIONS = 512
INNER = 8192
GLOBAL_POSITIONS = 16384


def head_rates(key, fast_share):
    first_key, second_key, prng_seed_extra = jax.random.split(key, 3)
    is_fast = jax.random.bernoulli(first_key, fast_share, (HEADS,))
    quick_rates = jnp.exp(jax.random.uniform(second_key, (HEADS,), jnp.float32, math.log(1.0 / 50.0), math.log(1.0 / 30.0)))
    slow_rates = jax.random.uniform(prng_seed_extra, (HEADS,), jnp.float32, 0.8, 1.6) / LOCAL_POSITIONS
    return jnp.where(is_fast, quick_rates, slow_rates)


def draw_log_rate(key, part):
    fast_share = 0.5
    channel_forget_factors = head_rates(key, fast_share)
    return jnp.log(channel_forget_factors)


def draw_step_raw(key, part):
    fast_share = 0.5
    channel_forget_factors = head_rates(key, fast_share)
    key = jax.random.fold_in(key, 41)
    first_key, second_key, prng_seed_extra, fourth_key = jax.random.split(key, 4)
    stochastic_perturbation = jnp.clip(0.5 * jax.random.normal(first_key, (GLOBAL_POSITIONS, HEADS), jnp.float32), -1.5, 1.5)
    beginning_positions = jax.random.uniform(second_key, (GLOBAL_POSITIONS // LOCAL_POSITIONS, 1, 1), jnp.float32, -0.5, 0.5)
    beginning_positions = jnp.broadcast_to(beginning_positions, (GLOBAL_POSITIONS // LOCAL_POSITIONS, LOCAL_POSITIONS, 1)).reshape(GLOBAL_POSITIONS, 1)
    cluster_lengths = jax.random.bernoulli(prng_seed_extra, 3.0 / LOCAL_POSITIONS, (GLOBAL_POSITIONS, 1))
    objective_scores = jax.random.uniform(fourth_key, (GLOBAL_POSITIONS, HEADS), jnp.float32, 0.2, 0.45)
    return (stochastic_perturbation + beginning_positions + jnp.where(cluster_lengths, objective_scores / channel_forget_factors, 0.0)).astype(jnp.bfloat16)


def draw_gate_input(key, part):
    key = jax.random.fold_in(key, 23)
    first_key, second_key, prng_seed_extra = jax.random.split(key, 3)
    standard = jnp.clip(jax.random.normal(first_key, (GLOBAL_POSITIONS, INNER), jnp.float32), -2.5, 2.5)
    columns = jnp.exp(jax.random.uniform(second_key, (INNER,), jnp.float32, math.log(0.4), math.log(4.0)))
    row_scales = jnp.exp(jax.random.uniform(prng_seed_extra, (GLOBAL_POSITIONS, 1), jnp.float32, math.log(0.5), math.log(2.0)))
    return (standard * columns * row_scales).astype(jnp.bfloat16)


def raised(values, own_key, source, target, parts, factor):
    def block_of(dim):
        return (jnp.arange(values.shape[dim]) // (values.shape[dim] // parts)).reshape((-1,) + (1,) * (values.ndim - 1 - dim))

    first = jax.random.permutation(own_key, parts)[block_of(target)]
    far = (block_of(target) + parts // 2) % parts
    return jnp.where((block_of(source) == first) | (block_of(source) == far), factor * values, values)


def levels(stream_key, shape, pieces, low, high):
    factor_of = 1.0
    for position, shards_of in pieces:
        steps = jax.random.uniform(jax.random.fold_in(jax.random.fold_in(stream_key, 6), position), (shards_of,), jnp.float32, low / len(pieces), high / len(pieces))
        factor_of = factor_of * jnp.repeat(jnp.exp(steps), shape[position] // shards_of).reshape((-1,) + (1,) * (len(shape) - 1 - position))
    return factor_of


def gaussian(own_key, extent, scale, bound, pieces=(), held_as=jnp.bfloat16):
    entries = scale * jax.random.normal(own_key, extent, jnp.float32)
    if pieces:
        entries = entries * levels(own_key, extent, pieces, -0.22, 0.18)
    return jnp.clip(entries, -bound, bound).astype(held_as)


def noise_with(stream_key, dims, width, bound, cuts, heavy, held_as=jnp.bfloat16):
    values = width * jax.random.normal(stream_key, dims, jnp.float32)
    if cuts:
        values = values * levels(stream_key, dims, cuts, -0.22, 0.18)
    return jnp.clip(raised(values, jax.random.fold_in(stream_key, 3), *heavy), -bound, bound).astype(held_as)


def setup_inputs(seed: int = 0) -> dict:
    seeds = jax.random.split(jax.random.key(seed), 11)
    scan_input = gaussian(seeds[0], (GLOBAL_POSITIONS, INNER), 1.0, 6.0, ((0, 32), (1, 8)))
    gate_input = draw_gate_input(jax.random.fold_in(seeds[10], 71), 0)
    state_proj = gaussian(seeds[2], (GLOBAL_POSITIONS, 2, GROUPS * STATE), (STATE ** -0.25), 4.0, ((0, 32), (2, 8)))
    step_raw = draw_step_raw(jax.random.fold_in(seeds[10], 71), 0)
    log_rate = draw_log_rate(jax.random.fold_in(seeds[10], 71), 0)
    step_bias = jnp.clip(jax.random.uniform(seeds[5], (HEADS,), jnp.float32, -0.5, 0.5) * levels(seeds[5], (HEADS,), ((0, 8),), -0.4, 0.0), -0.5, 0.5)
    skip_gain = jnp.clip(0.5 + 1.5 * jax.random.uniform(seeds[6], (HEADS,), jnp.float32) ** levels(seeds[6], (HEADS,), ((0, 8),), -0.2, 0.2), 0.5, 2.0)
    norm_gain = jnp.clip(1.0 + 0.18 * jax.random.normal(seeds[7], (INNER,), jnp.float32), 0.1, 1.9)
    out_proj = gaussian(seeds[8], (D, INNER), INNER ** -0.5, 0.0625, ((0, 32), (1, 8)))
    out_cotangent = noise_with(seeds[9], (GLOBAL_POSITIONS, D), 1.0, 6.0, ((0, 32), (1, 8)), (0, 1, 32, 2.75))
    return {"scan_input": scan_input, "gate_input": gate_input, "state_proj": state_proj, "step_raw": step_raw, "log_rate": log_rate, "step_bias": step_bias, "skip_gain": skip_gain, "norm_gain": norm_gain, "out_proj": out_proj, "out_cotangent": out_cotangent}


precise = lax.Precision.HIGHEST

def serial_states(local_states, totals):

    def advance(carried, inputs_now):
        portion, overall = inputs_now
        return (jnp.exp(overall)[:, :, None, None] * carried + portion, carried)
    _, entering = lax.scan(advance, jnp.zeros_like(local_states[0]), (local_states, totals))
    return entering

def mixer(values, gates, projections, raw_steps, log_rate, step_bias, skip_gain, norm_gain, per_group, block_len):
    tokens, inner_width = values.shape
    head_count = raw_steps.shape[1]
    head_width = inner_width // head_count
    groups = head_count // per_group
    state_size = projections.shape[2] // groups
    blocks = tokens // block_len
    step_size = jax.nn.softplus(raw_steps + step_bias)
    decay_log = -step_size * jnp.exp(log_rate)
    running = jnp.cumsum(decay_log.reshape(blocks, block_len, head_count), axis=1)
    driven = (values.reshape(tokens, head_count, head_width) * step_size[:, :, None]).reshape(blocks, block_len, groups, per_group, head_width)
    b_part = projections[:, 0, :].reshape(blocks, block_len, groups, state_size)
    c_part = projections[:, 1, :].reshape(blocks, block_len, groups, state_size)
    intersection = jnp.einsum('cign,cjgn->cgij', c_part, b_part, precision=precise)
    run_heads = jnp.swapaxes(running, 1, 2).reshape(blocks, groups, per_group, block_len)
    differences = run_heads[..., :, None] - run_heads[..., None, :]
    causal = jnp.arange(block_len)[:, None] >= jnp.arange(block_len)[None, :]
    weights = jnp.where(causal, jnp.exp(jnp.where(causal, differences, 0.0)), 0.0) * intersection[:, :, None]
    inside = jnp.einsum('cgkij,cjgkp->cigkp', weights, driven, precision=precise)
    to_end = jnp.exp(running[:, -1:, :] - running).reshape(blocks, block_len, groups, per_group)
    local_states = jnp.einsum('cjgkp,cjgk,cjgn->cgkpn', driven, to_end, b_part, precision=precise)
    totals = running[:, -1, :].reshape(blocks, groups, per_group)
    entering = serial_states(local_states, totals)
    from_before = jnp.einsum('cign,cgkpn->cigkp', c_part, entering, precision=precise)
    from_before = from_before * jnp.exp(running).reshape(blocks, block_len, groups, per_group)[..., None]
    scan_out = (inside + from_before).reshape(tokens, head_count, head_width)
    scan_out = scan_out + skip_gain[:, None] * values.reshape(tokens, head_count, head_width)
    gated_out = scan_out.reshape(tokens, inner_width) * jax.nn.silu(gates)
    grouped = gated_out.reshape(tokens, groups, inner_width // groups)
    mean_sq = lax.optimization_barrier(jnp.mean(grouped * grouped, axis=2, keepdims=True))
    return (grouped * lax.rsqrt(mean_sq + 1e-05)).reshape(tokens, inner_width) * norm_gain

def reference(scan_input, gate_input, state_proj, step_raw, log_rate, step_bias, skip_gain, norm_gain, out_proj, out_cotangent):
    group_heads = HEADS // GROUPS
    block_len = 256 if LOCAL_POSITIONS % 256 == 0 else LOCAL_POSITIONS
    sequences = GLOBAL_POSITIONS // LOCAL_POSITIONS
    forward = partial(mixer, per_group=group_heads, block_len=block_len)

    def by_sequence(array):
        return array.reshape((sequences, LOCAL_POSITIONS) + array.shape[1:])

    def advance(carried, inputs_now):
        values, gates, projections, raw_steps, cotangent = inputs_now
        normed, pullback = jax.vjp(forward, values.astype(jnp.float32), gates.astype(jnp.float32), projections.astype(jnp.float32), raw_steps.astype(jnp.float32), log_rate, step_bias, skip_gain, norm_gain)
        normed_low = normed.astype(jnp.bfloat16)
        normed_cot = jnp.dot(cotangent, out_proj, preferred_element_type=jnp.float32)
        term = lax.dot_general(cotangent, normed_low, (((0,), (0,)), ((), ())), preferred_element_type=jnp.float32)
        gradients = pullback(normed_cot)
        summed = (carried[0] + term, carried[1] + gradients[4], carried[2] + gradients[5], carried[3] + gradients[6], carried[4] + gradients[7])
        return (summed, (gradients[0].astype(jnp.bfloat16), gradients[1].astype(jnp.bfloat16), gradients[2].astype(jnp.bfloat16), gradients[3]))
    initial = (jnp.zeros((D, INNER), jnp.float32), jnp.zeros((HEADS,), jnp.float32), jnp.zeros((HEADS,), jnp.float32), jnp.zeros((HEADS,), jnp.float32), jnp.zeros((INNER,), jnp.float32))
    summed, stacked = lax.scan(advance, initial, (by_sequence(scan_input), by_sequence(gate_input), by_sequence(state_proj), by_sequence(step_raw), by_sequence(out_cotangent)))
    norm_scale = 1.0 / math.sqrt(GLOBAL_POSITIONS)
    return (stacked[0].reshape(GLOBAL_POSITIONS, INNER), stacked[1].reshape(GLOBAL_POSITIONS, INNER), stacked[2].reshape(GLOBAL_POSITIONS, 2, GROUPS * STATE), stacked[3].reshape(GLOBAL_POSITIONS, HEADS), summed[0] * norm_scale, summed[1] * norm_scale, summed[2] * norm_scale, summed[3] * norm_scale, summed[4] * norm_scale)
```

```python
import math

import jax
import jax.numpy as jnp
from jax import lax
from jax.experimental import pallas as pl
from jax.experimental.pallas import tpu as pltpu
from jax.sharding import PartitionSpec as P

TOKENS = 512
CHANNELS = 1024
HEADS = 16
WIDTH = 64
STATE = 256
CHUNK = 128
CHUNKS = TOKENS // CHUNK
LANES = 128
PAIRS = HEADS // 2
EPS = 1e-05

F32 = jnp.float32
BF16 = jnp.bfloat16


def dot(a, b, over=(1, 0)):
    return lax.dot_general(
        a, b, (((over[0],), (over[1],)), ((), ())), preferred_element_type=F32
    )


def three_parts(v):
    hi = v.astype(BF16).astype(F32)
    rest = v - hi
    mid = rest.astype(BF16).astype(F32)
    return hi, mid, rest - mid


def packed(v):
    hi, mid, low = three_parts(v)
    return (hi + pltpu.roll(mid, HEADS, 1) + pltpu.roll(low, 2 * HEADS, 1)).astype(BF16)


def halves(v):
    hi = v.astype(BF16)
    return hi, (v - hi.astype(F32)).astype(BF16)


def folded(v):
    middle = v.shape[1] // 2
    return v[:, :middle] + v[:, middle:]


def triangle(lower):
    i = lax.broadcasted_iota(jnp.int32, (CHUNK, CHUNK), 0)
    j = lax.broadcasted_iota(jnp.int32, (CHUNK, CHUNK), 1)
    return i >= j if lower else i <= j


def picker(pair, width):
    row = lax.broadcasted_iota(jnp.int32, (LANES, 2 * width), 0)
    col = lax.broadcasted_iota(jnp.int32, (LANES, 2 * width), 1)
    head = 2 * pair + col // width
    return jnp.where((row % HEADS == head) & (row < 3 * HEADS), 1.0, 0.0).astype(BF16)


def softplus(v):
    return jnp.maximum(v, 0.0) + jnp.log1p(jnp.exp(-jnp.abs(v)))


def head_lanes():
    return lax.broadcasted_iota(jnp.int32, (TOKENS, LANES), 1) < HEADS


def steps_of(raw_ref, bias_ref, rate_ref):
    step = jnp.where(head_lanes(), softplus(raw_ref[...].astype(F32) + bias_ref[...]), 0.0)
    return step, -step * jnp.exp(rate_ref[...])


def prepare(raw_ref, raw_t_ref, bias_ref, rate_ref, bias_t_ref, rate_t_ref, b_ref, c_ref,
            step_pack, run_pack, run_rows, step_rows, overlap):
    step, decay = steps_of(raw_ref, bias_ref, rate_ref)
    step_pack[...] = packed(step)
    lower = jnp.where(triangle(True), 1.0, 0.0).astype(BF16)
    upper = jnp.where(triangle(False), 1.0, 0.0).astype(BF16)
    decay_pack = packed(decay)
    keep = lax.broadcasted_iota(jnp.int32, (CHUNK, LANES), 1) < HEADS
    step_t = softplus(raw_t_ref[...].astype(F32) + bias_t_ref[...])
    decay_t = three_parts(-step_t * jnp.exp(rate_t_ref[...]))
    for pair in range(PAIRS):
        step_rows[pair] = step_t[2 * pair : 2 * pair + 2, :]
    for c in range(CHUNKS):
        rows = slice(c * CHUNK, (c + 1) * CHUNK)
        total = dot(lower, decay_pack[rows])
        total = total + pltpu.roll(total, LANES - HEADS, 1) + pltpu.roll(total, LANES - 2 * HEADS, 1)
        run_pack[rows, :] = packed(jnp.where(keep, total, 0.0))
        across = sum(dot(part[:, rows].astype(BF16), upper) for part in decay_t)
        for pair in range(PAIRS):
            run_rows[pair, :, rows] = across[2 * pair : 2 * pair + 2, :]
        overlap[c] = jnp.where(triangle(True), dot(c_ref[rows, :], b_ref[rows, :], (1, 1)), 0.0)


def first_half():
    return lax.broadcasted_iota(jnp.int32, (CHUNK, LANES), 1) < WIDTH


def apart(v):
    first = first_half()
    return jnp.concatenate([jnp.where(first, v, 0.0), jnp.where(first, 0.0, v)], axis=0).astype(BF16)


def decays(columns, run_rows, pair, rows):
    out = []
    for h in range(2):
        across = run_rows[pair, h : h + 1, rows]
        out.append(jnp.exp(jnp.minimum(columns[:, h * CHUNK : (h + 1) * CHUNK] - across, 0.0)))
    return out


def forward_kernel(x_ref, g_ref, b_ref, bt_ref, c_ref, raw_ref, raw_t_ref, bias_ref, rate_ref,
                   bias_t_ref, rate_t_ref, skip_ref, gain_ref,
                   low_ref, scan_ref, gated_ref, state_ref, scale_ref,
                   step_pack, run_pack, run_rows, step_rows, overlap, squares):
    pair = pl.program_id(0)

    @pl.when(pair == 0)
    def _():
        prepare(raw_ref, raw_t_ref, bias_ref, rate_ref, bias_t_ref, rate_t_ref, b_ref, c_ref,
                step_pack, run_pack, run_rows, step_rows, overlap)
        squares[...] = jnp.zeros_like(squares)

    narrow, wide = picker(pair, WIDTH), picker(pair, CHUNK)
    skip = skip_ref[:, pl.ds(pl.multiple_of(pair * LANES, LANES), LANES)]
    state = None
    for c in range(CHUNKS):
        rows = slice(c * CHUNK, (c + 1) * CHUNK)
        x = x_ref[rows, :].astype(F32)
        step = dot(step_pack[rows, :], narrow)
        run = dot(run_pack[rows, :], narrow)
        columns = dot(run_pack[rows, :], wide)
        weights = []
        for h, one in enumerate(decays(columns, run_rows, pair, rows)):
            weights.append(halves(one * overlap[c] * step_rows[pair, h : h + 1, rows]))
        x_apart = apart(x)
        y = dot(
            jnp.concatenate([weights[h][part] for part in range(2) for h in range(2)], axis=1),
            jnp.concatenate([x_apart, x_apart], axis=0),
        )
        if c > 0:
            state_ref[0, c - 1] = state
            held = jnp.concatenate(halves(state), axis=1)
            y = y + jnp.exp(run) * folded(dot(c_ref[rows, :], held))
        if c < CHUNKS - 1:
            end = run[CHUNK - 1 :, :]
            fresh = jnp.concatenate(halves(x * step * jnp.exp(end - run)), axis=1)
            local = folded(dot(bt_ref[:, rows], fresh))
            state = local if c == 0 else jnp.exp(end) * state + local
        scan_ref[rows, :] = y
        g = g_ref[rows, :].astype(F32)
        gated = (y + skip * x) * (g / (1.0 + jnp.exp(-g)))
        gated_ref[rows, pl.ds(pl.multiple_of(pair * LANES, LANES), LANES)] = gated
        squares[rows, :] += gated * gated

    @pl.when(pair == PAIRS - 1)
    def _():
        for c in range(CHUNKS):
            rows = slice(c * CHUNK, (c + 1) * CHUNK)
            mean = jnp.sum(squares[rows, :], axis=1, keepdims=True) * (1.0 / CHANNELS)
            scale = lax.rsqrt(mean + EPS)
            scale_ref[rows, :] = jnp.broadcast_to(scale, (CHUNK, LANES))
            low_ref[rows, :] = (gated_ref[rows, :] * scale * gain_ref[...]).astype(BF16)


def backward_kernel(x_ref, g_ref, cot_ref, scan_ref, state_ref, scale_ref, pull_ref,
                    b_ref, c_ref, ct_ref, raw_ref, raw_t_ref, bias_ref, rate_ref,
                    bias_t_ref, rate_t_ref, skip_ref, gain_ref,
                    dx_ref, dg_ref, db_ref, dc_ref, step_ref, small_ref,
                    step_pack, run_pack, run_rows, step_rows, overlap, d_overlap, d_b, d_c, flow, direct, lanes):
    pair = pl.program_id(0)

    @pl.when(pair == 0)
    def _():
        prepare(raw_ref, raw_t_ref, bias_ref, rate_ref, bias_t_ref, rate_t_ref, b_ref, c_ref,
                step_pack, run_pack, run_rows, step_rows, overlap)
        for held in (d_overlap, d_b, d_c, flow, direct, lanes):
            held[...] = jnp.zeros_like(held)

    narrow, wide = picker(pair, WIDTH), picker(pair, CHUNK)
    here = pl.ds(pl.multiple_of(pair * LANES, LANES), LANES)
    skip, gain = skip_ref[:, here], gain_ref[:, here]
    first = first_half()
    lane = lax.broadcasted_iota(jnp.int32, (CHUNK, LANES), 1)

    def by_head(v):
        one = jnp.sum(jnp.where(first, v, 0.0), axis=1, keepdims=True)
        two = jnp.sum(jnp.where(first, 0.0, v), axis=1, keepdims=True)
        return jnp.where(lane == 2 * pair, one, jnp.where(lane == 2 * pair + 1, two, 0.0))

    d_state = None
    skip_sum = jnp.zeros((1, LANES), F32)
    for c in reversed(range(CHUNKS)):
        rows = slice(c * CHUNK, (c + 1) * CHUNK)
        x = x_ref[rows, :].astype(F32)
        g = g_ref[rows, :].astype(F32)
        scan = scan_ref[rows, :]
        out = scan + skip * x
        sig = 1.0 / (1.0 + jnp.exp(-g))
        silu = g * sig
        d_gated = scale_ref[rows, :] * gain * cot_ref[rows, :] - out * silu * pull_ref[rows, :]
        dy = d_gated * silu
        dg_ref[rows, :] = (d_gated * out * (sig + silu * (1.0 - sig))).astype(BF16)
        skip_sum = skip_sum + jnp.sum(dy * x, axis=0, keepdims=True)

        step = dot(step_pack[rows, :], narrow)
        run = dot(run_pack[rows, :], narrow)
        columns = dot(run_pack[rows, :], wide)
        driven = x * step
        dy_hi, dy_low = (apart(part.astype(F32)) for part in halves(dy))
        factor = decays(columns, run_rows, pair, rows)
        products = dot(
            jnp.concatenate([dy_hi, dy_low], axis=1),
            jnp.concatenate([x_ref[rows, :], x_ref[rows, :]], axis=1),
            (1, 1),
        )
        step_row = step_rows[pair, :, rows]
        d_overlap[c] += (
            factor[0] * products[:CHUNK] * step_row[:1] + factor[1] * products[CHUNK:] * step_row[1:]
        )
        weights = [halves(one * overlap[c]) for one in factor]
        weights_hi = jnp.concatenate([one[0] for one in weights], axis=0)
        weights_low = jnp.concatenate([one[1] for one in weights], axis=0)
        d_driven = folded(dot(weights_hi, jnp.concatenate([dy_hi, dy_low], axis=1), (0, 0)))
        d_driven = d_driven + dot(weights_low, dy_hi, (0, 0))
        entering_hi, entering_low = halves(dy * jnp.exp(run))
        entering = jnp.concatenate([entering_hi, entering_low], axis=1)
        end = run[CHUNK - 1 :, :]
        if c > 0:
            held = state_ref[0, c - 1]
            held_hi, held_low = halves(held)
            d_c[rows, :] += dot(
                entering, jnp.concatenate([held_hi, held_hi], axis=1), (1, 1)
            ) + dot(entering_hi, held_low, (1, 1))
        if c < CHUNKS - 1:
            to_end = jnp.exp(end - run)
            d_hi, d_low = halves(d_state)
            from_state = to_end * folded(
                dot(b_ref[rows, :], jnp.concatenate([d_hi, d_low], axis=1))
            )
            fresh_hi, fresh_low = halves(driven * to_end)
            d_b[rows, :] += dot(
                jnp.concatenate([fresh_hi, fresh_low], axis=1),
                jnp.concatenate([d_hi, d_hi], axis=1),
                (1, 1),
            ) + dot(fresh_hi, d_low, (1, 1))
            crossing = jnp.sum(driven * from_state, axis=0, keepdims=True)
            if c > 0:
                carried = jnp.sum(held * d_state, axis=0, keepdims=True)
                crossing = crossing + jnp.exp(end) * carried
            lanes[c : c + 1, here] = crossing
            d_driven = d_driven + from_state
        if c > 0:
            back = folded(dot(ct_ref[:, rows], entering))
            d_state = back if d_state is None else jnp.exp(end) * d_state + back
        flow[rows, :] += by_head(dy * scan - driven * d_driven)
        direct[rows, :] += by_head(x * d_driven)
        dx_ref[rows, :] = (step * d_driven + skip * dy).astype(BF16)
    lanes[CHUNKS : CHUNKS + 1, here] = skip_sum

    @pl.when(pair == PAIRS - 1)
    def _():
        channel = lax.broadcasted_iota(jnp.int32, (CHANNELS, LANES), 0) // WIDTH
        head = lax.broadcasted_iota(jnp.int32, (CHANNELS, LANES), 1)
        gather = jnp.where(channel == head, 1.0, 0.0).astype(BF16)
        heads = sum(dot(part.astype(BF16), gather) for part in three_parts(lanes[...]))
        step_all, decay_all = steps_of(raw_ref, bias_ref, rate_ref)
        rate = jnp.exp(rate_ref[...])
        upper = jnp.where(triangle(False), 1.0, 0.0).astype(BF16)
        keep = lane < HEADS
        rate_sum = jnp.zeros((1, LANES), F32)
        bias_sum = jnp.zeros((1, LANES), F32)
        for c in range(CHUNKS):
            rows = slice(c * CHUNK, (c + 1) * CHUNK)
            d_decay = sum(dot(upper, part.astype(BF16)) for part in three_parts(flow[rows, :]))
            d_decay = d_decay + heads[c : c + 1, :]
            d_step = direct[rows, :] - d_decay * rate
            before = raw_ref[rows, :].astype(F32) + bias_ref[...]
            d_raw = jnp.where(keep, d_step / (1.0 + jnp.exp(-before)), 0.0)
            step_ref[rows, :] = d_raw[:, :HEADS]
            bias_sum = bias_sum + jnp.sum(d_raw, axis=0, keepdims=True)
            rate_sum = rate_sum + jnp.sum(
                jnp.where(keep, d_decay * decay_all[rows], 0.0), axis=0, keepdims=True
            )
            d_hi, d_low = halves(jnp.where(triangle(True), d_overlap[c], 0.0))
            dc_ref[rows, :] = (
                d_c[rows, :] + dot(d_hi, b_ref[rows, :]) + dot(d_low, b_ref[rows, :])
            ).astype(BF16)
            db_ref[rows, :] = (
                d_b[rows, :] + dot(d_hi, c_ref[rows, :], (0, 0)) + dot(d_low, c_ref[rows, :], (0, 0))
            ).astype(BF16)
        small_ref[...] = jnp.concatenate(
            [rate_sum, bias_sum, heads[CHUNKS : CHUNKS + 1, :], jnp.zeros((5, LANES), F32)], axis=0
        )


def whole(shape):
    return pl.BlockSpec(shape, lambda *_: (0,) * len(shape))


def by_pair(rows):
    return pl.BlockSpec((rows, LANES), lambda p, *_: (0, p))


VMEM_LIMIT = 56 * 1024 * 1024

TABLES = [
    pltpu.VMEM((TOKENS, LANES), BF16),
    pltpu.VMEM((TOKENS, LANES), BF16),
    pltpu.VMEM((PAIRS, 2, TOKENS), F32),
    pltpu.VMEM((PAIRS, 2, TOKENS), F32),
    pltpu.VMEM((CHUNKS, CHUNK, CHUNK), F32),
]

PARAMETERS = [
    whole((TOKENS, LANES)),
    whole((HEADS, TOKENS)),
    whole((1, LANES)),
    whole((1, LANES)),
    whole((HEADS, 1)),
    whole((HEADS, 1)),
    whole((1, CHANNELS)),
    whole((1, CHANNELS)),
]


def scan_forward(x, g, b, bt, c, parameters):
    return pl.pallas_call(
        forward_kernel,
        grid=(PAIRS,),
        in_specs=[
            by_pair(TOKENS),
            by_pair(TOKENS),
            whole((TOKENS, STATE)),
            whole((STATE, TOKENS)),
            whole((TOKENS, STATE)),
        ]
        + PARAMETERS,
        out_specs=[
            whole((TOKENS, CHANNELS)),
            by_pair(TOKENS),
            whole((TOKENS, CHANNELS)),
            pl.BlockSpec((1, CHUNKS - 1, STATE, LANES), lambda p: (p, 0, 0, 0)),
            whole((TOKENS, LANES)),
        ],
        out_shape=[
            jax.ShapeDtypeStruct((TOKENS, CHANNELS), BF16),
            jax.ShapeDtypeStruct((TOKENS, CHANNELS), F32),
            jax.ShapeDtypeStruct((TOKENS, CHANNELS), F32),
            jax.ShapeDtypeStruct((PAIRS, CHUNKS - 1, STATE, LANES), F32),
            jax.ShapeDtypeStruct((TOKENS, LANES), F32),
        ],
        scratch_shapes=TABLES + [pltpu.VMEM((TOKENS, LANES), F32)],
        compiler_params=pltpu.CompilerParams(vmem_limit_bytes=VMEM_LIMIT),
        cost_estimate=pl.CostEstimate(flops=16 * 10**9, bytes_accessed=10**7, transcendentals=0),
        name="scan_forward",
    )(x, g, b, bt, c, *parameters)


def scan_backward(x, g, cot, scan, states, scale, pull, b, c, ct, parameters):
    return pl.pallas_call(
        backward_kernel,
        grid=(PAIRS,),
        in_specs=[
            by_pair(TOKENS),
            by_pair(TOKENS),
            by_pair(TOKENS),
            by_pair(TOKENS),
            pl.BlockSpec((1, CHUNKS - 1, STATE, LANES), lambda p: (p, 0, 0, 0)),
            whole((TOKENS, LANES)),
            whole((TOKENS, LANES)),
            whole((TOKENS, STATE)),
            whole((TOKENS, STATE)),
            whole((STATE, TOKENS)),
        ]
        + PARAMETERS,
        out_specs=[
            by_pair(TOKENS),
            by_pair(TOKENS),
            whole((TOKENS, STATE)),
            whole((TOKENS, STATE)),
            whole((TOKENS, HEADS)),
            whole((8, LANES)),
        ],
        out_shape=[
            jax.ShapeDtypeStruct((TOKENS, CHANNELS), BF16),
            jax.ShapeDtypeStruct((TOKENS, CHANNELS), BF16),
            jax.ShapeDtypeStruct((TOKENS, STATE), BF16),
            jax.ShapeDtypeStruct((TOKENS, STATE), BF16),
            jax.ShapeDtypeStruct((TOKENS, HEADS), F32),
            jax.ShapeDtypeStruct((8, LANES), F32),
        ],
        scratch_shapes=TABLES
        + [
            pltpu.VMEM((CHUNKS, CHUNK, CHUNK), F32),
            pltpu.VMEM((TOKENS, STATE), F32),
            pltpu.VMEM((TOKENS, STATE), F32),
            pltpu.VMEM((TOKENS, LANES), F32),
            pltpu.VMEM((TOKENS, LANES), F32),
            pltpu.VMEM((8, CHANNELS), F32),
        ],
        compiler_params=pltpu.CompilerParams(vmem_limit_bytes=VMEM_LIMIT),
        cost_estimate=pl.CostEstimate(flops=20 * 10**9, bytes_accessed=10**7, transcendentals=0),
        name="scan_backward",
    )(x, g, cot, scan, states, scale, pull, b, c, ct, *parameters)


FEATURES = 512
BLOCK = 128
SHARDS = 8


def term_kernel(count, added, slot, slots, places, *refs):
    pieces, low_ref = refs[:count], refs[count]
    sent_ref = refs[count + 1] if added else None
    out_ref, held, done = refs[-3:]
    turned = jnp.concatenate([piece[...] for piece in pieces], axis=1).T
    for n in range(CHANNELS // COLUMNS):
        cols = slice(n * COLUMNS, (n + 1) * COLUMNS)
        term = dot(turned, low_ref[:, cols])
        for k in range(count):
            part = term[k * BLOCK : (k + 1) * BLOCK]
            if added:
                row = pl.multiple_of(places[k] * BLOCK, BLOCK)
                part = part + sent_ref[pl.ds(row, BLOCK), cols].astype(F32)
            held[k * BLOCK : (k + 1) * BLOCK, cols] = part.astype(BF16)
    copies = []
    for k in range(count):
        row = pl.multiple_of((places[k] * slots + slot) * BLOCK, BLOCK)
        copies.append(
            pltpu.make_async_copy(
                held.at[k * BLOCK : (k + 1) * BLOCK], out_ref.at[pl.ds(row, BLOCK)], done.at[k]
            )
        )
        copies[-1].start()
    for copy in copies:
        copy.wait()


def terms(places, block, pieces, low, sent=None, base=None, slot=0, slots=1):
    count = len(pieces)
    rows = SHARDS * slots * BLOCK
    more, specs, aliases = [], [], {}
    if sent is not None:
        more.append(sent)
        specs.append(whole((SHARDS * BLOCK, CHANNELS)))
    if base is not None:
        aliases = {2 + count + len(more): 0}
        more.append(base)
        specs.append(pl.BlockSpec(memory_space=pl.ANY))

    def kernel(*refs):
        term_kernel(count, sent is not None, slot, slots, *refs)

    return pl.pallas_call(
        kernel,
        grid_spec=pltpu.PrefetchScalarGridSpec(
            num_scalar_prefetch=1,
            grid=(1,),
            in_specs=[pl.BlockSpec((TOKENS, BLOCK), lambda _, at: (0, at[count]))] * count
            + [whole((TOKENS, CHANNELS))]
            + specs,
            out_specs=pl.BlockSpec(memory_space=pl.ANY),
            scratch_shapes=[
                pltpu.VMEM((count * BLOCK, CHANNELS), BF16),
                pltpu.SemaphoreType.DMA((count,)),
            ],
        ),
        out_shape=jax.ShapeDtypeStruct((rows, CHANNELS), BF16),
        input_output_aliases=aliases,
        compiler_params=pltpu.CompilerParams(vmem_limit_bytes=VMEM_LIMIT),
        cost_estimate=pl.CostEstimate(
            flops=count * 5 * 10**8, bytes_accessed=4 * 10**6, transcendentals=0
        ),
        name="terms" if sent is None else "terms_added",
    )(jnp.stack(list(places) + [block]).astype(jnp.int32), *pieces, low, *more)


COLUMNS = 256


def product_kernel(places, *refs):
    pieces = refs[:SHARDS]
    rows_ref, gated_ref, scale_ref, gain_ref = refs[SHARDS : SHARDS + 4]
    cot_ref, gain_grad_ref, pull_ref, sums = refs[SHARDS + 4 :]
    step = pl.program_id(0)
    starts = [pl.multiple_of(places[k] * FEATURES, FEATURES) for k in range(SHARDS)]
    cot_ref[...] = dot(
        jnp.concatenate([piece[...] for piece in pieces], axis=1),
        jnp.concatenate([rows_ref[pl.ds(start, FEATURES), :] for start in starts], axis=0),
    )

    @pl.when(step == 0)
    def _():
        sums[...] = jnp.zeros_like(sums)

    scale = scale_ref[...]
    for half in range(COLUMNS // LANES):
        cols = slice(half * LANES, (half + 1) * LANES)
        with_gated = cot_ref[:, cols] * gated_ref[:, cols]
        gain_grad_ref[:, cols] = jnp.sum(with_gated * scale, axis=0, keepdims=True)
        sums[...] += with_gated * gain_ref[:, cols]

    @pl.when(step == pl.num_programs(0) - 1)
    def _():
        pulled = jnp.sum(sums[...], axis=1, keepdims=True) * (1.0 / CHANNELS)
        pull_ref[...] = scale * scale * scale * pulled


def products(places, pieces, rows, gated, scale, gain):
    depth = SHARDS * FEATURES
    return pl.pallas_call(
        product_kernel,
        grid_spec=pltpu.PrefetchScalarGridSpec(
            num_scalar_prefetch=1,
            grid=(CHANNELS // COLUMNS,),
            in_specs=[whole((TOKENS, FEATURES))] * SHARDS
            + [
                pl.BlockSpec((depth, COLUMNS), lambda n, *_: (0, n)),
                pl.BlockSpec((TOKENS, COLUMNS), lambda n, *_: (0, n)),
                whole((TOKENS, LANES)),
                pl.BlockSpec((1, COLUMNS), lambda n, *_: (0, n)),
            ],
            out_specs=[
                pl.BlockSpec((TOKENS, COLUMNS), lambda n, *_: (0, n)),
                pl.BlockSpec((1, COLUMNS), lambda n, *_: (0, n)),
                whole((TOKENS, LANES)),
            ],
            scratch_shapes=[pltpu.VMEM((TOKENS, LANES), F32)],
        ),
        out_shape=[
            jax.ShapeDtypeStruct((TOKENS, CHANNELS), F32),
            jax.ShapeDtypeStruct((1, CHANNELS), F32),
            jax.ShapeDtypeStruct((TOKENS, LANES), F32),
        ],
        compiler_params=pltpu.CompilerParams(vmem_limit_bytes=VMEM_LIMIT),
        cost_estimate=pl.CostEstimate(
            flops=12 * 10**9, bytes_accessed=16 * 10**6, transcendentals=0
        ),
        name="products",
    )(places, *pieces, rows, gated, scale, gain)


def along_x(step):
    return [(x * 2 + h, (x + step) % 4 * 2 + h) for x in range(4) for h in range(2)]


def beside(shard):
    return lax.ppermute(shard, "tp", along_x(1)), lax.ppermute(shard, "tp", along_x(-1))


def beyond(before, after):
    half = before.shape[0] // 2
    top = lax.ppermute(before[:half], "tp", along_x(1))
    low = lax.ppermute(after[half:], "tp", along_x(-1))
    return top, low


def swap(bit):
    return [(b, b ^ bit) for b in range(32)]


def local_parameters(step_raw, log_rate, step_bias, skip_gain, norm_gain):
    def padded(v):
        return jnp.pad(v, (0, LANES - HEADS)).reshape(1, LANES)

    return (
        jnp.pad(step_raw, ((0, 0), (0, LANES - HEADS))),
        step_raw.T,
        padded(step_bias),
        padded(log_rate),
        step_bias.reshape(HEADS, 1),
        log_rate.reshape(HEADS, 1),
        jnp.repeat(skip_gain, WIDTH).reshape(1, CHANNELS),
        norm_gain.reshape(1, CHANNELS),
    )


def shards(
    scan_input,
    gate_input,
    state_proj,
    step_raw,
    log_rate,
    step_bias,
    skip_gain,
    norm_gain,
    out_proj,
    out_cotangent,
):
    norm_scale = 1.0 / math.sqrt(TOKENS * 32)
    block = lax.axis_index("blk")
    core, y_lo = block % 2, block // 2 % 2
    rows = lax.all_gather(out_proj, "blk", axis=0, tiled=True)
    own = out_cotangent
    partner = lax.ppermute(own, "tp", [(t, t ^ 1) for t in range(8)])
    before, after = beside(own)
    partner, before, after, scan_input = lax.optimization_barrier(
        (partner, before, after, scan_input)
    )
    partner_before, partner_after = beside(partner)
    far_parts = beyond(before, after)

    parameters = local_parameters(step_raw, log_rate, step_bias, skip_gain, norm_gain)
    b, c = state_proj[:, 0, :], state_proj[:, 1, :]
    low, scan, gated, states, scale = scan_forward(
        scan_input, gate_input, b, b.T, c, parameters
    )
    partner_before, partner_after, far_parts, low = lax.optimization_barrier(
        (partner_before, partner_after, far_parts, low)
    )
    far = jnp.concatenate(far_parts, axis=0)
    partner_far = jnp.concatenate(beyond(partner_before, partner_after), axis=0)
    early = [own, before, after, far, partner, partner_before, partner_after]
    me = lax.axis_index("tp")
    x, h = me // 2, me % 2
    places = [(x + shift) % 4 * 2 + row for row in (h, 1 - h) for shift in (0, 3, 1, 2)]

    mine, mine_y = 2 * y_lo + core, 2 * (1 - y_lo) + core
    theirs, theirs_y = 2 * y_lo + 1 - core, 2 * (1 - y_lo) + 1 - core

    base_y = terms(places[:-1], theirs_y, early, low)
    base = terms(places[:-1], theirs, early, low)
    base_y, base, partner_far = lax.optimization_barrier((base_y, base, partner_far))
    pieces = early + [partner_far]

    def sent_of(block, base):
        full = terms(places[-1:], block, pieces[-1:], low, base=base)
        return lax.ppermute(full, "blk", swap(1))

    sent_y, sent = sent_of(theirs_y, base_y), sent_of(theirs, base)
    both = terms(places, mine_y, pieces, low, sent_y, slots=2)
    rows, low = lax.optimization_barrier((rows, low))
    both = terms(places, mine, pieces, low, sent, base=both, slot=1, slots=2)
    by_z = [[z * 4 + rest for z in range(8)] for rest in range(4)]
    plane = lax.psum_scatter(
        both, "blk", scatter_dimension=0, tiled=True, axis_index_groups=by_z
    )
    given = lax.ppermute(plane[:BLOCK], "blk", swap(2))
    weight_grad = (plane[BLOCK:].astype(F32) + given.astype(F32)) * norm_scale

    rows, _ = lax.optimization_barrier((rows, both))
    cot, gain_grad, pull = products(
        jnp.stack(places).astype(jnp.int32), pieces, rows, gated, scale, parameters[-1]
    )
    dx, dg, db, dc, step_grad, small = scan_backward(
        scan_input, gate_input, cot, scan, states, scale, pull, b, c, c.T, parameters
    )
    summed = jnp.concatenate([small, gain_grad.reshape(8, LANES)], axis=0)
    for bit in (1, 2, 4, 8, 16):
        summed = summed + lax.ppermute(summed, "blk", swap(bit))
    summed = summed * norm_scale
    return (
        dx,
        dg,
        jnp.stack([db, dc], axis=1),
        step_grad,
        weight_grad,
        summed[0, :HEADS],
        summed[1, :HEADS],
        summed[2, :HEADS],
        summed[8:].reshape(CHANNELS),
    )


def solution(mesh):
    placed = (
        P("blk", "tp"),
        P("blk", "tp"),
        P("blk", None, "tp"),
        P("blk", "tp"),
        P("tp"),
        P("tp"),
        P("tp"),
        P("tp"),
        P("blk", "tp"),
        P("blk", "tp"),
    )
    return jax.shard_map(
        shards,
        mesh=mesh,
        in_specs=placed,
        out_specs=(
            P("blk", "tp"),
            P("blk", "tp"),
            P("blk", None, "tp"),
            P("blk", "tp"),
            P("blk", "tp"),
            P("tp"),
            P("tp"),
            P("tp"),
            P("tp"),
        ),
        check_vma=False,
    )
```

```python
import math

import jax
import jax.numpy as jnp
from jax import lax
from jax.experimental import pallas as pl
from jax.experimental.pallas import tpu as pltpu
from jax.sharding import PartitionSpec as P

TOKENS = 512
CHANNELS = 1024
HEADS = 16
WIDTH = 64
STATE = 256
CHUNK = 128
CHUNKS = TOKENS // CHUNK
LANES = 128
PAIRS = HEADS // 2
EPS = 1e-05

F32 = jnp.float32
BF16 = jnp.bfloat16


def dot(a, b, over=(1, 0)):
    return lax.dot_general(
        a, b, (((over[0],), (over[1],)), ((), ())), preferred_element_type=F32
    )


def three_parts(v):
    hi = v.astype(BF16).astype(F32)
    rest = v - hi
    mid = rest.astype(BF16).astype(F32)
    return hi, mid, rest - mid


def packed(v):
    hi, mid, low = three_parts(v)
    return (hi + pltpu.roll(mid, HEADS, 1) + pltpu.roll(low, 2 * HEADS, 1)).astype(BF16)


def halves(v):
    hi = v.astype(BF16)
    return hi, (v - hi.astype(F32)).astype(BF16)


def folded(v):
    middle = v.shape[1] // 2
    return v[:, :middle] + v[:, middle:]


def triangle(lower):
    i = lax.broadcasted_iota(jnp.int32, (CHUNK, CHUNK), 0)
    j = lax.broadcasted_iota(jnp.int32, (CHUNK, CHUNK), 1)
    return i >= j if lower else i <= j


def picker(pair, width):
    row = lax.broadcasted_iota(jnp.int32, (LANES, 2 * width), 0)
    col = lax.broadcasted_iota(jnp.int32, (LANES, 2 * width), 1)
    head = 2 * pair + col // width
    return jnp.where((row % HEADS == head) & (row < 3 * HEADS), 1.0, 0.0).astype(BF16)


def softplus(v):
    return jnp.maximum(v, 0.0) + jnp.log1p(jnp.exp(-jnp.abs(v)))


def head_lanes():
    return lax.broadcasted_iota(jnp.int32, (TOKENS, LANES), 1) < HEADS


def steps_of(raw_ref, bias_ref, rate_ref):
    step = jnp.where(head_lanes(), softplus(raw_ref[...].astype(F32) + bias_ref[...]), 0.0)
    return step, -step * jnp.exp(rate_ref[...])


def prepare(raw_ref, raw_t_ref, bias_ref, rate_ref, bias_t_ref, rate_t_ref, b_ref, c_ref,
            step_pack, run_pack, run_rows, step_rows, overlap):
    step, decay = steps_of(raw_ref, bias_ref, rate_ref)
    step_pack[...] = packed(step)
    lower = jnp.where(triangle(True), 1.0, 0.0).astype(BF16)
    upper = jnp.where(triangle(False), 1.0, 0.0).astype(BF16)
    decay_pack = packed(decay)
    keep = lax.broadcasted_iota(jnp.int32, (CHUNK, LANES), 1) < HEADS
    step_t = softplus(raw_t_ref[...].astype(F32) + bias_t_ref[...])
    decay_t = three_parts(-step_t * jnp.exp(rate_t_ref[...]))
    for pair in range(PAIRS):
        step_rows[pair] = step_t[2 * pair : 2 * pair + 2, :]
    for c in range(CHUNKS):
        rows = slice(c * CHUNK, (c + 1) * CHUNK)
        total = dot(lower, decay_pack[rows])
        total = total + pltpu.roll(total, LANES - HEADS, 1) + pltpu.roll(total, LANES - 2 * HEADS, 1)
        run_pack[rows, :] = packed(jnp.where(keep, total, 0.0))
        across = sum(dot(part[:, rows].astype(BF16), upper) for part in decay_t)
        for pair in range(PAIRS):
            run_rows[pair, :, rows] = across[2 * pair : 2 * pair + 2, :]
        overlap[c] = jnp.where(triangle(True), dot(c_ref[rows, :], b_ref[rows, :], (1, 1)), 0.0)


def first_half():
    return lax.broadcasted_iota(jnp.int32, (CHUNK, LANES), 1) < WIDTH


def apart(v):
    first = first_half()
    return jnp.concatenate([jnp.where(first, v, 0.0), jnp.where(first, 0.0, v)], axis=0).astype(BF16)


def decays(columns, run_rows, pair, rows):
    out = []
    for h in range(2):
        across = run_rows[pair, h : h + 1, rows]
        out.append(jnp.exp(jnp.minimum(columns[:, h * CHUNK : (h + 1) * CHUNK] - across, 0.0)))
    return out


def forward_kernel(x_ref, g_ref, b_ref, bt_ref, c_ref, raw_ref, raw_t_ref, bias_ref, rate_ref,
                   bias_t_ref, rate_t_ref, skip_ref, gain_ref,
                   low_ref, scan_ref, gated_ref, state_ref, scale_ref,
                   step_pack, run_pack, run_rows, step_rows, overlap, squares):
    pair = pl.program_id(0)

    @pl.when(pair == 0)
    def _():
        prepare(raw_ref, raw_t_ref, bias_ref, rate_ref, bias_t_ref, rate_t_ref, b_ref, c_ref,
                step_pack, run_pack, run_rows, step_rows, overlap)
        squares[...] = jnp.zeros_like(squares)

    narrow, wide = picker(pair, WIDTH), picker(pair, CHUNK)
    skip = skip_ref[:, pl.ds(pl.multiple_of(pair * LANES, LANES), LANES)]
    state = None
    for c in range(CHUNKS):
        rows = slice(c * CHUNK, (c + 1) * CHUNK)
        x = x_ref[rows, :].astype(F32)
        step = dot(step_pack[rows, :], narrow)
        run = dot(run_pack[rows, :], narrow)
        columns = dot(run_pack[rows, :], wide)
        weights = []
        for h, one in enumerate(decays(columns, run_rows, pair, rows)):
            weights.append(halves(one * overlap[c] * step_rows[pair, h : h + 1, rows]))
        x_apart = apart(x)
        y = dot(
            jnp.concatenate([weights[h][part] for part in range(2) for h in range(2)], axis=1),
            jnp.concatenate([x_apart, x_apart], axis=0),
        )
        if c > 0:
            state_ref[0, c - 1] = state
            held = jnp.concatenate(halves(state), axis=1)
            y = y + jnp.exp(run) * folded(dot(c_ref[rows, :], held))
        if c < CHUNKS - 1:
            end = run[CHUNK - 1 :, :]
            fresh = jnp.concatenate(halves(x * step * jnp.exp(end - run)), axis=1)
            local = folded(dot(bt_ref[:, rows], fresh))
            state = local if c == 0 else jnp.exp(end) * state + local
        scan_ref[rows, :] = y
        g = g_ref[rows, :].astype(F32)
        gated = (y + skip * x) * (g / (1.0 + jnp.exp(-g)))
        gated_ref[rows, pl.ds(pl.multiple_of(pair * LANES, LANES), LANES)] = gated
        squares[rows, :] += gated * gated

    @pl.when(pair == PAIRS - 1)
    def _():
        for c in range(CHUNKS):
            rows = slice(c * CHUNK, (c + 1) * CHUNK)
            mean = jnp.sum(squares[rows, :], axis=1, keepdims=True) * (1.0 / CHANNELS)
            scale = lax.rsqrt(mean + EPS)
            scale_ref[rows, :] = jnp.broadcast_to(scale, (CHUNK, LANES))
            low_ref[:, rows] = (gated_ref[rows, :] * scale * gain_ref[...]).T.astype(BF16)


def backward_kernel(x_ref, g_ref, cot_ref, scan_ref, state_ref, scale_ref, pull_ref,
                    b_ref, c_ref, ct_ref, raw_ref, raw_t_ref, bias_ref, rate_ref,
                    bias_t_ref, rate_t_ref, skip_ref, gain_ref,
                    dx_ref, dg_ref, db_ref, dc_ref, step_ref, small_ref,
                    step_pack, run_pack, run_rows, step_rows, overlap, d_overlap, d_b, d_c, flow, direct, lanes):
    pair = pl.program_id(0)

    @pl.when(pair == 0)
    def _():
        prepare(raw_ref, raw_t_ref, bias_ref, rate_ref, bias_t_ref, rate_t_ref, b_ref, c_ref,
                step_pack, run_pack, run_rows, step_rows, overlap)
        for held in (d_overlap, d_b, d_c, flow, direct, lanes):
            held[...] = jnp.zeros_like(held)

    narrow, wide = picker(pair, WIDTH), picker(pair, CHUNK)
    here = pl.ds(pl.multiple_of(pair * LANES, LANES), LANES)
    skip, gain = skip_ref[:, here], gain_ref[:, here]
    first = first_half()
    lane = lax.broadcasted_iota(jnp.int32, (CHUNK, LANES), 1)

    def by_head(v):
        one = jnp.sum(jnp.where(first, v, 0.0), axis=1, keepdims=True)
        two = jnp.sum(jnp.where(first, 0.0, v), axis=1, keepdims=True)
        return jnp.where(lane == 2 * pair, one, jnp.where(lane == 2 * pair + 1, two, 0.0))

    d_state = None
    skip_sum = jnp.zeros((1, LANES), F32)
    for c in reversed(range(CHUNKS)):
        rows = slice(c * CHUNK, (c + 1) * CHUNK)
        x = x_ref[rows, :].astype(F32)
        g = g_ref[rows, :].astype(F32)
        scan = scan_ref[rows, :]
        out = scan + skip * x
        sig = 1.0 / (1.0 + jnp.exp(-g))
        silu = g * sig
        d_gated = scale_ref[rows, :] * gain * cot_ref[rows, :] - out * silu * pull_ref[rows, :]
        dy = d_gated * silu
        dg_ref[rows, :] = (d_gated * out * (sig + silu * (1.0 - sig))).astype(BF16)
        skip_sum = skip_sum + jnp.sum(dy * x, axis=0, keepdims=True)

        step = dot(step_pack[rows, :], narrow)
        run = dot(run_pack[rows, :], narrow)
        columns = dot(run_pack[rows, :], wide)
        driven = x * step
        dy_hi, dy_low = (apart(part.astype(F32)) for part in halves(dy))
        factor = decays(columns, run_rows, pair, rows)
        products = dot(
            jnp.concatenate([dy_hi, dy_low], axis=1),
            jnp.concatenate([x_ref[rows, :], x_ref[rows, :]], axis=1),
            (1, 1),
        )
        step_row = step_rows[pair, :, rows]
        d_overlap[c] += (
            factor[0] * products[:CHUNK] * step_row[:1] + factor[1] * products[CHUNK:] * step_row[1:]
        )
        weights = [halves(one * overlap[c]) for one in factor]
        weights_hi = jnp.concatenate([one[0] for one in weights], axis=0)
        weights_low = jnp.concatenate([one[1] for one in weights], axis=0)
        d_driven = folded(dot(weights_hi, jnp.concatenate([dy_hi, dy_low], axis=1), (0, 0)))
        d_driven = d_driven + dot(weights_low, dy_hi, (0, 0))
        entering_hi, entering_low = halves(dy * jnp.exp(run))
        entering = jnp.concatenate([entering_hi, entering_low], axis=1)
        end = run[CHUNK - 1 :, :]
        if c > 0:
            held = state_ref[0, c - 1]
            held_hi, held_low = halves(held)
            d_c[rows, :] += dot(
                entering, jnp.concatenate([held_hi, held_hi], axis=1), (1, 1)
            ) + dot(entering_hi, held_low, (1, 1))
        if c < CHUNKS - 1:
            to_end = jnp.exp(end - run)
            d_hi, d_low = halves(d_state)
            from_state = to_end * folded(
                dot(b_ref[rows, :], jnp.concatenate([d_hi, d_low], axis=1))
            )
            fresh_hi, fresh_low = halves(driven * to_end)
            d_b[rows, :] += dot(
                jnp.concatenate([fresh_hi, fresh_low], axis=1),
                jnp.concatenate([d_hi, d_hi], axis=1),
                (1, 1),
            ) + dot(fresh_hi, d_low, (1, 1))
            crossing = jnp.sum(driven * from_state, axis=0, keepdims=True)
            if c > 0:
                carried = jnp.sum(held * d_state, axis=0, keepdims=True)
                crossing = crossing + jnp.exp(end) * carried
            lanes[c : c + 1, here] = crossing
            d_driven = d_driven + from_state
        if c > 0:
            back = folded(dot(ct_ref[:, rows], entering))
            d_state = back if d_state is None else jnp.exp(end) * d_state + back
        flow[rows, :] += by_head(dy * scan - driven * d_driven)
        direct[rows, :] += by_head(x * d_driven)
        dx_ref[rows, :] = (step * d_driven + skip * dy).astype(BF16)
    lanes[CHUNKS : CHUNKS + 1, here] = skip_sum

    @pl.when(pair == PAIRS - 1)
    def _():
        channel = lax.broadcasted_iota(jnp.int32, (CHANNELS, LANES), 0) // WIDTH
        head = lax.broadcasted_iota(jnp.int32, (CHANNELS, LANES), 1)
        gather = jnp.where(channel == head, 1.0, 0.0).astype(BF16)
        heads = sum(dot(part.astype(BF16), gather) for part in three_parts(lanes[...]))
        step_all, decay_all = steps_of(raw_ref, bias_ref, rate_ref)
        rate = jnp.exp(rate_ref[...])
        upper = jnp.where(triangle(False), 1.0, 0.0).astype(BF16)
        keep = lane < HEADS
        rate_sum = jnp.zeros((1, LANES), F32)
        bias_sum = jnp.zeros((1, LANES), F32)
        for c in range(CHUNKS):
            rows = slice(c * CHUNK, (c + 1) * CHUNK)
            d_decay = sum(dot(upper, part.astype(BF16)) for part in three_parts(flow[rows, :]))
            d_decay = d_decay + heads[c : c + 1, :]
            d_step = direct[rows, :] - d_decay * rate
            before = raw_ref[rows, :].astype(F32) + bias_ref[...]
            d_raw = jnp.where(keep, d_step / (1.0 + jnp.exp(-before)), 0.0)
            step_ref[rows, :] = d_raw[:, :HEADS]
            bias_sum = bias_sum + jnp.sum(d_raw, axis=0, keepdims=True)
            rate_sum = rate_sum + jnp.sum(
                jnp.where(keep, d_decay * decay_all[rows], 0.0), axis=0, keepdims=True
            )
            d_hi, d_low = halves(jnp.where(triangle(True), d_overlap[c], 0.0))
            dc_ref[rows, :] = (
                d_c[rows, :] + dot(d_hi, b_ref[rows, :]) + dot(d_low, b_ref[rows, :])
            ).astype(BF16)
            db_ref[rows, :] = (
                d_b[rows, :] + dot(d_hi, c_ref[rows, :], (0, 0)) + dot(d_low, c_ref[rows, :], (0, 0))
            ).astype(BF16)
        small_ref[...] = jnp.concatenate(
            [rate_sum, bias_sum, heads[CHUNKS : CHUNKS + 1, :], jnp.zeros((5, LANES), F32)], axis=0
        )


def whole(shape):
    return pl.BlockSpec(shape, lambda *_: (0,) * len(shape))


def by_pair(rows):
    return pl.BlockSpec((rows, LANES), lambda p, *_: (0, p))


VMEM_LIMIT = 56 * 1024 * 1024

TABLES = [
    pltpu.VMEM((TOKENS, LANES), BF16),
    pltpu.VMEM((TOKENS, LANES), BF16),
    pltpu.VMEM((PAIRS, 2, TOKENS), F32),
    pltpu.VMEM((PAIRS, 2, TOKENS), F32),
    pltpu.VMEM((CHUNKS, CHUNK, CHUNK), F32),
]

PARAMETERS = [
    whole((TOKENS, LANES)),
    whole((HEADS, TOKENS)),
    whole((1, LANES)),
    whole((1, LANES)),
    whole((HEADS, 1)),
    whole((HEADS, 1)),
    whole((1, CHANNELS)),
    whole((1, CHANNELS)),
]


def scan_forward(x, g, b, bt, c, parameters):
    return pl.pallas_call(
        forward_kernel,
        grid=(PAIRS,),
        in_specs=[
            by_pair(TOKENS),
            by_pair(TOKENS),
            whole((TOKENS, STATE)),
            whole((STATE, TOKENS)),
            whole((TOKENS, STATE)),
        ]
        + PARAMETERS,
        out_specs=[
            whole((CHANNELS, TOKENS)),
            by_pair(TOKENS),
            whole((TOKENS, CHANNELS)),
            pl.BlockSpec((1, CHUNKS - 1, STATE, LANES), lambda p: (p, 0, 0, 0)),
            whole((TOKENS, LANES)),
        ],
        out_shape=[
            jax.ShapeDtypeStruct((CHANNELS, TOKENS), BF16),
            jax.ShapeDtypeStruct((TOKENS, CHANNELS), F32),
            jax.ShapeDtypeStruct((TOKENS, CHANNELS), F32),
            jax.ShapeDtypeStruct((PAIRS, CHUNKS - 1, STATE, LANES), F32),
            jax.ShapeDtypeStruct((TOKENS, LANES), F32),
        ],
        scratch_shapes=TABLES + [pltpu.VMEM((TOKENS, LANES), F32)],
        compiler_params=pltpu.CompilerParams(vmem_limit_bytes=VMEM_LIMIT),
        cost_estimate=pl.CostEstimate(flops=16 * 10**9, bytes_accessed=10**7, transcendentals=0),
        name="scan_forward",
    )(x, g, b, bt, c, *parameters)


def scan_backward(x, g, cot, scan, states, scale, pull, b, c, ct, parameters):
    return pl.pallas_call(
        backward_kernel,
        grid=(PAIRS,),
        in_specs=[
            by_pair(TOKENS),
            by_pair(TOKENS),
            by_pair(TOKENS),
            by_pair(TOKENS),
            pl.BlockSpec((1, CHUNKS - 1, STATE, LANES), lambda p: (p, 0, 0, 0)),
            whole((TOKENS, LANES)),
            whole((TOKENS, LANES)),
            whole((TOKENS, STATE)),
            whole((TOKENS, STATE)),
            whole((STATE, TOKENS)),
        ]
        + PARAMETERS,
        out_specs=[
            by_pair(TOKENS),
            by_pair(TOKENS),
            whole((TOKENS, STATE)),
            whole((TOKENS, STATE)),
            whole((TOKENS, HEADS)),
            whole((8, LANES)),
        ],
        out_shape=[
            jax.ShapeDtypeStruct((TOKENS, CHANNELS), BF16),
            jax.ShapeDtypeStruct((TOKENS, CHANNELS), BF16),
            jax.ShapeDtypeStruct((TOKENS, STATE), BF16),
            jax.ShapeDtypeStruct((TOKENS, STATE), BF16),
            jax.ShapeDtypeStruct((TOKENS, HEADS), F32),
            jax.ShapeDtypeStruct((8, LANES), F32),
        ],
        scratch_shapes=TABLES
        + [
            pltpu.VMEM((CHUNKS, CHUNK, CHUNK), F32),
            pltpu.VMEM((TOKENS, STATE), F32),
            pltpu.VMEM((TOKENS, STATE), F32),
            pltpu.VMEM((TOKENS, LANES), F32),
            pltpu.VMEM((TOKENS, LANES), F32),
            pltpu.VMEM((8, CHANNELS), F32),
        ],
        compiler_params=pltpu.CompilerParams(vmem_limit_bytes=VMEM_LIMIT),
        cost_estimate=pl.CostEstimate(flops=20 * 10**9, bytes_accessed=10**7, transcendentals=0),
        name="scan_backward",
    )(x, g, cot, scan, states, scale, pull, b, c, ct, *parameters)


FEATURES = 512
BLOCK = 128
SHARDS = 8


def term_kernel(count, added, placed, places, *refs):
    pieces, low_ref = refs[: 2 * count], refs[2 * count]
    sent_ref = refs[2 * count + 1] if added else None
    out_ref, held, done = refs[-3:]
    copies = []
    for k in range(count):
        blocks = [piece[...] for piece in pieces[2 * k : 2 * k + 2]]
        term = dot(low_ref[...], jnp.concatenate(blocks, axis=1))
        for slot in range(2):
            n = 2 * k + slot
            here = slice(n * CHANNELS, (n + 1) * CHANNELS)
            part = term[:, slot * BLOCK : (slot + 1) * BLOCK]
            if added:
                part = part + sent_ref[here, :].astype(F32)
            held[here, :] = part.astype(BF16)
            start = n * CHANNELS
            if placed:
                start = pl.multiple_of((places[k] * 2 + slot) * CHANNELS, CHANNELS)
            copies.append(
                pltpu.make_async_copy(
                    held.at[here], out_ref.at[pl.ds(start, CHANNELS)], done.at[n]
                )
            )
            copies[-1].start()
    for copy in copies:
        copy.wait()


def terms(places, blocks, pieces, low, sent=None, base=None):
    count = len(pieces)
    added = sent is not None
    rows = 2 * CHANNELS * (SHARDS if added else count)
    more, specs, aliases = [], [], {}
    if added:
        more.append(sent)
        specs.append(whole((2 * CHANNELS * count, BLOCK)))
    if base is not None:
        aliases = {2 + 2 * count + len(more): 0}
        more.append(base)
        specs.append(pl.BlockSpec(memory_space=pl.ANY))

    def kernel(*refs):
        term_kernel(count, added, added, *refs)

    def lanes(slot):
        return pl.BlockSpec((TOKENS, BLOCK), lambda _, at: (0, at[count + slot]))

    return pl.pallas_call(
        kernel,
        grid_spec=pltpu.PrefetchScalarGridSpec(
            num_scalar_prefetch=1,
            grid=(1,),
            in_specs=[lanes(0), lanes(1)] * count + [whole((CHANNELS, TOKENS))] + specs,
            out_specs=pl.BlockSpec(memory_space=pl.ANY),
            scratch_shapes=[
                pltpu.VMEM((2 * count * CHANNELS, BLOCK), BF16),
                pltpu.SemaphoreType.DMA((2 * count,)),
            ],
        ),
        out_shape=jax.ShapeDtypeStruct((rows, BLOCK), BF16),
        input_output_aliases=aliases,
        compiler_params=pltpu.CompilerParams(vmem_limit_bytes=VMEM_LIMIT),
        cost_estimate=pl.CostEstimate(
            flops=(count + 1) * 7 * 10**8, bytes_accessed=2 * 10**6, transcendentals=0
        ),
        name="terms_added" if added else "terms",
    )(
        jnp.stack(list(places) + list(blocks)).astype(jnp.int32),
        *[piece for piece in pieces for _ in range(2)],
        low,
        *more,
    )


def finish_kernel(scale, kept_ref, given_ref, out_ref):
    total = kept_ref[...].astype(F32) + given_ref[...].astype(F32)
    out_ref[...] = (total * scale).T


def finish(plane, given, scale):
    return pl.pallas_call(
        lambda *refs: finish_kernel(scale, *refs),
        grid=(1,),
        in_specs=[pl.BlockSpec((CHANNELS, BLOCK), lambda _: (1, 0)), whole((CHANNELS, BLOCK))],
        out_specs=whole((BLOCK, CHANNELS)),
        out_shape=jax.ShapeDtypeStruct((BLOCK, CHANNELS), F32),
        name="finish",
    )(plane, given)


COLUMNS = 256


def product_kernel(places, *refs):
    pieces = refs[:SHARDS]
    rows_ref, gated_ref, scale_ref, gain_ref = refs[SHARDS : SHARDS + 4]
    cot_ref, gain_grad_ref, pull_ref, sums = refs[SHARDS + 4 :]
    step = pl.program_id(0)
    starts = [pl.multiple_of(places[k] * FEATURES, FEATURES) for k in range(SHARDS)]
    cot_ref[...] = dot(
        jnp.concatenate([piece[...] for piece in pieces], axis=1),
        jnp.concatenate([rows_ref[pl.ds(start, FEATURES), :] for start in starts], axis=0),
    )

    @pl.when(step == 0)
    def _():
        sums[...] = jnp.zeros_like(sums)

    scale = scale_ref[...]
    for half in range(COLUMNS // LANES):
        cols = slice(half * LANES, (half + 1) * LANES)
        with_gated = cot_ref[:, cols] * gated_ref[:, cols]
        gain_grad_ref[:, cols] = jnp.sum(with_gated * scale, axis=0, keepdims=True)
        sums[...] += with_gated * gain_ref[:, cols]

    @pl.when(step == pl.num_programs(0) - 1)
    def _():
        pulled = jnp.sum(sums[...], axis=1, keepdims=True) * (1.0 / CHANNELS)
        pull_ref[...] = scale * scale * scale * pulled


def products(places, pieces, rows, gated, scale, gain):
    depth = SHARDS * FEATURES
    return pl.pallas_call(
        product_kernel,
        grid_spec=pltpu.PrefetchScalarGridSpec(
            num_scalar_prefetch=1,
            grid=(CHANNELS // COLUMNS,),
            in_specs=[whole((TOKENS, FEATURES))] * SHARDS
            + [
                pl.BlockSpec((depth, COLUMNS), lambda n, *_: (0, n)),
                pl.BlockSpec((TOKENS, COLUMNS), lambda n, *_: (0, n)),
                whole((TOKENS, LANES)),
                pl.BlockSpec((1, COLUMNS), lambda n, *_: (0, n)),
            ],
            out_specs=[
                pl.BlockSpec((TOKENS, COLUMNS), lambda n, *_: (0, n)),
                pl.BlockSpec((1, COLUMNS), lambda n, *_: (0, n)),
                whole((TOKENS, LANES)),
            ],
            scratch_shapes=[pltpu.VMEM((TOKENS, LANES), F32)],
        ),
        out_shape=[
            jax.ShapeDtypeStruct((TOKENS, CHANNELS), F32),
            jax.ShapeDtypeStruct((1, CHANNELS), F32),
            jax.ShapeDtypeStruct((TOKENS, LANES), F32),
        ],
        compiler_params=pltpu.CompilerParams(vmem_limit_bytes=VMEM_LIMIT),
        cost_estimate=pl.CostEstimate(
            flops=12 * 10**9, bytes_accessed=16 * 10**6, transcendentals=0
        ),
        name="products",
    )(places, *pieces, rows, gated, scale, gain)


def along_x(step):
    return [(x * 2 + h, (x + step) % 4 * 2 + h) for x in range(4) for h in range(2)]


def beside(shard):
    return lax.ppermute(shard, "tp", along_x(1)), lax.ppermute(shard, "tp", along_x(-1))


def beyond(before, after):
    half = before.shape[0] // 2
    top = lax.ppermute(before[:half], "tp", along_x(1))
    low = lax.ppermute(after[half:], "tp", along_x(-1))
    return top, low


def swap(bit):
    return [(b, b ^ bit) for b in range(32)]


def local_parameters(step_raw, log_rate, step_bias, skip_gain, norm_gain):
    def padded(v):
        return jnp.pad(v, (0, LANES - HEADS)).reshape(1, LANES)

    return (
        jnp.pad(step_raw, ((0, 0), (0, LANES - HEADS))),
        step_raw.T,
        padded(step_bias),
        padded(log_rate),
        step_bias.reshape(HEADS, 1),
        log_rate.reshape(HEADS, 1),
        jnp.repeat(skip_gain, WIDTH).reshape(1, CHANNELS),
        norm_gain.reshape(1, CHANNELS),
    )


def shards(
    scan_input,
    gate_input,
    state_proj,
    step_raw,
    log_rate,
    step_bias,
    skip_gain,
    norm_gain,
    out_proj,
    out_cotangent,
):
    norm_scale = 1.0 / math.sqrt(TOKENS * 32)
    block = lax.axis_index("blk")
    core, y_lo = block % 2, block // 2 % 2
    by_z = [[z * 4 + rest for z in range(8)] for rest in range(4)]
    rows = lax.all_gather(out_proj, "blk", axis=0, tiled=True)
    own = out_cotangent
    partner = lax.ppermute(own, "tp", [(t, t ^ 1) for t in range(8)])
    before, after = beside(own)
    partner, before, after, scan_input = lax.optimization_barrier(
        (partner, before, after, scan_input)
    )
    partner_before, partner_after = beside(partner)
    far_parts = beyond(before, after)

    parameters = local_parameters(step_raw, log_rate, step_bias, skip_gain, norm_gain)
    b, c = state_proj[:, 0, :], state_proj[:, 1, :]
    low, scan, gated, states, scale = scan_forward(
        scan_input, gate_input, b, b.T, c, parameters
    )
    partner_before, partner_after, far_parts, low = lax.optimization_barrier(
        (partner_before, partner_after, far_parts, low)
    )
    far = jnp.concatenate(far_parts, axis=0)
    partner_far = beyond(partner_before, partner_after)
    early = [own, before, after, far, partner, partner_before, partner_after]
    me = lax.axis_index("tp")
    x, h = me // 2, me % 2
    places = [(x + shift) % 4 * 2 + row for row in (h, 1 - h) for shift in (0, 3, 1, 2)]

    mine, mine_y = 2 * y_lo + core, 2 * (1 - y_lo) + core
    theirs, theirs_y = 2 * y_lo + 1 - core, 2 * (1 - y_lo) + 1 - core

    theirs_early = terms(places[:-1], (theirs_y, theirs), early, low)
    sent_early = lax.ppermute(theirs_early, "blk", swap(1))
    partner_far, _ = lax.optimization_barrier((partner_far, theirs_early))
    last = [jnp.concatenate(partner_far, axis=0)]
    sent_last = lax.ppermute(terms(places[-1:], (theirs_y, theirs), last, low), "blk", swap(1))
    both = terms(places[:-1], (mine_y, mine), early, low, sent_early)
    both = terms(places[-1:], (mine_y, mine), last, low, sent_last, base=both)
    plane = lax.psum_scatter(
        both, "blk", scatter_dimension=0, tiled=True, axis_index_groups=by_z
    )
    given = lax.ppermute(plane[:CHANNELS], "blk", swap(2))
    weight_grad = finish(plane, given, norm_scale)

    rows, _ = lax.optimization_barrier((rows, both))
    cot, gain_grad, pull = products(
        jnp.stack(places).astype(jnp.int32),
        early + last,
        rows,
        gated,
        scale,
        parameters[-1],
    )
    dx, dg, db, dc, step_grad, small = scan_backward(
        scan_input, gate_input, cot, scan, states, scale, pull, b, c, c.T, parameters
    )
    summed = jnp.concatenate([small, gain_grad.reshape(8, LANES)], axis=0)
    for bit in (1, 2, 4, 8, 16):
        summed = summed + lax.ppermute(summed, "blk", swap(bit))
    summed = summed * norm_scale
    return (
        dx,
        dg,
        jnp.stack([db, dc], axis=1),
        step_grad,
        weight_grad,
        summed[0, :HEADS],
        summed[1, :HEADS],
        summed[2, :HEADS],
        summed[8:].reshape(CHANNELS),
    )


def solution(mesh):
    placed = (
        P("blk", "tp"),
        P("blk", "tp"),
        P("blk", None, "tp"),
        P("blk", "tp"),
        P("tp"),
        P("tp"),
        P("tp"),
        P("tp"),
        P("blk", "tp"),
        P("blk", "tp"),
    )
    return jax.shard_map(
        shards,
        mesh=mesh,
        in_specs=placed,
        out_specs=(
            P("blk", "tp"),
            P("blk", "tp"),
            P("blk", None, "tp"),
            P("blk", "tp"),
            P("blk", "tp"),
            P("tp"),
            P("tp"),
            P("tp"),
            P("tp"),
        ),
        check_vma=False,
    )
```

```python
import math

import jax
import jax.numpy as jnp
from jax import lax
from jax.experimental import pallas as pl
from jax.experimental.pallas import tpu as pltpu
from jax.sharding import PartitionSpec as P

TOKENS = 512
CHANNELS = 1024
HEADS = 16
WIDTH = 64
STATE = 256
CHUNK = 128
CHUNKS = TOKENS // CHUNK
LANES = 128
PAIRS = HEADS // 2
EPS = 1e-05

F32 = jnp.float32
BF16 = jnp.bfloat16


def dot(a, b, over=(1, 0)):
    return lax.dot_general(
        a, b, (((over[0],), (over[1],)), ((), ())), preferred_element_type=F32
    )


def three_parts(v):
    hi = v.astype(BF16).astype(F32)
    rest = v - hi
    mid = rest.astype(BF16).astype(F32)
    return hi, mid, rest - mid


def packed(v):
    hi, mid, low = three_parts(v)
    return (hi + pltpu.roll(mid, HEADS, 1) + pltpu.roll(low, 2 * HEADS, 1)).astype(BF16)


def halves(v):
    hi = v.astype(BF16)
    return hi, (v - hi.astype(F32)).astype(BF16)


def folded(v):
    middle = v.shape[1] // 2
    return v[:, :middle] + v[:, middle:]


def triangle(lower):
    i = lax.broadcasted_iota(jnp.int32, (CHUNK, CHUNK), 0)
    j = lax.broadcasted_iota(jnp.int32, (CHUNK, CHUNK), 1)
    return i >= j if lower else i <= j


def picker(pair, width):
    row = lax.broadcasted_iota(jnp.int32, (LANES, 2 * width), 0)
    col = lax.broadcasted_iota(jnp.int32, (LANES, 2 * width), 1)
    head = 2 * pair + col // width
    return jnp.where((row % HEADS == head) & (row < 3 * HEADS), 1.0, 0.0).astype(BF16)


def softplus(v):
    return jnp.maximum(v, 0.0) + jnp.log1p(jnp.exp(-jnp.abs(v)))


def head_lanes():
    return lax.broadcasted_iota(jnp.int32, (TOKENS, LANES), 1) < HEADS


def steps_of(raw_ref, bias_ref, rate_ref):
    step = jnp.where(head_lanes(), softplus(raw_ref[...].astype(F32) + bias_ref[...]), 0.0)
    return step, -step * jnp.exp(rate_ref[...])


def prepare(raw_ref, raw_t_ref, bias_ref, rate_ref, bias_t_ref, rate_t_ref, b_ref, c_ref,
            step_pack, run_pack, run_rows, step_rows, overlap):
    step, decay = steps_of(raw_ref, bias_ref, rate_ref)
    step_pack[...] = packed(step)
    lower = jnp.where(triangle(True), 1.0, 0.0).astype(BF16)
    upper = jnp.where(triangle(False), 1.0, 0.0).astype(BF16)
    decay_pack = packed(decay)
    keep = lax.broadcasted_iota(jnp.int32, (CHUNK, LANES), 1) < HEADS
    step_t = softplus(raw_t_ref[...].astype(F32) + bias_t_ref[...])
    decay_t = three_parts(-step_t * jnp.exp(rate_t_ref[...]))
    for pair in range(PAIRS):
        step_rows[pair] = step_t[2 * pair : 2 * pair + 2, :]
    for c in range(CHUNKS):
        rows = slice(c * CHUNK, (c + 1) * CHUNK)
        total = dot(lower, decay_pack[rows])
        total = total + pltpu.roll(total, LANES - HEADS, 1) + pltpu.roll(total, LANES - 2 * HEADS, 1)
        run_pack[rows, :] = packed(jnp.where(keep, total, 0.0))
        across = sum(dot(part[:, rows].astype(BF16), upper) for part in decay_t)
        for pair in range(PAIRS):
            run_rows[pair, :, rows] = across[2 * pair : 2 * pair + 2, :]
        overlap[c] = jnp.where(triangle(True), dot(c_ref[rows, :], b_ref[rows, :], (1, 1)), 0.0)


def first_half():
    return lax.broadcasted_iota(jnp.int32, (CHUNK, LANES), 1) < WIDTH


def apart(v):
    first = first_half()
    return jnp.concatenate([jnp.where(first, v, 0.0), jnp.where(first, 0.0, v)], axis=0).astype(BF16)


def decays(columns, run_rows, pair, rows):
    out = []
    for h in range(2):
        across = run_rows[pair, h : h + 1, rows]
        out.append(jnp.exp(jnp.minimum(columns[:, h * CHUNK : (h + 1) * CHUNK] - across, 0.0)))
    return out


def forward_kernel(x_ref, g_ref, b_ref, bt_ref, c_ref, raw_ref, raw_t_ref, bias_ref, rate_ref,
                   bias_t_ref, rate_t_ref, skip_ref, gain_ref,
                   low_ref, scan_ref, gated_ref, state_ref, scale_ref,
                   step_pack, run_pack, run_rows, step_rows, overlap, squares):
    pair = pl.program_id(0)

    @pl.when(pair == 0)
    def _():
        prepare(raw_ref, raw_t_ref, bias_ref, rate_ref, bias_t_ref, rate_t_ref, b_ref, c_ref,
                step_pack, run_pack, run_rows, step_rows, overlap)
        squares[...] = jnp.zeros_like(squares)

    narrow, wide = picker(pair, WIDTH), picker(pair, CHUNK)
    skip = skip_ref[:, pl.ds(pl.multiple_of(pair * LANES, LANES), LANES)]
    state = None
    for c in range(CHUNKS):
        rows = slice(c * CHUNK, (c + 1) * CHUNK)
        x = x_ref[rows, :].astype(F32)
        step = dot(step_pack[rows, :], narrow)
        run = dot(run_pack[rows, :], narrow)
        columns = dot(run_pack[rows, :], wide)
        weights = []
        for h, one in enumerate(decays(columns, run_rows, pair, rows)):
            weights.append(halves(one * overlap[c] * step_rows[pair, h : h + 1, rows]))
        x_apart = apart(x)
        y = dot(
            jnp.concatenate([weights[h][part] for part in range(2) for h in range(2)], axis=1),
            jnp.concatenate([x_apart, x_apart], axis=0),
        )
        if c > 0:
            state_ref[0, c - 1] = state
            held = jnp.concatenate(halves(state), axis=1)
            y = y + jnp.exp(run) * folded(dot(c_ref[rows, :], held))
        if c < CHUNKS - 1:
            end = run[CHUNK - 1 :, :]
            fresh = jnp.concatenate(halves(x * step * jnp.exp(end - run)), axis=1)
            local = folded(dot(bt_ref[:, rows], fresh))
            state = local if c == 0 else jnp.exp(end) * state + local
        scan_ref[rows, :] = y
        g = g_ref[rows, :].astype(F32)
        gated = (y + skip * x) * (g / (1.0 + jnp.exp(-g)))
        gated_ref[rows, pl.ds(pl.multiple_of(pair * LANES, LANES), LANES)] = gated
        squares[rows, :] += gated * gated

    @pl.when(pair == PAIRS - 1)
    def _():
        for c in range(CHUNKS):
            rows = slice(c * CHUNK, (c + 1) * CHUNK)
            mean = jnp.sum(squares[rows, :], axis=1, keepdims=True) * (1.0 / CHANNELS)
            scale = lax.rsqrt(mean + EPS)
            scale_ref[rows, :] = jnp.broadcast_to(scale, (CHUNK, LANES))
            low_ref[:, rows] = (gated_ref[rows, :] * scale * gain_ref[...]).T.astype(BF16)


def backward_kernel(x_ref, g_ref, cot_ref, scan_ref, state_ref, scale_ref, pull_ref,
                    b_ref, c_ref, ct_ref, raw_ref, raw_t_ref, bias_ref, rate_ref,
                    bias_t_ref, rate_t_ref, skip_ref, gain_ref,
                    dx_ref, dg_ref, db_ref, dc_ref, step_ref, small_ref,
                    step_pack, run_pack, run_rows, step_rows, overlap, d_overlap, d_b, d_c, flow, direct, lanes):
    pair = pl.program_id(0)

    @pl.when(pair == 0)
    def _():
        prepare(raw_ref, raw_t_ref, bias_ref, rate_ref, bias_t_ref, rate_t_ref, b_ref, c_ref,
                step_pack, run_pack, run_rows, step_rows, overlap)
        for held in (d_overlap, d_b, d_c, flow, direct, lanes):
            held[...] = jnp.zeros_like(held)

    narrow, wide = picker(pair, WIDTH), picker(pair, CHUNK)
    here = pl.ds(pl.multiple_of(pair * LANES, LANES), LANES)
    skip, gain = skip_ref[:, here], gain_ref[:, here]
    first = first_half()
    lane = lax.broadcasted_iota(jnp.int32, (CHUNK, LANES), 1)

    def by_head(v):
        one = jnp.sum(jnp.where(first, v, 0.0), axis=1, keepdims=True)
        two = jnp.sum(jnp.where(first, 0.0, v), axis=1, keepdims=True)
        return jnp.where(lane == 2 * pair, one, jnp.where(lane == 2 * pair + 1, two, 0.0))

    d_state = None
    skip_sum = jnp.zeros((1, LANES), F32)
    for c in reversed(range(CHUNKS)):
        rows = slice(c * CHUNK, (c + 1) * CHUNK)
        x = x_ref[rows, :].astype(F32)
        g = g_ref[rows, :].astype(F32)
        scan = scan_ref[rows, :]
        out = scan + skip * x
        sig = 1.0 / (1.0 + jnp.exp(-g))
        silu = g * sig
        d_gated = scale_ref[rows, :] * gain * cot_ref[rows, :] - out * silu * pull_ref[rows, :]
        dy = d_gated * silu
        dg_ref[rows, :] = (d_gated * out * (sig + silu * (1.0 - sig))).astype(BF16)
        skip_sum = skip_sum + jnp.sum(dy * x, axis=0, keepdims=True)

        step = dot(step_pack[rows, :], narrow)
        run = dot(run_pack[rows, :], narrow)
        columns = dot(run_pack[rows, :], wide)
        driven = x * step
        dy_hi, dy_low = (apart(part.astype(F32)) for part in halves(dy))
        factor = decays(columns, run_rows, pair, rows)
        products = dot(
            jnp.concatenate([dy_hi, dy_low], axis=1),
            jnp.concatenate([x_ref[rows, :], x_ref[rows, :]], axis=1),
            (1, 1),
        )
        step_row = step_rows[pair, :, rows]
        d_overlap[c] += (
            factor[0] * products[:CHUNK] * step_row[:1] + factor[1] * products[CHUNK:] * step_row[1:]
        )
        weights = [halves(one * overlap[c]) for one in factor]
        weights_hi = jnp.concatenate([one[0] for one in weights], axis=0)
        weights_low = jnp.concatenate([one[1] for one in weights], axis=0)
        d_driven = folded(dot(weights_hi, jnp.concatenate([dy_hi, dy_low], axis=1), (0, 0)))
        d_driven = d_driven + dot(weights_low, dy_hi, (0, 0))
        entering_hi, entering_low = halves(dy * jnp.exp(run))
        entering = jnp.concatenate([entering_hi, entering_low], axis=1)
        end = run[CHUNK - 1 :, :]
        if c > 0:
            held = state_ref[0, c - 1]
            held_hi, held_low = halves(held)
            d_c[rows, :] += dot(
                entering, jnp.concatenate([held_hi, held_hi], axis=1), (1, 1)
            ) + dot(entering_hi, held_low, (1, 1))
        if c < CHUNKS - 1:
            to_end = jnp.exp(end - run)
            d_hi, d_low = halves(d_state)
            from_state = to_end * folded(
                dot(b_ref[rows, :], jnp.concatenate([d_hi, d_low], axis=1))
            )
            fresh_hi, fresh_low = halves(driven * to_end)
            d_b[rows, :] += dot(
                jnp.concatenate([fresh_hi, fresh_low], axis=1),
                jnp.concatenate([d_hi, d_hi], axis=1),
                (1, 1),
            ) + dot(fresh_hi, d_low, (1, 1))
            crossing = jnp.sum(driven * from_state, axis=0, keepdims=True)
            if c > 0:
                carried = jnp.sum(held * d_state, axis=0, keepdims=True)
                crossing = crossing + jnp.exp(end) * carried
            lanes[c : c + 1, here] = crossing
            d_driven = d_driven + from_state
        if c > 0:
            back = folded(dot(ct_ref[:, rows], entering))
            d_state = back if d_state is None else jnp.exp(end) * d_state + back
        flow[rows, :] += by_head(dy * scan - driven * d_driven)
        direct[rows, :] += by_head(x * d_driven)
        dx_ref[rows, :] = (step * d_driven + skip * dy).astype(BF16)
    lanes[CHUNKS : CHUNKS + 1, here] = skip_sum

    @pl.when(pair == PAIRS - 1)
    def _():
        channel = lax.broadcasted_iota(jnp.int32, (CHANNELS, LANES), 0) // WIDTH
        head = lax.broadcasted_iota(jnp.int32, (CHANNELS, LANES), 1)
        gather = jnp.where(channel == head, 1.0, 0.0).astype(BF16)
        heads = sum(dot(part.astype(BF16), gather) for part in three_parts(lanes[...]))
        step_all, decay_all = steps_of(raw_ref, bias_ref, rate_ref)
        rate = jnp.exp(rate_ref[...])
        upper = jnp.where(triangle(False), 1.0, 0.0).astype(BF16)
        keep = lane < HEADS
        rate_sum = jnp.zeros((1, LANES), F32)
        bias_sum = jnp.zeros((1, LANES), F32)
        for c in range(CHUNKS):
            rows = slice(c * CHUNK, (c + 1) * CHUNK)
            d_decay = sum(dot(upper, part.astype(BF16)) for part in three_parts(flow[rows, :]))
            d_decay = d_decay + heads[c : c + 1, :]
            d_step = direct[rows, :] - d_decay * rate
            before = raw_ref[rows, :].astype(F32) + bias_ref[...]
            d_raw = jnp.where(keep, d_step / (1.0 + jnp.exp(-before)), 0.0)
            step_ref[rows, :] = d_raw[:, :HEADS]
            bias_sum = bias_sum + jnp.sum(d_raw, axis=0, keepdims=True)
            rate_sum = rate_sum + jnp.sum(
                jnp.where(keep, d_decay * decay_all[rows], 0.0), axis=0, keepdims=True
            )
            d_hi, d_low = halves(jnp.where(triangle(True), d_overlap[c], 0.0))
            dc_ref[rows, :] = (
                d_c[rows, :] + dot(d_hi, b_ref[rows, :]) + dot(d_low, b_ref[rows, :])
            ).astype(BF16)
            db_ref[rows, :] = (
                d_b[rows, :] + dot(d_hi, c_ref[rows, :], (0, 0)) + dot(d_low, c_ref[rows, :], (0, 0))
            ).astype(BF16)
        small_ref[...] = jnp.concatenate(
            [rate_sum, bias_sum, heads[CHUNKS : CHUNKS + 1, :], jnp.zeros((5, LANES), F32)], axis=0
        )


def whole(shape):
    return pl.BlockSpec(shape, lambda *_: (0,) * len(shape))


def by_pair(rows):
    return pl.BlockSpec((rows, LANES), lambda p, *_: (0, p))


VMEM_LIMIT = 56 * 1024 * 1024

TABLES = [
    pltpu.VMEM((TOKENS, LANES), BF16),
    pltpu.VMEM((TOKENS, LANES), BF16),
    pltpu.VMEM((PAIRS, 2, TOKENS), F32),
    pltpu.VMEM((PAIRS, 2, TOKENS), F32),
    pltpu.VMEM((CHUNKS, CHUNK, CHUNK), F32),
]

PARAMETERS = [
    whole((TOKENS, LANES)),
    whole((HEADS, TOKENS)),
    whole((1, LANES)),
    whole((1, LANES)),
    whole((HEADS, 1)),
    whole((HEADS, 1)),
    whole((1, CHANNELS)),
    whole((1, CHANNELS)),
]


def scan_forward(x, g, b, bt, c, parameters):
    return pl.pallas_call(
        forward_kernel,
        grid=(PAIRS,),
        in_specs=[
            by_pair(TOKENS),
            by_pair(TOKENS),
            whole((TOKENS, STATE)),
            whole((STATE, TOKENS)),
            whole((TOKENS, STATE)),
        ]
        + PARAMETERS,
        out_specs=[
            whole((CHANNELS, TOKENS)),
            by_pair(TOKENS),
            whole((TOKENS, CHANNELS)),
            pl.BlockSpec((1, CHUNKS - 1, STATE, LANES), lambda p: (p, 0, 0, 0)),
            whole((TOKENS, LANES)),
        ],
        out_shape=[
            jax.ShapeDtypeStruct((CHANNELS, TOKENS), BF16),
            jax.ShapeDtypeStruct((TOKENS, CHANNELS), F32),
            jax.ShapeDtypeStruct((TOKENS, CHANNELS), F32),
            jax.ShapeDtypeStruct((PAIRS, CHUNKS - 1, STATE, LANES), F32),
            jax.ShapeDtypeStruct((TOKENS, LANES), F32),
        ],
        scratch_shapes=TABLES + [pltpu.VMEM((TOKENS, LANES), F32)],
        compiler_params=pltpu.CompilerParams(vmem_limit_bytes=VMEM_LIMIT),
        cost_estimate=pl.CostEstimate(flops=16 * 10**9, bytes_accessed=10**7, transcendentals=0),
        name="scan_forward",
    )(x, g, b, bt, c, *parameters)


def scan_backward(x, g, cot, scan, states, scale, pull, b, c, ct, parameters):
    return pl.pallas_call(
        backward_kernel,
        grid=(PAIRS,),
        in_specs=[
            by_pair(TOKENS),
            by_pair(TOKENS),
            by_pair(TOKENS),
            by_pair(TOKENS),
            pl.BlockSpec((1, CHUNKS - 1, STATE, LANES), lambda p: (p, 0, 0, 0)),
            whole((TOKENS, LANES)),
            whole((TOKENS, LANES)),
            whole((TOKENS, STATE)),
            whole((TOKENS, STATE)),
            whole((STATE, TOKENS)),
        ]
        + PARAMETERS,
        out_specs=[
            by_pair(TOKENS),
            by_pair(TOKENS),
            whole((TOKENS, STATE)),
            whole((TOKENS, STATE)),
            whole((TOKENS, HEADS)),
            whole((8, LANES)),
        ],
        out_shape=[
            jax.ShapeDtypeStruct((TOKENS, CHANNELS), BF16),
            jax.ShapeDtypeStruct((TOKENS, CHANNELS), BF16),
            jax.ShapeDtypeStruct((TOKENS, STATE), BF16),
            jax.ShapeDtypeStruct((TOKENS, STATE), BF16),
            jax.ShapeDtypeStruct((TOKENS, HEADS), F32),
            jax.ShapeDtypeStruct((8, LANES), F32),
        ],
        scratch_shapes=TABLES
        + [
            pltpu.VMEM((CHUNKS, CHUNK, CHUNK), F32),
            pltpu.VMEM((TOKENS, STATE), F32),
            pltpu.VMEM((TOKENS, STATE), F32),
            pltpu.VMEM((TOKENS, LANES), F32),
            pltpu.VMEM((TOKENS, LANES), F32),
            pltpu.VMEM((8, CHANNELS), F32),
        ],
        compiler_params=pltpu.CompilerParams(vmem_limit_bytes=VMEM_LIMIT),
        cost_estimate=pl.CostEstimate(flops=20 * 10**9, bytes_accessed=10**7, transcendentals=0),
        name="scan_backward",
    )(x, g, cot, scan, states, scale, pull, b, c, ct, *parameters)


FEATURES = 512
BLOCK = 128
SHARDS = 8


def term_kernel(count, added, placed, places, *refs):
    pieces, low_ref = refs[: 2 * count], refs[2 * count]
    sent_refs = refs[2 * count + 1 : -3]
    out_ref, held, done = refs[-3:]
    per = 2 * CHANNELS
    sent = [
        ref.at[start : start + per] for ref in sent_refs for start in range(0, ref.shape[0], per)
    ]
    copies = []
    for k in range(count):
        blocks = [piece[...] for piece in pieces[2 * k : 2 * k + 2]]
        term = dot(low_ref[...], jnp.concatenate(blocks, axis=1))
        for slot in range(2):
            n = 2 * k + slot
            here = slice(n * CHANNELS, (n + 1) * CHANNELS)
            part = term[:, slot * BLOCK : (slot + 1) * BLOCK]
            if added:
                part = part + sent[k][slot * CHANNELS : (slot + 1) * CHANNELS, :].astype(F32)
            held[here, :] = part.astype(BF16)
            start = n * CHANNELS
            if placed:
                start = pl.multiple_of((places[k] * 2 + slot) * CHANNELS, CHANNELS)
            copies.append(
                pltpu.make_async_copy(
                    held.at[here], out_ref.at[pl.ds(start, CHANNELS)], done.at[n]
                )
            )
            copies[-1].start()
    for copy in copies:
        copy.wait()


def terms(places, blocks, pieces, low, sent=()):
    count = len(pieces)
    added = len(sent) > 0
    rows = 2 * CHANNELS * count
    specs = [whole(part.shape) for part in sent]

    def kernel(*refs):
        term_kernel(count, added, added, *refs)

    def lanes(slot):
        return pl.BlockSpec((TOKENS, BLOCK), lambda _, at: (0, at[count + slot]))

    return pl.pallas_call(
        kernel,
        grid_spec=pltpu.PrefetchScalarGridSpec(
            num_scalar_prefetch=1,
            grid=(1,),
            in_specs=[lanes(0), lanes(1)] * count + [whole((CHANNELS, TOKENS))] + specs,
            out_specs=pl.BlockSpec(memory_space=pl.ANY),
            scratch_shapes=[
                pltpu.VMEM((2 * count * CHANNELS, BLOCK), BF16),
                pltpu.SemaphoreType.DMA((2 * count,)),
            ],
        ),
        out_shape=jax.ShapeDtypeStruct((rows, BLOCK), BF16),
        compiler_params=pltpu.CompilerParams(vmem_limit_bytes=VMEM_LIMIT),
        cost_estimate=pl.CostEstimate(
            flops=(count + 1) * 7 * 10**8, bytes_accessed=2 * 10**6, transcendentals=0
        ),
        name="terms_added" if added else "terms",
    )(
        jnp.stack(list(places) + list(blocks)).astype(jnp.int32),
        *[piece for piece in pieces for _ in range(2)],
        low,
        *sent,
    )


def finish_kernel(scale, kept_ref, given_ref, out_ref):
    total = kept_ref[...].astype(F32) + given_ref[...].astype(F32)
    out_ref[...] = (total * scale).T


def finish(plane, given, scale):
    return pl.pallas_call(
        lambda *refs: finish_kernel(scale, *refs),
        grid=(1,),
        in_specs=[pl.BlockSpec((CHANNELS, BLOCK), lambda _: (1, 0)), whole((CHANNELS, BLOCK))],
        out_specs=whole((BLOCK, CHANNELS)),
        out_shape=jax.ShapeDtypeStruct((BLOCK, CHANNELS), F32),
        name="finish",
    )(plane, given)


COLUMNS = 256


def product_kernel(places, *refs):
    pieces = refs[:SHARDS]
    rows_ref, gated_ref, scale_ref, gain_ref = refs[SHARDS : SHARDS + 4]
    cot_ref, gain_grad_ref, pull_ref, sums = refs[SHARDS + 4 :]
    step = pl.program_id(0)
    starts = [pl.multiple_of(places[k] * FEATURES, FEATURES) for k in range(SHARDS)]
    cot_ref[...] = dot(
        jnp.concatenate([piece[...] for piece in pieces], axis=1),
        jnp.concatenate([rows_ref[pl.ds(start, FEATURES), :] for start in starts], axis=0),
    )

    @pl.when(step == 0)
    def _():
        sums[...] = jnp.zeros_like(sums)

    scale = scale_ref[...]
    for half in range(COLUMNS // LANES):
        cols = slice(half * LANES, (half + 1) * LANES)
        with_gated = cot_ref[:, cols] * gated_ref[:, cols]
        gain_grad_ref[:, cols] = jnp.sum(with_gated * scale, axis=0, keepdims=True)
        sums[...] += with_gated * gain_ref[:, cols]

    @pl.when(step == pl.num_programs(0) - 1)
    def _():
        pulled = jnp.sum(sums[...], axis=1, keepdims=True) * (1.0 / CHANNELS)
        pull_ref[...] = scale * scale * scale * pulled


def products(places, pieces, rows, gated, scale, gain):
    depth = SHARDS * FEATURES
    return pl.pallas_call(
        product_kernel,
        grid_spec=pltpu.PrefetchScalarGridSpec(
            num_scalar_prefetch=1,
            grid=(CHANNELS // COLUMNS,),
            in_specs=[whole((TOKENS, FEATURES))] * SHARDS
            + [
                pl.BlockSpec((depth, COLUMNS), lambda n, *_: (0, n)),
                pl.BlockSpec((TOKENS, COLUMNS), lambda n, *_: (0, n)),
                whole((TOKENS, LANES)),
                pl.BlockSpec((1, COLUMNS), lambda n, *_: (0, n)),
            ],
            out_specs=[
                pl.BlockSpec((TOKENS, COLUMNS), lambda n, *_: (0, n)),
                pl.BlockSpec((1, COLUMNS), lambda n, *_: (0, n)),
                whole((TOKENS, LANES)),
            ],
            scratch_shapes=[pltpu.VMEM((TOKENS, LANES), F32)],
        ),
        out_shape=[
            jax.ShapeDtypeStruct((TOKENS, CHANNELS), F32),
            jax.ShapeDtypeStruct((1, CHANNELS), F32),
            jax.ShapeDtypeStruct((TOKENS, LANES), F32),
        ],
        compiler_params=pltpu.CompilerParams(vmem_limit_bytes=VMEM_LIMIT),
        cost_estimate=pl.CostEstimate(
            flops=12 * 10**9, bytes_accessed=16 * 10**6, transcendentals=0
        ),
        name="products",
    )(places, *pieces, rows, gated, scale, gain)


def along_x(step):
    return [(x * 2 + h, (x + step) % 4 * 2 + h) for x in range(4) for h in range(2)]


def beside(shard):
    return lax.ppermute(shard, "tp", along_x(1)), lax.ppermute(shard, "tp", along_x(-1))


def beyond(before, after):
    half = before.shape[0] // 2
    top = lax.ppermute(before[:half], "tp", along_x(1))
    low = lax.ppermute(after[half:], "tp", along_x(-1))
    return top, low


def swap(bit):
    return [(b, b ^ bit) for b in range(32)]


def local_parameters(step_raw, log_rate, step_bias, skip_gain, norm_gain):
    def padded(v):
        return jnp.pad(v, (0, LANES - HEADS)).reshape(1, LANES)

    return (
        jnp.pad(step_raw, ((0, 0), (0, LANES - HEADS))),
        step_raw.T,
        padded(step_bias),
        padded(log_rate),
        step_bias.reshape(HEADS, 1),
        log_rate.reshape(HEADS, 1),
        jnp.repeat(skip_gain, WIDTH).reshape(1, CHANNELS),
        norm_gain.reshape(1, CHANNELS),
    )


def shards(
    scan_input,
    gate_input,
    state_proj,
    step_raw,
    log_rate,
    step_bias,
    skip_gain,
    norm_gain,
    out_proj,
    out_cotangent,
):
    norm_scale = 1.0 / math.sqrt(TOKENS * 32)
    block = lax.axis_index("blk")
    core, y_lo = block % 2, block // 2 % 2
    by_z = [[z * 4 + rest for z in range(8)] for rest in range(4)]
    rows = lax.all_gather(out_proj, "blk", axis=0, tiled=True)
    own = out_cotangent
    partner = lax.ppermute(own, "tp", [(t, t ^ 1) for t in range(8)])
    before, after = beside(own)
    partner, before, after, scan_input = lax.optimization_barrier(
        (partner, before, after, scan_input)
    )
    partner_before, partner_after = beside(partner)
    far_parts = beyond(before, after)

    parameters = local_parameters(step_raw, log_rate, step_bias, skip_gain, norm_gain)
    b, c = state_proj[:, 0, :], state_proj[:, 1, :]
    low, scan, gated, states, scale = scan_forward(
        scan_input, gate_input, b, b.T, c, parameters
    )
    partner_before, partner_after, far_parts, low = lax.optimization_barrier(
        (partner_before, partner_after, far_parts, low)
    )
    far = jnp.concatenate(far_parts, axis=0)
    partner_far = beyond(partner_before, partner_after)
    early = [own, before, after, far, partner, partner_before, partner_after]
    me = lax.axis_index("tp")
    x, h = me // 2, me % 2
    places = [(x + shift) % 4 * 2 + row for row in (h, 1 - h) for shift in (0, 3, 1, 2)]

    mine, mine_y = 2 * y_lo + core, 2 * (1 - y_lo) + core
    theirs, theirs_y = 2 * y_lo + 1 - core, 2 * (1 - y_lo) + 1 - core

    theirs_early = terms(places[:-1], (theirs_y, theirs), early, low)
    theirs_early, partner_far = lax.optimization_barrier((theirs_early, partner_far))
    sent_early = lax.ppermute(theirs_early, "blk", swap(1))
    last = [jnp.concatenate(partner_far, axis=0)]
    sent_last = lax.ppermute(terms(places[-1:], (theirs_y, theirs), last, low), "blk", swap(1))
    both = terms(places, (mine_y, mine), early + last, low, (sent_early, sent_last))
    plane = lax.psum_scatter(
        both, "blk", scatter_dimension=0, tiled=True, axis_index_groups=by_z
    )
    rows, _ = lax.optimization_barrier((rows, both))
    cot, gain_grad, pull = products(
        jnp.stack(places).astype(jnp.int32),
        early + last,
        rows,
        gated,
        scale,
        parameters[-1],
    )
    dx, dg, db, dc, step_grad, small = scan_backward(
        scan_input, gate_input, cot, scan, states, scale, pull, b, c, c.T, parameters
    )
    summed = jnp.concatenate([small, gain_grad.reshape(8, LANES)], axis=0)
    for bit in (1, 2, 4, 8, 16):
        summed = summed + lax.ppermute(summed, "blk", swap(bit))
    plane, summed = lax.optimization_barrier((plane, summed))
    given = lax.ppermute(plane[:CHANNELS], "blk", swap(2))
    weight_grad = finish(plane, given, norm_scale)
    summed = summed * norm_scale
    return (
        dx,
        dg,
        jnp.stack([db, dc], axis=1),
        step_grad,
        weight_grad,
        summed[0, :HEADS],
        summed[1, :HEADS],
        summed[2, :HEADS],
        summed[8:].reshape(CHANNELS),
    )


def solution(mesh):
    placed = (
        P("blk", "tp"),
        P("blk", "tp"),
        P("blk", None, "tp"),
        P("blk", "tp"),
        P("tp"),
        P("tp"),
        P("tp"),
        P("tp"),
        P("blk", "tp"),
        P("blk", "tp"),
    )
    return jax.shard_map(
        shards,
        mesh=mesh,
        in_specs=placed,
        out_specs=(
            P("blk", "tp"),
            P("blk", "tp"),
            P("blk", None, "tp"),
            P("blk", "tp"),
            P("blk", "tp"),
            P("tp"),
            P("tp"),
            P("tp"),
            P("tp"),
        ),
        check_vma=False,
    )
```

```python
import math

import jax
import jax.numpy as jnp
from jax import lax
from jax.experimental import pallas as pl
from jax.experimental.pallas import tpu as pltpu
from jax.sharding import PartitionSpec as P

TOKENS = 512
CHANNELS = 1024
HEADS = 16
WIDTH = 64
STATE = 256
CHUNK = 128
CHUNKS = TOKENS // CHUNK
LANES = 128
PAIRS = HEADS // 2
EPS = 1e-05

F32 = jnp.float32
BF16 = jnp.bfloat16


def dot(a, b, over=(1, 0)):
    return lax.dot_general(
        a, b, (((over[0],), (over[1],)), ((), ())), preferred_element_type=F32
    )


def three_parts(v):
    hi = v.astype(BF16).astype(F32)
    rest = v - hi
    mid = rest.astype(BF16).astype(F32)
    return hi, mid, rest - mid


def packed(v):
    hi, mid, low = three_parts(v)
    return hi + pltpu.roll(mid, HEADS, 1) + pltpu.roll(low, 2 * HEADS, 1)


def halves(v):
    hi = v.astype(BF16)
    return hi, (v - hi.astype(F32)).astype(BF16)


def folded(v):
    middle = v.shape[1] // 2
    return v[:, :middle] + v[:, middle:]


def triangle(lower):
    i = lax.broadcasted_iota(jnp.int32, (CHUNK, CHUNK), 0)
    j = lax.broadcasted_iota(jnp.int32, (CHUNK, CHUNK), 1)
    return i >= j if lower else i <= j


def picker(pair):
    row = lax.broadcasted_iota(jnp.int32, (LANES, 4 * LANES), 0)
    col = lax.broadcasted_iota(jnp.int32, (LANES, 4 * LANES), 1)
    narrow = col < 2 * LANES
    head = 2 * pair + jnp.where(narrow, (col % LANES) // WIDTH, col // CHUNK - 2)
    first = jnp.where(col < LANES, 0, 3 * HEADS)
    hit = (row % HEADS == head) & (row >= first) & (row < first + 3 * HEADS)
    return jnp.where(hit, 1.0, 0.0).astype(BF16)


def softplus(v):
    return jnp.maximum(v, 0.0) + jnp.log1p(jnp.exp(-jnp.abs(v)))


def head_lanes():
    return lax.broadcasted_iota(jnp.int32, (TOKENS, LANES), 1) < HEADS


def steps_of(raw_ref, bias_ref, rate_ref):
    step = jnp.where(head_lanes(), softplus(raw_ref[...].astype(F32) + bias_ref[...]), 0.0)
    return step, -step * jnp.exp(rate_ref[...])


def prepare(raw_ref, raw_t_ref, bias_ref, rate_ref, bias_t_ref, rate_t_ref, b_ref, c_ref,
            pack, run_rows, step_rows, overlap):
    step, decay = steps_of(raw_ref, bias_ref, rate_ref)
    step_pack = packed(step)
    lower = jnp.where(triangle(True), 1.0, 0.0).astype(BF16)
    upper = jnp.where(triangle(False), 1.0, 0.0).astype(BF16)
    decay_pack = packed(decay).astype(BF16)
    keep = lax.broadcasted_iota(jnp.int32, (CHUNK, LANES), 1) < HEADS
    step_t = softplus(raw_t_ref[...].astype(F32) + bias_t_ref[...])
    decay_t = three_parts(-step_t * jnp.exp(rate_t_ref[...]))
    for pair in range(PAIRS):
        step_rows[pair] = step_t[2 * pair : 2 * pair + 2, :]
    for c in range(CHUNKS):
        rows = slice(c * CHUNK, (c + 1) * CHUNK)
        total = dot(lower, decay_pack[rows])
        total = total + pltpu.roll(total, LANES - HEADS, 1) + pltpu.roll(total, LANES - 2 * HEADS, 1)
        run_pack = pltpu.roll(packed(jnp.where(keep, total, 0.0)), 3 * HEADS, 1)
        pack[rows, :] = (step_pack[rows] + run_pack).astype(BF16)
        across = sum(dot(part[:, rows].astype(BF16), upper) for part in decay_t)
        for pair in range(PAIRS):
            run_rows[pair, :, rows] = across[2 * pair : 2 * pair + 2, :]
        overlap[c] = jnp.where(triangle(True), dot(c_ref[rows, :], b_ref[rows, :], (1, 1)), 0.0)


def first_half():
    return lax.broadcasted_iota(jnp.int32, (CHUNK, LANES), 1) < WIDTH


def apart(v):
    first = first_half()
    return jnp.concatenate([jnp.where(first, v, 0.0), jnp.where(first, 0.0, v)], axis=0).astype(BF16)


def decays(columns, run_rows, pair, rows):
    out = []
    for h in range(2):
        across = run_rows[pair, h : h + 1, rows]
        out.append(jnp.exp(jnp.minimum(columns[:, h * CHUNK : (h + 1) * CHUNK] - across, 0.0)))
    return out


def forward_kernel(x_ref, g_ref, b_ref, bt_ref, c_ref, raw_ref, raw_t_ref, bias_ref, rate_ref,
                   bias_t_ref, rate_t_ref, skip_ref, gain_ref,
                   low_ref, scan_ref, gated_ref, state_ref, scale_ref,
                   pack, run_rows, step_rows, overlap, spread, squares):
    pair = pl.program_id(0)

    @pl.when(pair == 0)
    def _():
        prepare(raw_ref, raw_t_ref, bias_ref, rate_ref, bias_t_ref, rate_t_ref, b_ref, c_ref,
                pack, run_rows, step_rows, overlap)
        squares[...] = jnp.zeros_like(squares)

    spread[...] = dot(pack[...], picker(pair))
    skip = skip_ref[:, pl.ds(pl.multiple_of(pair * LANES, LANES), LANES)]
    state = None
    for c in range(CHUNKS):
        rows = slice(c * CHUNK, (c + 1) * CHUNK)
        x = x_ref[rows, :].astype(F32)
        step, run = spread[rows, :LANES], spread[rows, LANES : 2 * LANES]
        columns = spread[rows, 2 * LANES :]
        weights = []
        for h, one in enumerate(decays(columns, run_rows, pair, rows)):
            weights.append(halves(one * overlap[c] * step_rows[pair, h : h + 1, rows]))
        y = dot(
            jnp.concatenate(
                [
                    jnp.concatenate([weights[h][part] for h in range(2)], axis=1)
                    for part in range(2)
                ],
                axis=0,
            ),
            apart(x),
        )
        y = y[:CHUNK] + y[CHUNK:]
        if c > 0:
            state_ref[0, c - 1] = state
            held = jnp.concatenate(halves(state), axis=1)
            y = y + jnp.exp(run) * folded(dot(c_ref[rows, :], held))
        if c < CHUNKS - 1:
            end = run[CHUNK - 1 :, :]
            fresh = jnp.concatenate(halves(x * step * jnp.exp(end - run)), axis=1)
            local = folded(dot(bt_ref[:, rows], fresh))
            state = local if c == 0 else jnp.exp(end) * state + local
        scan_ref[rows, :] = y
        g = g_ref[rows, :].astype(F32)
        gated = (y + skip * x) * (g / (1.0 + jnp.exp(-g)))
        gated_ref[rows, pl.ds(pl.multiple_of(pair * LANES, LANES), LANES)] = gated
        squares[rows, :] += gated * gated

    @pl.when(pair == PAIRS - 1)
    def _():
        for c in range(CHUNKS):
            rows = slice(c * CHUNK, (c + 1) * CHUNK)
            mean = jnp.sum(squares[rows, :], axis=1, keepdims=True) * (1.0 / CHANNELS)
            scale = lax.rsqrt(mean + EPS)
            scale_ref[rows, :] = jnp.broadcast_to(scale, (CHUNK, LANES))
            low_ref[:, rows] = (gated_ref[rows, :] * scale * gain_ref[...]).T.astype(BF16)


def backward_kernel(x_ref, g_ref, cot_ref, scan_ref, state_ref, scale_ref, pull_ref,
                    b_ref, c_ref, ct_ref, raw_ref, raw_t_ref, bias_ref, rate_ref,
                    bias_t_ref, rate_t_ref, skip_ref, gain_ref,
                    dx_ref, dg_ref, db_ref, dc_ref, step_ref, small_ref,
                    pack, run_rows, step_rows, overlap, spread, d_overlap, d_b, d_c, flow, direct, lanes):
    pair = pl.program_id(0)

    @pl.when(pair == 0)
    def _():
        prepare(raw_ref, raw_t_ref, bias_ref, rate_ref, bias_t_ref, rate_t_ref, b_ref, c_ref,
                pack, run_rows, step_rows, overlap)
        for held in (d_overlap, d_b, d_c, flow, direct, lanes):
            held[...] = jnp.zeros_like(held)

    spread[...] = dot(pack[...], picker(pair))
    here = pl.ds(pl.multiple_of(pair * LANES, LANES), LANES)
    skip, gain = skip_ref[:, here], gain_ref[:, here]
    first = first_half()
    lane = lax.broadcasted_iota(jnp.int32, (CHUNK, LANES), 1)

    def by_head(v):
        one = jnp.sum(jnp.where(first, v, 0.0), axis=1, keepdims=True)
        two = jnp.sum(jnp.where(first, 0.0, v), axis=1, keepdims=True)
        return jnp.where(lane == 2 * pair, one, jnp.where(lane == 2 * pair + 1, two, 0.0))

    d_state = None
    skip_sum = jnp.zeros((1, LANES), F32)
    for c in reversed(range(CHUNKS)):
        rows = slice(c * CHUNK, (c + 1) * CHUNK)
        x = x_ref[rows, :].astype(F32)
        g = g_ref[rows, :].astype(F32)
        scan = scan_ref[rows, :]
        out = scan + skip * x
        sig = 1.0 / (1.0 + jnp.exp(-g))
        silu = g * sig
        d_gated = scale_ref[rows, :] * gain * cot_ref[rows, :] - out * silu * pull_ref[rows, :]
        dy = d_gated * silu
        dg_ref[rows, :] = (d_gated * out * (sig + silu * (1.0 - sig))).astype(BF16)
        skip_sum = skip_sum + jnp.sum(dy * x, axis=0, keepdims=True)

        step, run = spread[rows, :LANES], spread[rows, LANES : 2 * LANES]
        columns = spread[rows, 2 * LANES :]
        driven = x * step
        dy_hi, dy_low = (apart(part.astype(F32)) for part in halves(dy))
        factor = decays(columns, run_rows, pair, rows)
        products = dot(
            jnp.concatenate([dy_hi, dy_low], axis=1),
            jnp.concatenate([x_ref[rows, :], x_ref[rows, :]], axis=1),
            (1, 1),
        )
        step_row = step_rows[pair, :, rows]
        d_overlap[c] += (
            factor[0] * products[:CHUNK] * step_row[:1] + factor[1] * products[CHUNK:] * step_row[1:]
        )
        weights = [halves(one * overlap[c]) for one in factor]
        weights = jnp.concatenate([jnp.concatenate(one, axis=1) for one in weights], axis=0)
        both = dot(weights, jnp.concatenate([dy_hi, dy_low], axis=1), (0, 0))
        d_driven = folded(both[:CHUNK]) + both[CHUNK:, :LANES]
        entering_hi, entering_low = halves(dy * jnp.exp(run))
        entering = jnp.concatenate([entering_hi, entering_low], axis=1)
        end = run[CHUNK - 1 :, :]
        if c > 0:
            held = state_ref[0, c - 1]
            held_hi, held_low = halves(held)
            d_c[rows, :] += dot(
                entering, jnp.concatenate([held_hi, held_hi], axis=1), (1, 1)
            ) + dot(entering_hi, held_low, (1, 1))
        if c < CHUNKS - 1:
            to_end = jnp.exp(end - run)
            d_hi, d_low = halves(d_state)
            from_state = to_end * folded(
                dot(b_ref[rows, :], jnp.concatenate([d_hi, d_low], axis=1))
            )
            fresh_hi, fresh_low = halves(driven * to_end)
            d_b[rows, :] += dot(
                jnp.concatenate([fresh_hi, fresh_low], axis=1),
                jnp.concatenate([d_hi, d_hi], axis=1),
                (1, 1),
            ) + dot(fresh_hi, d_low, (1, 1))
            crossing = jnp.sum(driven * from_state, axis=0, keepdims=True)
            if c > 0:
                carried = jnp.sum(held * d_state, axis=0, keepdims=True)
                crossing = crossing + jnp.exp(end) * carried
            lanes[c : c + 1, here] = crossing
            d_driven = d_driven + from_state
        if c > 0:
            back = folded(dot(ct_ref[:, rows], entering))
            d_state = back if d_state is None else jnp.exp(end) * d_state + back
        flow[rows, :] += by_head(dy * scan - driven * d_driven)
        direct[rows, :] += by_head(x * d_driven)
        dx_ref[rows, :] = (step * d_driven + skip * dy).astype(BF16)
    lanes[CHUNKS : CHUNKS + 1, here] = skip_sum

    @pl.when(pair == PAIRS - 1)
    def _():
        channel = lax.broadcasted_iota(jnp.int32, (CHANNELS, LANES), 0) // WIDTH
        head = lax.broadcasted_iota(jnp.int32, (CHANNELS, LANES), 1)
        gather = jnp.where(channel == head, 1.0, 0.0).astype(BF16)
        heads = sum(dot(part.astype(BF16), gather) for part in three_parts(lanes[...]))
        step_all, decay_all = steps_of(raw_ref, bias_ref, rate_ref)
        rate = jnp.exp(rate_ref[...])
        upper = jnp.where(triangle(False), 1.0, 0.0).astype(BF16)
        keep = lane < HEADS
        rate_sum = jnp.zeros((1, LANES), F32)
        bias_sum = jnp.zeros((1, LANES), F32)
        for c in range(CHUNKS):
            rows = slice(c * CHUNK, (c + 1) * CHUNK)
            d_decay = sum(dot(upper, part.astype(BF16)) for part in three_parts(flow[rows, :]))
            d_decay = d_decay + heads[c : c + 1, :]
            d_step = direct[rows, :] - d_decay * rate
            before = raw_ref[rows, :].astype(F32) + bias_ref[...]
            d_raw = jnp.where(keep, d_step / (1.0 + jnp.exp(-before)), 0.0)
            step_ref[rows, :] = d_raw[:, :HEADS]
            bias_sum = bias_sum + jnp.sum(d_raw, axis=0, keepdims=True)
            rate_sum = rate_sum + jnp.sum(
                jnp.where(keep, d_decay * decay_all[rows], 0.0), axis=0, keepdims=True
            )
            d_hi, d_low = halves(jnp.where(triangle(True), d_overlap[c], 0.0))
            dc_ref[rows, :] = (
                d_c[rows, :] + dot(d_hi, b_ref[rows, :]) + dot(d_low, b_ref[rows, :])
            ).astype(BF16)
            db_ref[rows, :] = (
                d_b[rows, :] + dot(d_hi, c_ref[rows, :], (0, 0)) + dot(d_low, c_ref[rows, :], (0, 0))
            ).astype(BF16)
        small_ref[...] = jnp.concatenate(
            [rate_sum, bias_sum, heads[CHUNKS : CHUNKS + 1, :], jnp.zeros((5, LANES), F32)], axis=0
        )


def whole(shape):
    return pl.BlockSpec(shape, lambda *_: (0,) * len(shape))


def by_pair(rows):
    return pl.BlockSpec((rows, LANES), lambda p, *_: (0, p))


VMEM_LIMIT = 56 * 1024 * 1024

TABLES = [
    pltpu.VMEM((TOKENS, LANES), BF16),
    pltpu.VMEM((PAIRS, 2, TOKENS), F32),
    pltpu.VMEM((PAIRS, 2, TOKENS), F32),
    pltpu.VMEM((CHUNKS, CHUNK, CHUNK), F32),
    pltpu.VMEM((TOKENS, 4 * LANES), F32),
]

PARAMETERS = [
    whole((TOKENS, LANES)),
    whole((HEADS, TOKENS)),
    whole((1, LANES)),
    whole((1, LANES)),
    whole((HEADS, 1)),
    whole((HEADS, 1)),
    whole((1, CHANNELS)),
    whole((1, CHANNELS)),
]


def scan_forward(x, g, b, bt, c, parameters):
    return pl.pallas_call(
        forward_kernel,
        grid=(PAIRS,),
        in_specs=[
            by_pair(TOKENS),
            by_pair(TOKENS),
            whole((TOKENS, STATE)),
            whole((STATE, TOKENS)),
            whole((TOKENS, STATE)),
        ]
        + PARAMETERS,
        out_specs=[
            whole((CHANNELS, TOKENS)),
            by_pair(TOKENS),
            whole((TOKENS, CHANNELS)),
            pl.BlockSpec((1, CHUNKS - 1, STATE, LANES), lambda p: (p, 0, 0, 0)),
            whole((TOKENS, LANES)),
        ],
        out_shape=[
            jax.ShapeDtypeStruct((CHANNELS, TOKENS), BF16),
            jax.ShapeDtypeStruct((TOKENS, CHANNELS), F32),
            jax.ShapeDtypeStruct((TOKENS, CHANNELS), F32),
            jax.ShapeDtypeStruct((PAIRS, CHUNKS - 1, STATE, LANES), F32),
            jax.ShapeDtypeStruct((TOKENS, LANES), F32),
        ],
        scratch_shapes=TABLES + [pltpu.VMEM((TOKENS, LANES), F32)],
        compiler_params=pltpu.CompilerParams(vmem_limit_bytes=VMEM_LIMIT),
        cost_estimate=pl.CostEstimate(flops=16 * 10**9, bytes_accessed=10**7, transcendentals=0),
        name="scan_forward",
    )(x, g, b, bt, c, *parameters)


def scan_backward(x, g, cot, scan, states, scale, pull, b, c, ct, parameters):
    return pl.pallas_call(
        backward_kernel,
        grid=(PAIRS,),
        in_specs=[
            by_pair(TOKENS),
            by_pair(TOKENS),
            by_pair(TOKENS),
            by_pair(TOKENS),
            pl.BlockSpec((1, CHUNKS - 1, STATE, LANES), lambda p: (p, 0, 0, 0)),
            whole((TOKENS, LANES)),
            whole((TOKENS, LANES)),
            whole((TOKENS, STATE)),
            whole((TOKENS, STATE)),
            whole((STATE, TOKENS)),
        ]
        + PARAMETERS,
        out_specs=[
            by_pair(TOKENS),
            by_pair(TOKENS),
            whole((TOKENS, STATE)),
            whole((TOKENS, STATE)),
            whole((TOKENS, HEADS)),
            whole((8, LANES)),
        ],
        out_shape=[
            jax.ShapeDtypeStruct((TOKENS, CHANNELS), BF16),
            jax.ShapeDtypeStruct((TOKENS, CHANNELS), BF16),
            jax.ShapeDtypeStruct((TOKENS, STATE), BF16),
            jax.ShapeDtypeStruct((TOKENS, STATE), BF16),
            jax.ShapeDtypeStruct((TOKENS, HEADS), F32),
            jax.ShapeDtypeStruct((8, LANES), F32),
        ],
        scratch_shapes=TABLES
        + [
            pltpu.VMEM((CHUNKS, CHUNK, CHUNK), F32),
            pltpu.VMEM((TOKENS, STATE), F32),
            pltpu.VMEM((TOKENS, STATE), F32),
            pltpu.VMEM((TOKENS, LANES), F32),
            pltpu.VMEM((TOKENS, LANES), F32),
            pltpu.VMEM((8, CHANNELS), F32),
        ],
        compiler_params=pltpu.CompilerParams(vmem_limit_bytes=VMEM_LIMIT),
        cost_estimate=pl.CostEstimate(flops=20 * 10**9, bytes_accessed=10**7, transcendentals=0),
        name="scan_backward",
    )(x, g, cot, scan, states, scale, pull, b, c, ct, *parameters)


FEATURES = 512
BLOCK = 128
SHARDS = 8


def term_kernel(count, added, placed, places, *refs):
    pieces, low_ref = refs[: 2 * count], refs[2 * count]
    sent_refs = refs[2 * count + 1 : -3]
    out_ref, held, done = refs[-3:]
    per = 2 * CHANNELS
    sent = [
        ref.at[start : start + per] for ref in sent_refs for start in range(0, ref.shape[0], per)
    ]
    copies = []
    for k in range(count):
        blocks = [piece[...] for piece in pieces[2 * k : 2 * k + 2]]
        term = dot(low_ref[...], jnp.concatenate(blocks, axis=1))
        for slot in range(2):
            n = 2 * k + slot
            here = slice(n * CHANNELS, (n + 1) * CHANNELS)
            part = term[:, slot * BLOCK : (slot + 1) * BLOCK]
            if added:
                part = part + sent[k][slot * CHANNELS : (slot + 1) * CHANNELS, :].astype(F32)
            held[here, :] = part.astype(BF16)
            start = n * CHANNELS
            if placed:
                start = pl.multiple_of((places[k] * 2 + slot) * CHANNELS, CHANNELS)
            copies.append(
                pltpu.make_async_copy(
                    held.at[here], out_ref.at[pl.ds(start, CHANNELS)], done.at[n]
                )
            )
            copies[-1].start()
    for copy in copies:
        copy.wait()


def terms(places, blocks, pieces, low, sent=()):
    count = len(pieces)
    added = len(sent) > 0
    rows = 2 * CHANNELS * count
    specs = [whole(part.shape) for part in sent]

    def kernel(*refs):
        term_kernel(count, added, added, *refs)

    def lanes(slot):
        return pl.BlockSpec((TOKENS, BLOCK), lambda _, at: (0, at[count + slot]))

    return pl.pallas_call(
        kernel,
        grid_spec=pltpu.PrefetchScalarGridSpec(
            num_scalar_prefetch=1,
            grid=(1,),
            in_specs=[lanes(0), lanes(1)] * count + [whole((CHANNELS, TOKENS))] + specs,
            out_specs=pl.BlockSpec(memory_space=pl.ANY),
            scratch_shapes=[
                pltpu.VMEM((2 * count * CHANNELS, BLOCK), BF16),
                pltpu.SemaphoreType.DMA((2 * count,)),
            ],
        ),
        out_shape=jax.ShapeDtypeStruct((rows, BLOCK), BF16),
        compiler_params=pltpu.CompilerParams(vmem_limit_bytes=VMEM_LIMIT),
        cost_estimate=pl.CostEstimate(
            flops=(count + 1) * 7 * 10**8, bytes_accessed=2 * 10**6, transcendentals=0
        ),
        name="terms_added" if added else "terms",
    )(
        jnp.stack(list(places) + list(blocks)).astype(jnp.int32),
        *[piece for piece in pieces for _ in range(2)],
        low,
        *sent,
    )


def finish_kernel(scale, kept_ref, given_ref, out_ref):
    total = kept_ref[...].astype(F32) + given_ref[...].astype(F32)
    out_ref[...] = (total * scale).T


def finish(plane, given, scale):
    return pl.pallas_call(
        lambda *refs: finish_kernel(scale, *refs),
        grid=(1,),
        in_specs=[pl.BlockSpec((CHANNELS, BLOCK), lambda _: (1, 0)), whole((CHANNELS, BLOCK))],
        out_specs=whole((BLOCK, CHANNELS)),
        out_shape=jax.ShapeDtypeStruct((BLOCK, CHANNELS), F32),
        name="finish",
    )(plane, given)


COLUMNS = 256


def product_kernel(places, *refs):
    pieces = refs[:SHARDS]
    rows_ref, gated_ref, scale_ref, gain_ref = refs[SHARDS : SHARDS + 4]
    cot_ref, gain_grad_ref, pull_ref, sums = refs[SHARDS + 4 :]
    step = pl.program_id(0)
    starts = [pl.multiple_of(places[k] * FEATURES, FEATURES) for k in range(SHARDS)]
    cot_ref[...] = dot(
        jnp.concatenate([piece[...] for piece in pieces], axis=1),
        jnp.concatenate([rows_ref[pl.ds(start, FEATURES), :] for start in starts], axis=0),
    )

    @pl.when(step == 0)
    def _():
        sums[...] = jnp.zeros_like(sums)

    scale = scale_ref[...]
    for half in range(COLUMNS // LANES):
        cols = slice(half * LANES, (half + 1) * LANES)
        with_gated = cot_ref[:, cols] * gated_ref[:, cols]
        gain_grad_ref[:, cols] = jnp.sum(with_gated * scale, axis=0, keepdims=True)
        sums[...] += with_gated * gain_ref[:, cols]

    @pl.when(step == pl.num_programs(0) - 1)
    def _():
        pulled = jnp.sum(sums[...], axis=1, keepdims=True) * (1.0 / CHANNELS)
        pull_ref[...] = scale * scale * scale * pulled


def products(places, pieces, rows, gated, scale, gain):
    depth = SHARDS * FEATURES
    return pl.pallas_call(
        product_kernel,
        grid_spec=pltpu.PrefetchScalarGridSpec(
            num_scalar_prefetch=1,
            grid=(CHANNELS // COLUMNS,),
            in_specs=[whole((TOKENS, FEATURES))] * SHARDS
            + [
                pl.BlockSpec((depth, COLUMNS), lambda n, *_: (0, n)),
                pl.BlockSpec((TOKENS, COLUMNS), lambda n, *_: (0, n)),
                whole((TOKENS, LANES)),
                pl.BlockSpec((1, COLUMNS), lambda n, *_: (0, n)),
            ],
            out_specs=[
                pl.BlockSpec((TOKENS, COLUMNS), lambda n, *_: (0, n)),
                pl.BlockSpec((1, COLUMNS), lambda n, *_: (0, n)),
                whole((TOKENS, LANES)),
            ],
            scratch_shapes=[pltpu.VMEM((TOKENS, LANES), F32)],
        ),
        out_shape=[
            jax.ShapeDtypeStruct((TOKENS, CHANNELS), F32),
            jax.ShapeDtypeStruct((1, CHANNELS), F32),
            jax.ShapeDtypeStruct((TOKENS, LANES), F32),
        ],
        compiler_params=pltpu.CompilerParams(vmem_limit_bytes=VMEM_LIMIT),
        cost_estimate=pl.CostEstimate(
            flops=12 * 10**9, bytes_accessed=16 * 10**6, transcendentals=0
        ),
        name="products",
    )(places, *pieces, rows, gated, scale, gain)


def along_x(step):
    return [(x * 2 + h, (x + step) % 4 * 2 + h) for x in range(4) for h in range(2)]


def beside(shard):
    return lax.ppermute(shard, "tp", along_x(1)), lax.ppermute(shard, "tp", along_x(-1))


def beyond(before, after):
    half = before.shape[0] // 2
    top = lax.ppermute(before[:half], "tp", along_x(1))
    low = lax.ppermute(after[half:], "tp", along_x(-1))
    return top, low


def swap(bit):
    return [(b, b ^ bit) for b in range(32)]


def local_parameters(step_raw, log_rate, step_bias, skip_gain, norm_gain):
    def padded(v):
        return jnp.pad(v, (0, LANES - HEADS)).reshape(1, LANES)

    return (
        jnp.pad(step_raw, ((0, 0), (0, LANES - HEADS))),
        step_raw.T,
        padded(step_bias),
        padded(log_rate),
        step_bias.reshape(HEADS, 1),
        log_rate.reshape(HEADS, 1),
        jnp.repeat(skip_gain, WIDTH).reshape(1, CHANNELS),
        norm_gain.reshape(1, CHANNELS),
    )


def shards(
    scan_input,
    gate_input,
    state_proj,
    step_raw,
    log_rate,
    step_bias,
    skip_gain,
    norm_gain,
    out_proj,
    out_cotangent,
):
    norm_scale = 1.0 / math.sqrt(TOKENS * 32)
    block = lax.axis_index("blk")
    core, y_lo = block % 2, block // 2 % 2
    by_z = [[z * 4 + rest for z in range(8)] for rest in range(4)]
    rows = lax.all_gather(out_proj, "blk", axis=0, tiled=True)
    own = out_cotangent
    partner = lax.ppermute(own, "tp", [(t, t ^ 1) for t in range(8)])
    before, after = beside(own)
    partner, before, after, scan_input = lax.optimization_barrier(
        (partner, before, after, scan_input)
    )
    partner_before, partner_after = beside(partner)
    far_parts = beyond(before, after)

    parameters = local_parameters(step_raw, log_rate, step_bias, skip_gain, norm_gain)
    b, c = state_proj[:, 0, :], state_proj[:, 1, :]
    low, scan, gated, states, scale = scan_forward(
        scan_input, gate_input, b, b.T, c, parameters
    )
    partner_before, partner_after, far_parts, low = lax.optimization_barrier(
        (partner_before, partner_after, far_parts, low)
    )
    far = jnp.concatenate(far_parts, axis=0)
    partner_far = beyond(partner_before, partner_after)
    early = [own, before, after, far, partner, partner_before, partner_after]
    me = lax.axis_index("tp")
    x, h = me // 2, me % 2
    places = [(x + shift) % 4 * 2 + row for row in (h, 1 - h) for shift in (0, 3, 1, 2)]

    mine, mine_y = 2 * y_lo + core, 2 * (1 - y_lo) + core
    theirs, theirs_y = 2 * y_lo + 1 - core, 2 * (1 - y_lo) + 1 - core

    theirs_early = terms(places[:-1], (theirs_y, theirs), early, low)
    theirs_early, partner_far = lax.optimization_barrier((theirs_early, partner_far))
    sent_early = lax.ppermute(theirs_early, "blk", swap(1))
    last = [jnp.concatenate(partner_far, axis=0)]
    sent_last = lax.ppermute(terms(places[-1:], (theirs_y, theirs), last, low), "blk", swap(1))
    both = terms(places, (mine_y, mine), early + last, low, (sent_early, sent_last))
    plane = lax.psum_scatter(
        both, "blk", scatter_dimension=0, tiled=True, axis_index_groups=by_z
    )
    rows, _ = lax.optimization_barrier((rows, both))
    cot, gain_grad, pull = products(
        jnp.stack(places).astype(jnp.int32),
        early + last,
        rows,
        gated,
        scale,
        parameters[-1],
    )
    dx, dg, db, dc, step_grad, small = scan_backward(
        scan_input, gate_input, cot, scan, states, scale, pull, b, c, c.T, parameters
    )
    summed = jnp.concatenate([small, gain_grad.reshape(8, LANES)], axis=0)
    for bit in (1, 4, 8, 16):
        summed = summed + lax.ppermute(summed, "blk", swap(bit))
    plane, summed = lax.optimization_barrier((plane, summed))
    given = lax.ppermute(plane[:CHANNELS], "blk", swap(2))
    weight_grad = finish(plane, given, norm_scale)
    summed = (summed + lax.ppermute(summed, "blk", swap(2))) * norm_scale
    return (
        dx,
        dg,
        jnp.stack([db, dc], axis=1),
        step_grad,
        weight_grad,
        summed[0, :HEADS],
        summed[1, :HEADS],
        summed[2, :HEADS],
        summed[8:].reshape(CHANNELS),
    )


def solution(mesh):
    placed = (
        P("blk", "tp"),
        P("blk", "tp"),
        P("blk", None, "tp"),
        P("blk", "tp"),
        P("tp"),
        P("tp"),
        P("tp"),
        P("tp"),
        P("blk", "tp"),
        P("blk", "tp"),
    )
    return jax.shard_map(
        shards,
        mesh=mesh,
        in_specs=placed,
        out_specs=(
            P("blk", "tp"),
            P("blk", "tp"),
            P("blk", None, "tp"),
            P("blk", "tp"),
            P("blk", "tp"),
            P("tp"),
            P("tp"),
            P("tp"),
            P("tp"),
        ),
        check_vma=False,
    )
```

```python
import math

import jax
import jax.numpy as jnp
from jax import lax
from jax.experimental import pallas as pl
from jax.experimental.pallas import tpu as pltpu
from jax.sharding import PartitionSpec as P

TOKENS = 512
CHANNELS = 1024
HEADS = 16
WIDTH = 64
STATE = 256
CHUNK = 128
CHUNKS = TOKENS // CHUNK
LANES = 128
PAIRS = HEADS // 2
EPS = 1e-05

F32 = jnp.float32
BF16 = jnp.bfloat16


def dot(a, b, over=(1, 0)):
    return lax.dot_general(
        a, b, (((over[0],), (over[1],)), ((), ())), preferred_element_type=F32
    )


def three_parts(v):
    hi = v.astype(BF16).astype(F32)
    rest = v - hi
    mid = rest.astype(BF16).astype(F32)
    return hi, mid, rest - mid


def packed(v):
    hi, mid, low = three_parts(v)
    return hi + pltpu.roll(mid, HEADS, 1) + pltpu.roll(low, 2 * HEADS, 1)


def halves(v):
    hi = v.astype(BF16)
    return hi, (v - hi.astype(F32)).astype(BF16)


def folded(v):
    middle = v.shape[1] // 2
    return v[:, :middle] + v[:, middle:]


def triangle(lower):
    i = lax.broadcasted_iota(jnp.int32, (CHUNK, CHUNK), 0)
    j = lax.broadcasted_iota(jnp.int32, (CHUNK, CHUNK), 1)
    return i >= j if lower else i <= j


def picker(pair):
    row = lax.broadcasted_iota(jnp.int32, (LANES, 4 * LANES), 0)
    col = lax.broadcasted_iota(jnp.int32, (LANES, 4 * LANES), 1)
    narrow = col < 2 * LANES
    head = 2 * pair + jnp.where(narrow, (col % LANES) // WIDTH, col // CHUNK - 2)
    first = jnp.where(col < LANES, 0, 3 * HEADS)
    hit = (row % HEADS == head) & (row >= first) & (row < first + 3 * HEADS)
    return jnp.where(hit, 1.0, 0.0).astype(BF16)


def softplus(v):
    return jnp.maximum(v, 0.0) + jnp.log1p(jnp.exp(-jnp.abs(v)))


def head_lanes():
    return lax.broadcasted_iota(jnp.int32, (TOKENS, LANES), 1) < HEADS


def steps_of(raw, bias_ref, rate_ref):
    step = jnp.where(head_lanes(), softplus(raw[...] + bias_ref[...]), 0.0)
    return step, -step * jnp.exp(rate_ref[...])


def prepare(raw_t_ref, bias_ref, rate_ref, bc_ref, turned, source,
            raw, pack, run_rows, step_rows, overlap):
    empty = jnp.zeros((CHUNK - HEADS, CHUNK), F32)
    for c in range(CHUNKS):
        rows = slice(c * CHUNK, (c + 1) * CHUNK)
        wide = jnp.concatenate([raw_t_ref[:, rows].astype(F32), empty], axis=0)
        raw[rows, :] = wide.T
        turned[:, rows] = bc_ref[rows, source : source + STATE].astype(F32).T.astype(BF16)
    step, decay = steps_of(raw, bias_ref, rate_ref)
    step_pack = packed(step)
    lower = jnp.where(triangle(True), 1.0, 0.0).astype(BF16)
    upper = jnp.where(triangle(False), 1.0, 0.0).astype(BF16)
    decay_pack = packed(decay).astype(BF16)
    keep = lax.broadcasted_iota(jnp.int32, (CHUNK, LANES), 1) < HEADS
    for c in range(CHUNKS):
        rows = slice(c * CHUNK, (c + 1) * CHUNK)
        total = dot(lower, decay_pack[rows])
        total = total + pltpu.roll(total, LANES - HEADS, 1) + pltpu.roll(total, LANES - 2 * HEADS, 1)
        run_pack = pltpu.roll(packed(jnp.where(keep, total, 0.0)), 3 * HEADS, 1)
        pack[rows, :] = (step_pack[rows] + run_pack).astype(BF16)
        step_t = step[rows].T
        decay_t = three_parts(decay[rows].T[:HEADS])
        across = sum(dot(part.astype(BF16), upper) for part in decay_t)
        for pair in range(PAIRS):
            heads = slice(2 * pair, 2 * pair + 2)
            run_rows[pair, :, rows] = across[heads, :]
            step_rows[pair, :, rows] = step_t[heads, :]
        b, c_low = bc_ref[rows, :STATE], bc_ref[rows, STATE:]
        overlap[c] = jnp.where(triangle(True), dot(c_low, b, (1, 1)), 0.0)


def first_half():
    return lax.broadcasted_iota(jnp.int32, (CHUNK, LANES), 1) < WIDTH


def apart(v):
    first = first_half()
    return jnp.concatenate([jnp.where(first, v, 0.0), jnp.where(first, 0.0, v)], axis=0).astype(BF16)


def decays(columns, run_rows, pair, rows):
    out = []
    for h in range(2):
        across = run_rows[pair, h : h + 1, rows]
        out.append(jnp.exp(jnp.minimum(columns[:, h * CHUNK : (h + 1) * CHUNK] - across, 0.0)))
    return out


def forward_kernel(x_ref, g_ref, bc_ref, raw_t_ref, bias_ref, rate_ref, skip_ref, gain_ref,
                   low_ref, scan_ref, gated_ref, state_ref, scale_ref,
                   raw, pack, run_rows, step_rows, overlap, spread, turned, squares):
    pair = pl.program_id(0)

    @pl.when(pair == 0)
    def _():
        prepare(raw_t_ref, bias_ref, rate_ref, bc_ref, turned, 0,
                raw, pack, run_rows, step_rows, overlap)
        squares[...] = jnp.zeros_like(squares)

    spread[...] = dot(pack[...], picker(pair))
    skip = skip_ref[:, pl.ds(pl.multiple_of(pair * LANES, LANES), LANES)]
    state = None
    for c in range(CHUNKS):
        rows = slice(c * CHUNK, (c + 1) * CHUNK)
        x = x_ref[rows, :].astype(F32)
        step, run = spread[rows, :LANES], spread[rows, LANES : 2 * LANES]
        columns = spread[rows, 2 * LANES :]
        weights = []
        for h, one in enumerate(decays(columns, run_rows, pair, rows)):
            weights.append(halves(one * overlap[c] * step_rows[pair, h : h + 1, rows]))
        y = dot(
            jnp.concatenate(
                [
                    jnp.concatenate([weights[h][part] for h in range(2)], axis=1)
                    for part in range(2)
                ],
                axis=0,
            ),
            apart(x),
        )
        y = y[:CHUNK] + y[CHUNK:]
        if c > 0:
            state_ref[0, c - 1] = state
            held = jnp.concatenate(halves(state), axis=1)
            y = y + jnp.exp(run) * folded(dot(bc_ref[rows, STATE:], held))
        if c < CHUNKS - 1:
            end = run[CHUNK - 1 :, :]
            fresh = jnp.concatenate(halves(x * step * jnp.exp(end - run)), axis=1)
            local = folded(dot(turned[:, rows], fresh))
            state = local if c == 0 else jnp.exp(end) * state + local
        scan_ref[rows, :] = y
        g = g_ref[rows, :].astype(F32)
        gated = (y + skip * x) * (g / (1.0 + jnp.exp(-g)))
        gated_ref[rows, pl.ds(pl.multiple_of(pair * LANES, LANES), LANES)] = gated
        squares[rows, :] += gated * gated

    @pl.when(pair == PAIRS - 1)
    def _():
        for c in range(CHUNKS):
            rows = slice(c * CHUNK, (c + 1) * CHUNK)
            mean = jnp.sum(squares[rows, :], axis=1, keepdims=True) * (1.0 / CHANNELS)
            scale = lax.rsqrt(mean + EPS)
            scale_ref[rows, :] = jnp.broadcast_to(scale, (CHUNK, LANES))
            low_ref[:, rows] = (gated_ref[rows, :] * scale * gain_ref[...]).T.astype(BF16)


def backward_kernel(x_ref, g_ref, cot_ref, scan_ref, state_ref, scale_ref, pull_ref,
                    bc_ref, raw_t_ref, bias_ref, rate_ref, skip_ref, gain_ref,
                    dx_ref, dg_ref, db_ref, dc_ref, step_ref, small_ref,
                    raw, pack, run_rows, step_rows, overlap, spread, turned, d_overlap, d_b, d_c, flow, direct, lanes):
    pair = pl.program_id(0)

    @pl.when(pair == 0)
    def _():
        prepare(raw_t_ref, bias_ref, rate_ref, bc_ref, turned, STATE,
                raw, pack, run_rows, step_rows, overlap)
        for held in (d_overlap, d_b, d_c, flow, direct, lanes):
            held[...] = jnp.zeros_like(held)

    spread[...] = dot(pack[...], picker(pair))
    here = pl.ds(pl.multiple_of(pair * LANES, LANES), LANES)
    skip, gain = skip_ref[:, here], gain_ref[:, here]
    first = first_half()
    lane = lax.broadcasted_iota(jnp.int32, (CHUNK, LANES), 1)

    def by_head(v):
        one = jnp.sum(jnp.where(first, v, 0.0), axis=1, keepdims=True)
        two = jnp.sum(jnp.where(first, 0.0, v), axis=1, keepdims=True)
        return jnp.where(lane == 2 * pair, one, jnp.where(lane == 2 * pair + 1, two, 0.0))

    d_state = None
    skip_sum = jnp.zeros((1, LANES), F32)
    for c in reversed(range(CHUNKS)):
        rows = slice(c * CHUNK, (c + 1) * CHUNK)
        x = x_ref[rows, :].astype(F32)
        g = g_ref[rows, :].astype(F32)
        scan = scan_ref[rows, :]
        out = scan + skip * x
        sig = 1.0 / (1.0 + jnp.exp(-g))
        silu = g * sig
        d_gated = scale_ref[rows, :] * gain * cot_ref[rows, :] - out * silu * pull_ref[rows, :]
        dy = d_gated * silu
        dg_ref[rows, :] = (d_gated * out * (sig + silu * (1.0 - sig))).astype(BF16)
        skip_sum = skip_sum + jnp.sum(dy * x, axis=0, keepdims=True)

        step, run = spread[rows, :LANES], spread[rows, LANES : 2 * LANES]
        columns = spread[rows, 2 * LANES :]
        driven = x * step
        dy_hi, dy_low = (apart(part.astype(F32)) for part in halves(dy))
        factor = decays(columns, run_rows, pair, rows)
        products = dot(
            jnp.concatenate([dy_hi, dy_low], axis=1),
            jnp.concatenate([x_ref[rows, :], x_ref[rows, :]], axis=1),
            (1, 1),
        )
        step_row = step_rows[pair, :, rows]
        d_overlap[c] += (
            factor[0] * products[:CHUNK] * step_row[:1] + factor[1] * products[CHUNK:] * step_row[1:]
        )
        weights = [halves(one * overlap[c]) for one in factor]
        weights = jnp.concatenate([jnp.concatenate(one, axis=1) for one in weights], axis=0)
        both = dot(weights, jnp.concatenate([dy_hi, dy_low], axis=1), (0, 0))
        d_driven = folded(both[:CHUNK]) + both[CHUNK:, :LANES]
        entering_hi, entering_low = halves(dy * jnp.exp(run))
        entering = jnp.concatenate([entering_hi, entering_low], axis=1)
        end = run[CHUNK - 1 :, :]
        if c > 0:
            held = state_ref[0, c - 1]
            held_hi, held_low = halves(held)
            d_c[rows, :] += dot(
                entering, jnp.concatenate([held_hi, held_hi], axis=1), (1, 1)
            ) + dot(entering_hi, held_low, (1, 1))
        if c < CHUNKS - 1:
            to_end = jnp.exp(end - run)
            d_hi, d_low = halves(d_state)
            from_state = to_end * folded(
                dot(bc_ref[rows, :STATE], jnp.concatenate([d_hi, d_low], axis=1))
            )
            fresh_hi, fresh_low = halves(driven * to_end)
            d_b[rows, :] += dot(
                jnp.concatenate([fresh_hi, fresh_low], axis=1),
                jnp.concatenate([d_hi, d_hi], axis=1),
                (1, 1),
            ) + dot(fresh_hi, d_low, (1, 1))
            crossing = jnp.sum(driven * from_state, axis=0, keepdims=True)
            if c > 0:
                carried = jnp.sum(held * d_state, axis=0, keepdims=True)
                crossing = crossing + jnp.exp(end) * carried
            lanes[c : c + 1, here] = crossing
            d_driven = d_driven + from_state
        if c > 0:
            back = folded(dot(turned[:, rows], entering))
            d_state = back if d_state is None else jnp.exp(end) * d_state + back
        flow[rows, :] += by_head(dy * scan - driven * d_driven)
        direct[rows, :] += by_head(x * d_driven)
        dx_ref[rows, :] = (step * d_driven + skip * dy).astype(BF16)
    lanes[CHUNKS : CHUNKS + 1, here] = skip_sum

    @pl.when(pair == PAIRS - 1)
    def _():
        channel = lax.broadcasted_iota(jnp.int32, (CHANNELS, LANES), 0) // WIDTH
        head = lax.broadcasted_iota(jnp.int32, (CHANNELS, LANES), 1)
        gather = jnp.where(channel == head, 1.0, 0.0).astype(BF16)
        heads = sum(dot(part.astype(BF16), gather) for part in three_parts(lanes[...]))
        step_all, decay_all = steps_of(raw, bias_ref, rate_ref)
        rate = jnp.exp(rate_ref[...])
        upper = jnp.where(triangle(False), 1.0, 0.0).astype(BF16)
        keep = lane < HEADS
        rate_sum = jnp.zeros((1, LANES), F32)
        bias_sum = jnp.zeros((1, LANES), F32)
        for c in range(CHUNKS):
            rows = slice(c * CHUNK, (c + 1) * CHUNK)
            d_decay = sum(dot(upper, part.astype(BF16)) for part in three_parts(flow[rows, :]))
            d_decay = d_decay + heads[c : c + 1, :]
            d_step = direct[rows, :] - d_decay * rate
            before = raw[rows, :] + bias_ref[...]
            d_raw = jnp.where(keep, d_step / (1.0 + jnp.exp(-before)), 0.0)
            step_ref[:, rows] = d_raw.T[:HEADS, :]
            bias_sum = bias_sum + jnp.sum(d_raw, axis=0, keepdims=True)
            rate_sum = rate_sum + jnp.sum(
                jnp.where(keep, d_decay * decay_all[rows], 0.0), axis=0, keepdims=True
            )
            d_hi, d_low = halves(jnp.where(triangle(True), d_overlap[c], 0.0))
            dc_ref[rows, :] = (
                d_c[rows, :] + dot(d_hi, bc_ref[rows, :STATE]) + dot(d_low, bc_ref[rows, :STATE])
            ).astype(BF16)
            db_ref[rows, :] = (
                d_b[rows, :]
                + dot(d_hi, bc_ref[rows, STATE:], (0, 0))
                + dot(d_low, bc_ref[rows, STATE:], (0, 0))
            ).astype(BF16)
        small_ref[...] = jnp.concatenate(
            [rate_sum, bias_sum, heads[CHUNKS : CHUNKS + 1, :], jnp.zeros((5, LANES), F32)], axis=0
        )


def whole(shape):
    return pl.BlockSpec(shape, lambda *_: (0,) * len(shape))


def by_pair(rows):
    return pl.BlockSpec((rows, LANES), lambda p, *_: (0, p))


VMEM_LIMIT = 56 * 1024 * 1024

TABLES = [
    pltpu.VMEM((TOKENS, LANES), F32),
    pltpu.VMEM((TOKENS, LANES), BF16),
    pltpu.VMEM((PAIRS, 2, TOKENS), F32),
    pltpu.VMEM((PAIRS, 2, TOKENS), F32),
    pltpu.VMEM((CHUNKS, CHUNK, CHUNK), F32),
    pltpu.VMEM((TOKENS, 4 * LANES), F32),
    pltpu.VMEM((STATE, TOKENS), BF16),
]

PARAMETERS = [
    whole((TOKENS, 2 * STATE)),
    whole((HEADS, TOKENS)),
    whole((1, LANES)),
    whole((1, LANES)),
    whole((1, CHANNELS)),
    whole((1, CHANNELS)),
]


def scan_forward(x, g, parameters):
    return pl.pallas_call(
        forward_kernel,
        grid=(PAIRS,),
        in_specs=[
            by_pair(TOKENS),
            by_pair(TOKENS),
        ]
        + PARAMETERS,
        out_specs=[
            whole((CHANNELS, TOKENS)),
            by_pair(TOKENS),
            whole((TOKENS, CHANNELS)),
            pl.BlockSpec((1, CHUNKS - 1, STATE, LANES), lambda p: (p, 0, 0, 0)),
            whole((TOKENS, LANES)),
        ],
        out_shape=[
            jax.ShapeDtypeStruct((CHANNELS, TOKENS), BF16),
            jax.ShapeDtypeStruct((TOKENS, CHANNELS), F32),
            jax.ShapeDtypeStruct((TOKENS, CHANNELS), F32),
            jax.ShapeDtypeStruct((PAIRS, CHUNKS - 1, STATE, LANES), F32),
            jax.ShapeDtypeStruct((TOKENS, LANES), F32),
        ],
        scratch_shapes=TABLES + [pltpu.VMEM((TOKENS, LANES), F32)],
        compiler_params=pltpu.CompilerParams(vmem_limit_bytes=VMEM_LIMIT),
        cost_estimate=pl.CostEstimate(flops=16 * 10**9, bytes_accessed=10**7, transcendentals=0),
        name="scan_forward",
    )(x, g, *parameters)


def scan_backward(x, g, cot, scan, states, scale, pull, parameters):
    return pl.pallas_call(
        backward_kernel,
        grid=(PAIRS,),
        in_specs=[
            by_pair(TOKENS),
            by_pair(TOKENS),
            by_pair(TOKENS),
            by_pair(TOKENS),
            pl.BlockSpec((1, CHUNKS - 1, STATE, LANES), lambda p: (p, 0, 0, 0)),
            whole((TOKENS, LANES)),
            whole((TOKENS, LANES)),
        ]
        + PARAMETERS,
        out_specs=[
            by_pair(TOKENS),
            by_pair(TOKENS),
            whole((TOKENS, STATE)),
            whole((TOKENS, STATE)),
            whole((HEADS, TOKENS)),
            whole((8, LANES)),
        ],
        out_shape=[
            jax.ShapeDtypeStruct((TOKENS, CHANNELS), BF16),
            jax.ShapeDtypeStruct((TOKENS, CHANNELS), BF16),
            jax.ShapeDtypeStruct((TOKENS, STATE), BF16),
            jax.ShapeDtypeStruct((TOKENS, STATE), BF16),
            jax.ShapeDtypeStruct((HEADS, TOKENS), F32),
            jax.ShapeDtypeStruct((8, LANES), F32),
        ],
        scratch_shapes=TABLES
        + [
            pltpu.VMEM((CHUNKS, CHUNK, CHUNK), F32),
            pltpu.VMEM((TOKENS, STATE), F32),
            pltpu.VMEM((TOKENS, STATE), F32),
            pltpu.VMEM((TOKENS, LANES), F32),
            pltpu.VMEM((TOKENS, LANES), F32),
            pltpu.VMEM((8, CHANNELS), F32),
        ],
        compiler_params=pltpu.CompilerParams(vmem_limit_bytes=VMEM_LIMIT),
        cost_estimate=pl.CostEstimate(flops=20 * 10**9, bytes_accessed=10**7, transcendentals=0),
        name="scan_backward",
    )(x, g, cot, scan, states, scale, pull, *parameters)


FEATURES = 512
BLOCK = 128
SHARDS = 8


def term_kernel(count, added, placed, places, *refs):
    pieces, low_ref = refs[: 2 * count], refs[2 * count]
    sent_refs = refs[2 * count + 1 : -3]
    out_ref, held, done = refs[-3:]
    per = 2 * CHANNELS
    sent = [
        ref.at[start : start + per] for ref in sent_refs for start in range(0, ref.shape[0], per)
    ]
    copies = []
    for k in range(count):
        blocks = [piece[...] for piece in pieces[2 * k : 2 * k + 2]]
        term = dot(low_ref[...], jnp.concatenate(blocks, axis=1))
        for slot in range(2):
            n = 2 * k + slot
            here = slice(n * CHANNELS, (n + 1) * CHANNELS)
            part = term[:, slot * BLOCK : (slot + 1) * BLOCK]
            if added:
                part = part + sent[k][slot * CHANNELS : (slot + 1) * CHANNELS, :].astype(F32)
            held[here, :] = part.astype(BF16)
            start = n * CHANNELS
            if placed:
                start = pl.multiple_of((places[k] * 2 + slot) * CHANNELS, CHANNELS)
            copies.append(
                pltpu.make_async_copy(
                    held.at[here], out_ref.at[pl.ds(start, CHANNELS)], done.at[n]
                )
            )
            copies[-1].start()
    for copy in copies:
        copy.wait()


def terms(places, blocks, pieces, low, sent=()):
    count = len(pieces)
    added = len(sent) > 0
    rows = 2 * CHANNELS * count
    specs = [whole(part.shape) for part in sent]

    def kernel(*refs):
        term_kernel(count, added, added, *refs)

    def lanes(slot):
        return pl.BlockSpec((TOKENS, BLOCK), lambda _, at: (0, at[count + slot]))

    return pl.pallas_call(
        kernel,
        grid_spec=pltpu.PrefetchScalarGridSpec(
            num_scalar_prefetch=1,
            grid=(1,),
            in_specs=[lanes(0), lanes(1)] * count + [whole((CHANNELS, TOKENS))] + specs,
            out_specs=pl.BlockSpec(memory_space=pl.ANY),
            scratch_shapes=[
                pltpu.VMEM((2 * count * CHANNELS, BLOCK), BF16),
                pltpu.SemaphoreType.DMA((2 * count,)),
            ],
        ),
        out_shape=jax.ShapeDtypeStruct((rows, BLOCK), BF16),
        compiler_params=pltpu.CompilerParams(vmem_limit_bytes=VMEM_LIMIT),
        cost_estimate=pl.CostEstimate(
            flops=(count + 1) * 7 * 10**8, bytes_accessed=2 * 10**6, transcendentals=0
        ),
        name="terms_added" if added else "terms",
    )(
        jnp.stack(list(places) + list(blocks)).astype(jnp.int32),
        *[piece for piece in pieces for _ in range(2)],
        low,
        *sent,
    )


def finish_kernel(scale, kept_ref, given_ref, out_ref):
    total = kept_ref[...].astype(F32) + given_ref[...].astype(F32)
    out_ref[...] = (total * scale).T


def finish(plane, given, scale):
    return pl.pallas_call(
        lambda *refs: finish_kernel(scale, *refs),
        grid=(1,),
        in_specs=[pl.BlockSpec((CHANNELS, BLOCK), lambda _: (1, 0)), whole((CHANNELS, BLOCK))],
        out_specs=whole((BLOCK, CHANNELS)),
        out_shape=jax.ShapeDtypeStruct((BLOCK, CHANNELS), F32),
        cost_estimate=pl.CostEstimate(flops=4 * 10**9, bytes_accessed=10**6, transcendentals=0),
        name="finish",
    )(plane, given)


COLUMNS = 256


def product_kernel(places, *refs):
    pieces = refs[:SHARDS]
    rows_ref, gated_ref, scale_ref, gain_ref = refs[SHARDS : SHARDS + 4]
    cot_ref, gain_grad_ref, pull_ref, sums = refs[SHARDS + 4 :]
    step = pl.program_id(0)
    starts = [pl.multiple_of(places[k] * FEATURES, FEATURES) for k in range(SHARDS)]
    cot_ref[...] = dot(
        jnp.concatenate([piece[...] for piece in pieces], axis=1),
        jnp.concatenate([rows_ref[pl.ds(start, FEATURES), :] for start in starts], axis=0),
    )

    @pl.when(step == 0)
    def _():
        sums[...] = jnp.zeros_like(sums)

    scale = scale_ref[...]
    for half in range(COLUMNS // LANES):
        cols = slice(half * LANES, (half + 1) * LANES)
        with_gated = cot_ref[:, cols] * gated_ref[:, cols]
        gain_grad_ref[:, cols] = jnp.sum(with_gated * scale, axis=0, keepdims=True)
        sums[...] += with_gated * gain_ref[:, cols]

    @pl.when(step == pl.num_programs(0) - 1)
    def _():
        pulled = jnp.sum(sums[...], axis=1, keepdims=True) * (1.0 / CHANNELS)
        pull_ref[...] = scale * scale * scale * pulled


def products(places, pieces, rows, gated, scale, gain):
    depth = SHARDS * FEATURES
    return pl.pallas_call(
        product_kernel,
        grid_spec=pltpu.PrefetchScalarGridSpec(
            num_scalar_prefetch=1,
            grid=(CHANNELS // COLUMNS,),
            in_specs=[whole((TOKENS, FEATURES))] * SHARDS
            + [
                pl.BlockSpec((depth, COLUMNS), lambda n, *_: (0, n)),
                pl.BlockSpec((TOKENS, COLUMNS), lambda n, *_: (0, n)),
                whole((TOKENS, LANES)),
                pl.BlockSpec((1, COLUMNS), lambda n, *_: (0, n)),
            ],
            out_specs=[
                pl.BlockSpec((TOKENS, COLUMNS), lambda n, *_: (0, n)),
                pl.BlockSpec((1, COLUMNS), lambda n, *_: (0, n)),
                whole((TOKENS, LANES)),
            ],
            scratch_shapes=[pltpu.VMEM((TOKENS, LANES), F32)],
        ),
        out_shape=[
            jax.ShapeDtypeStruct((TOKENS, CHANNELS), F32),
            jax.ShapeDtypeStruct((1, CHANNELS), F32),
            jax.ShapeDtypeStruct((TOKENS, LANES), F32),
        ],
        compiler_params=pltpu.CompilerParams(vmem_limit_bytes=VMEM_LIMIT),
        cost_estimate=pl.CostEstimate(
            flops=12 * 10**9, bytes_accessed=16 * 10**6, transcendentals=0
        ),
        name="products",
    )(places, *pieces, rows, gated, scale, gain)


def along_x(step):
    return [(x * 2 + h, (x + step) % 4 * 2 + h) for x in range(4) for h in range(2)]


def beside(shard):
    return lax.ppermute(shard, "tp", along_x(1)), lax.ppermute(shard, "tp", along_x(-1))


def beyond(before, after):
    half = before.shape[0] // 2
    top = lax.ppermute(before[:half], "tp", along_x(1))
    low = lax.ppermute(after[half:], "tp", along_x(-1))
    return top, low


def swap(bit):
    return [(b, b ^ bit) for b in range(32)]


def local_parameters(state_proj, step_raw, log_rate, step_bias, skip_gain, norm_gain):
    def padded(v):
        return jnp.pad(v, (0, LANES - HEADS)).reshape(1, LANES)

    return (
        state_proj.reshape(TOKENS, 2 * STATE),
        step_raw.T,
        padded(step_bias),
        padded(log_rate),
        jnp.repeat(skip_gain, WIDTH).reshape(1, CHANNELS),
        norm_gain.reshape(1, CHANNELS),
    )


def shards(
    scan_input,
    gate_input,
    state_proj,
    step_raw,
    log_rate,
    step_bias,
    skip_gain,
    norm_gain,
    out_proj,
    out_cotangent,
):
    norm_scale = 1.0 / math.sqrt(TOKENS * 32)
    block = lax.axis_index("blk")
    core, y_lo = block % 2, block // 2 % 2
    by_z = [[z * 4 + rest for z in range(8)] for rest in range(4)]
    rows = lax.all_gather(out_proj, "blk", axis=0, tiled=True)
    own = out_cotangent
    partner = lax.ppermute(own, "tp", [(t, t ^ 1) for t in range(8)])
    before, after = beside(own)
    partner, before, after, scan_input = lax.optimization_barrier(
        (partner, before, after, scan_input)
    )
    partner_before, partner_after = beside(partner)
    far_parts = beyond(before, after)

    parameters = local_parameters(
        state_proj, step_raw, log_rate, step_bias, skip_gain, norm_gain
    )
    low, scan, gated, states, scale = scan_forward(scan_input, gate_input, parameters)
    partner_before, partner_after, far_parts, low = lax.optimization_barrier(
        (partner_before, partner_after, far_parts, low)
    )
    far = jnp.concatenate(far_parts, axis=0)
    partner_far = beyond(partner_before, partner_after)
    early = [own, before, after, far, partner, partner_before, partner_after]
    me = lax.axis_index("tp")
    x, h = me // 2, me % 2
    places = [(x + shift) % 4 * 2 + row for row in (h, 1 - h) for shift in (0, 3, 1, 2)]

    mine, mine_y = 2 * y_lo + core, 2 * (1 - y_lo) + core
    theirs, theirs_y = 2 * y_lo + 1 - core, 2 * (1 - y_lo) + 1 - core

    theirs_early = terms(places[:-1], (theirs_y, theirs), early, low)
    theirs_early, partner_far = lax.optimization_barrier((theirs_early, partner_far))
    sent_early = lax.ppermute(theirs_early, "blk", swap(1))
    last = [jnp.concatenate(partner_far, axis=0)]
    sent_last = lax.ppermute(terms(places[-1:], (theirs_y, theirs), last, low), "blk", swap(1))
    both = terms(places, (mine_y, mine), early + last, low, (sent_early, sent_last))
    plane = lax.psum_scatter(
        both, "blk", scatter_dimension=0, tiled=True, axis_index_groups=by_z
    )
    rows, _ = lax.optimization_barrier((rows, both))
    cot, gain_grad, pull = products(
        jnp.stack(places).astype(jnp.int32),
        early + last,
        rows,
        gated,
        scale,
        parameters[-1],
    )
    dx, dg, db, dc, step_grad, small = scan_backward(
        scan_input, gate_input, cot, scan, states, scale, pull, parameters
    )
    summed = jnp.concatenate([small, gain_grad.reshape(8, LANES)], axis=0)
    for bit in (1, 4, 8):
        summed = summed + lax.ppermute(summed, "blk", swap(bit))
    state_grad = jnp.stack([db, dc], axis=1)
    plane, summed, state_grad = lax.optimization_barrier((plane, summed, state_grad))
    given = lax.ppermute(plane[:CHANNELS], "blk", swap(2))
    summed = summed + lax.ppermute(summed, "blk", swap(16))
    given, summed = lax.optimization_barrier((given, summed))
    weight_grad = finish(plane, given, norm_scale)
    summed = (summed + lax.ppermute(summed, "blk", swap(2))) * norm_scale
    return (
        dx,
        dg,
        state_grad,
        step_grad.T,
        weight_grad,
        summed[0, :HEADS],
        summed[1, :HEADS],
        summed[2, :HEADS],
        summed[8:].reshape(CHANNELS),
    )


def solution(mesh):
    placed = (
        P("blk", "tp"),
        P("blk", "tp"),
        P("blk", None, "tp"),
        P("blk", "tp"),
        P("tp"),
        P("tp"),
        P("tp"),
        P("tp"),
        P("blk", "tp"),
        P("blk", "tp"),
    )
    return jax.shard_map(
        shards,
        mesh=mesh,
        in_specs=placed,
        out_specs=(
            P("blk", "tp"),
            P("blk", "tp"),
            P("blk", None, "tp"),
            P("blk", "tp"),
            P("blk", "tp"),
            P("tp"),
            P("tp"),
            P("tp"),
            P("tp"),
        ),
        check_vma=False,
    )
```

```python
import math

import jax
import jax.numpy as jnp
from jax import lax
from jax.experimental import pallas as pl
from jax.experimental.pallas import tpu as pltpu
from jax.sharding import PartitionSpec as P

TOKENS = 512
CHANNELS = 1024
HEADS = 16
WIDTH = 64
STATE = 256
CHUNK = 128
CHUNKS = TOKENS // CHUNK
LANES = 128
PAIRS = HEADS // 2
EPS = 1e-05

F32 = jnp.float32
BF16 = jnp.bfloat16


def dot(a, b, over=(1, 0)):
    return lax.dot_general(
        a, b, (((over[0],), (over[1],)), ((), ())), preferred_element_type=F32
    )


def three_parts(v):
    hi = v.astype(BF16).astype(F32)
    rest = v - hi
    mid = rest.astype(BF16).astype(F32)
    return hi, mid, rest - mid


def packed(v):
    hi, mid, low = three_parts(v)
    return hi + pltpu.roll(mid, HEADS, 1) + pltpu.roll(low, 2 * HEADS, 1)


def halves(v):
    hi = v.astype(BF16)
    return hi, (v - hi.astype(F32)).astype(BF16)


def folded(v):
    middle = v.shape[1] // 2
    return v[:, :middle] + v[:, middle:]


def triangle(lower):
    i = lax.broadcasted_iota(jnp.int32, (CHUNK, CHUNK), 0)
    j = lax.broadcasted_iota(jnp.int32, (CHUNK, CHUNK), 1)
    return i >= j if lower else i <= j


def picker(pair):
    row = lax.broadcasted_iota(jnp.int32, (LANES, 4 * LANES), 0)
    col = lax.broadcasted_iota(jnp.int32, (LANES, 4 * LANES), 1)
    narrow = col < 2 * LANES
    head = 2 * pair + jnp.where(narrow, (col % LANES) // WIDTH, col // CHUNK - 2)
    first = jnp.where(col < LANES, 0, 3 * HEADS)
    hit = (row % HEADS == head) & (row >= first) & (row < first + 3 * HEADS)
    return jnp.where(hit, 1.0, 0.0).astype(BF16)


def softplus(v):
    return jnp.maximum(v, 0.0) + jnp.log1p(jnp.exp(-jnp.abs(v)))


def head_lanes():
    return lax.broadcasted_iota(jnp.int32, (TOKENS, LANES), 1) < HEADS


def steps_of(raw, bias_ref, rate_ref):
    step = jnp.where(head_lanes(), softplus(raw[...] + bias_ref[...]), 0.0)
    return step, -step * jnp.exp(rate_ref[...])


def prepare(raw_t_ref, bias_ref, rate_ref, bc_ref, turned, source,
            raw, pack, run_rows, step_rows, overlap):
    empty = jnp.zeros((CHUNK - HEADS, CHUNK), F32)
    for c in range(CHUNKS):
        rows = slice(c * CHUNK, (c + 1) * CHUNK)
        wide = jnp.concatenate([raw_t_ref[:, rows].astype(F32), empty], axis=0)
        raw[rows, :] = wide.T
        turned[:, rows] = bc_ref[rows, source : source + STATE].astype(F32).T.astype(BF16)
    step, decay = steps_of(raw, bias_ref, rate_ref)
    step_pack = packed(step)
    lower = jnp.where(triangle(True), 1.0, 0.0).astype(BF16)
    upper = jnp.where(triangle(False), 1.0, 0.0).astype(BF16)
    decay_pack = packed(decay).astype(BF16)
    keep = lax.broadcasted_iota(jnp.int32, (CHUNK, LANES), 1) < HEADS
    for c in range(CHUNKS):
        rows = slice(c * CHUNK, (c + 1) * CHUNK)
        total = dot(lower, decay_pack[rows])
        total = total + pltpu.roll(total, LANES - HEADS, 1) + pltpu.roll(total, LANES - 2 * HEADS, 1)
        run_pack = pltpu.roll(packed(jnp.where(keep, total, 0.0)), 3 * HEADS, 1)
        pack[rows, :] = (step_pack[rows] + run_pack).astype(BF16)
        step_t = step[rows].T
        decay_t = three_parts(decay[rows].T[:HEADS])
        across = sum(dot(part.astype(BF16), upper) for part in decay_t)
        for pair in range(PAIRS):
            heads = slice(2 * pair, 2 * pair + 2)
            run_rows[pair, :, rows] = across[heads, :]
            step_rows[pair, :, rows] = step_t[heads, :]
        b, c_low = bc_ref[rows, :STATE], bc_ref[rows, STATE:]
        overlap[c] = jnp.where(triangle(True), dot(c_low, b, (1, 1)), 0.0)


def first_half():
    return lax.broadcasted_iota(jnp.int32, (CHUNK, LANES), 1) < WIDTH


def apart(v):
    first = first_half()
    return jnp.concatenate([jnp.where(first, v, 0.0), jnp.where(first, 0.0, v)], axis=0).astype(BF16)


def decays(columns, run_rows, pair, rows):
    out = []
    for h in range(2):
        across = run_rows[pair, h : h + 1, rows]
        out.append(jnp.exp(jnp.minimum(columns[:, h * CHUNK : (h + 1) * CHUNK] - across, 0.0)))
    return out


def forward_kernel(x_ref, g_ref, bc_ref, raw_t_ref, bias_ref, rate_ref, skip_ref, gain_ref,
                   low_ref, scan_ref, gated_ref, state_ref, scale_ref,
                   raw, pack, run_rows, step_rows, overlap, spread, turned, squares):
    pair = pl.program_id(0)

    @pl.when(pair == 0)
    def _():
        prepare(raw_t_ref, bias_ref, rate_ref, bc_ref, turned, 0,
                raw, pack, run_rows, step_rows, overlap)
        squares[...] = jnp.zeros_like(squares)

    spread[...] = dot(pack[...], picker(pair))
    skip = skip_ref[:, pl.ds(pl.multiple_of(pair * LANES, LANES), LANES)]
    state = None
    for c in range(CHUNKS):
        rows = slice(c * CHUNK, (c + 1) * CHUNK)
        x = x_ref[rows, :].astype(F32)
        step, run = spread[rows, :LANES], spread[rows, LANES : 2 * LANES]
        columns = spread[rows, 2 * LANES :]
        weights = []
        for h, one in enumerate(decays(columns, run_rows, pair, rows)):
            weights.append(halves(one * overlap[c] * step_rows[pair, h : h + 1, rows]))
        y = dot(
            jnp.concatenate(
                [
                    jnp.concatenate([weights[h][part] for h in range(2)], axis=1)
                    for part in range(2)
                ],
                axis=0,
            ),
            apart(x),
        )
        y = y[:CHUNK] + y[CHUNK:]
        if c > 0:
            state_ref[0, c - 1] = state
            held = jnp.concatenate(halves(state), axis=1)
            y = y + jnp.exp(run) * folded(dot(bc_ref[rows, STATE:], held))
        if c < CHUNKS - 1:
            end = run[CHUNK - 1 :, :]
            fresh = jnp.concatenate(halves(x * step * jnp.exp(end - run)), axis=1)
            local = folded(dot(turned[:, rows], fresh))
            state = local if c == 0 else jnp.exp(end) * state + local
        scan_ref[rows, :] = y
        g = g_ref[rows, :].astype(F32)
        gated = (y + skip * x) * (g / (1.0 + jnp.exp(-g)))
        gated_ref[rows, pl.ds(pl.multiple_of(pair * LANES, LANES), LANES)] = gated
        squares[rows, :] += gated * gated

    @pl.when(pair == PAIRS - 1)
    def _():
        for c in range(CHUNKS):
            rows = slice(c * CHUNK, (c + 1) * CHUNK)
            mean = jnp.sum(squares[rows, :], axis=1, keepdims=True) * (1.0 / CHANNELS)
            scale = lax.rsqrt(mean + EPS)
            scale_ref[rows, :] = jnp.broadcast_to(scale, (CHUNK, LANES))
            low_ref[:, rows] = (gated_ref[rows, :] * scale * gain_ref[...]).T.astype(BF16)


def backward_kernel(x_ref, g_ref, cot_ref, scan_ref, state_ref, scale_ref, pull_ref,
                    bc_ref, raw_t_ref, bias_ref, rate_ref, skip_ref, gain_ref,
                    dx_ref, dg_ref, db_ref, dc_ref, step_ref, small_ref,
                    raw, pack, run_rows, step_rows, overlap, spread, turned, d_overlap, d_b, d_c, flow, direct, lanes):
    pair = pl.program_id(0)

    @pl.when(pair == 0)
    def _():
        prepare(raw_t_ref, bias_ref, rate_ref, bc_ref, turned, STATE,
                raw, pack, run_rows, step_rows, overlap)
        for held in (d_overlap, d_b, d_c, flow, direct, lanes):
            held[...] = jnp.zeros_like(held)

    spread[...] = dot(pack[...], picker(pair))
    here = pl.ds(pl.multiple_of(pair * LANES, LANES), LANES)
    skip, gain = skip_ref[:, here], gain_ref[:, here]
    first = first_half()
    lane = lax.broadcasted_iota(jnp.int32, (CHUNK, LANES), 1)

    def by_head(v):
        one = jnp.sum(jnp.where(first, v, 0.0), axis=1, keepdims=True)
        two = jnp.sum(jnp.where(first, 0.0, v), axis=1, keepdims=True)
        return jnp.where(lane == 2 * pair, one, jnp.where(lane == 2 * pair + 1, two, 0.0))

    d_state = None
    skip_sum = jnp.zeros((1, LANES), F32)
    for c in reversed(range(CHUNKS)):
        rows = slice(c * CHUNK, (c + 1) * CHUNK)
        x = x_ref[rows, :].astype(F32)
        g = g_ref[rows, :].astype(F32)
        scan = scan_ref[rows, :]
        out = scan + skip * x
        sig = 1.0 / (1.0 + jnp.exp(-g))
        silu = g * sig
        d_gated = scale_ref[rows, :] * gain * cot_ref[rows, :] - out * silu * pull_ref[rows, :]
        dy = d_gated * silu
        dg_ref[rows, :] = (d_gated * out * (sig + silu * (1.0 - sig))).astype(BF16)
        skip_sum = skip_sum + jnp.sum(dy * x, axis=0, keepdims=True)

        step, run = spread[rows, :LANES], spread[rows, LANES : 2 * LANES]
        columns = spread[rows, 2 * LANES :]
        driven = x * step
        dy_hi, dy_low = (apart(part.astype(F32)) for part in halves(dy))
        factor = decays(columns, run_rows, pair, rows)
        products = dot(
            jnp.concatenate([dy_hi, dy_low], axis=1),
            jnp.concatenate([x_ref[rows, :], x_ref[rows, :]], axis=1),
            (1, 1),
        )
        step_row = step_rows[pair, :, rows]
        d_overlap[c] += (
            factor[0] * products[:CHUNK] * step_row[:1] + factor[1] * products[CHUNK:] * step_row[1:]
        )
        weights = [halves(one * overlap[c]) for one in factor]
        weights = jnp.concatenate([jnp.concatenate(one, axis=1) for one in weights], axis=0)
        both = dot(weights, jnp.concatenate([dy_hi, dy_low], axis=1), (0, 0))
        d_driven = folded(both[:CHUNK]) + both[CHUNK:, :LANES]
        entering_hi, entering_low = halves(dy * jnp.exp(run))
        entering = jnp.concatenate([entering_hi, entering_low], axis=1)
        end = run[CHUNK - 1 :, :]
        if c > 0:
            held = state_ref[0, c - 1]
            held_hi, held_low = halves(held)
            d_c[rows, :] += dot(
                entering, jnp.concatenate([held_hi, held_hi], axis=1), (1, 1)
            ) + dot(entering_hi, held_low, (1, 1))
        if c < CHUNKS - 1:
            to_end = jnp.exp(end - run)
            d_hi, d_low = halves(d_state)
            from_state = to_end * folded(
                dot(bc_ref[rows, :STATE], jnp.concatenate([d_hi, d_low], axis=1))
            )
            fresh_hi, fresh_low = halves(driven * to_end)
            d_b[rows, :] += dot(
                jnp.concatenate([fresh_hi, fresh_low], axis=1),
                jnp.concatenate([d_hi, d_hi], axis=1),
                (1, 1),
            ) + dot(fresh_hi, d_low, (1, 1))
            crossing = jnp.sum(driven * from_state, axis=0, keepdims=True)
            if c > 0:
                carried = jnp.sum(held * d_state, axis=0, keepdims=True)
                crossing = crossing + jnp.exp(end) * carried
            lanes[c : c + 1, here] = crossing
            d_driven = d_driven + from_state
        if c > 0:
            back = folded(dot(turned[:, rows], entering))
            d_state = back if d_state is None else jnp.exp(end) * d_state + back
        flow[rows, :] += by_head(dy * scan - driven * d_driven)
        direct[rows, :] += by_head(x * d_driven)
        dx_ref[rows, :] = (step * d_driven + skip * dy).astype(BF16)
    lanes[CHUNKS : CHUNKS + 1, here] = skip_sum

    @pl.when(pair == PAIRS - 1)
    def _():
        channel = lax.broadcasted_iota(jnp.int32, (CHANNELS, LANES), 0) // WIDTH
        head = lax.broadcasted_iota(jnp.int32, (CHANNELS, LANES), 1)
        gather = jnp.where(channel == head, 1.0, 0.0).astype(BF16)
        heads = sum(dot(part.astype(BF16), gather) for part in three_parts(lanes[...]))
        step_all, decay_all = steps_of(raw, bias_ref, rate_ref)
        rate = jnp.exp(rate_ref[...])
        upper = jnp.where(triangle(False), 1.0, 0.0).astype(BF16)
        keep = lane < HEADS
        rate_sum = jnp.zeros((1, LANES), F32)
        bias_sum = jnp.zeros((1, LANES), F32)
        for c in range(CHUNKS):
            rows = slice(c * CHUNK, (c + 1) * CHUNK)
            d_decay = sum(dot(upper, part.astype(BF16)) for part in three_parts(flow[rows, :]))
            d_decay = d_decay + heads[c : c + 1, :]
            d_step = direct[rows, :] - d_decay * rate
            before = raw[rows, :] + bias_ref[...]
            d_raw = jnp.where(keep, d_step / (1.0 + jnp.exp(-before)), 0.0)
            step_ref[:, rows] = d_raw.T[:HEADS, :]
            bias_sum = bias_sum + jnp.sum(d_raw, axis=0, keepdims=True)
            rate_sum = rate_sum + jnp.sum(
                jnp.where(keep, d_decay * decay_all[rows], 0.0), axis=0, keepdims=True
            )
            d_hi, d_low = halves(jnp.where(triangle(True), d_overlap[c], 0.0))
            dc_ref[rows, :] = (
                d_c[rows, :] + dot(d_hi, bc_ref[rows, :STATE]) + dot(d_low, bc_ref[rows, :STATE])
            ).astype(BF16)
            db_ref[rows, :] = (
                d_b[rows, :]
                + dot(d_hi, bc_ref[rows, STATE:], (0, 0))
                + dot(d_low, bc_ref[rows, STATE:], (0, 0))
            ).astype(BF16)
        small_ref[...] = jnp.concatenate(
            [rate_sum, bias_sum, heads[CHUNKS : CHUNKS + 1, :], jnp.zeros((5, LANES), F32)], axis=0
        )


def whole(shape):
    return pl.BlockSpec(shape, lambda *_: (0,) * len(shape))


def by_pair(rows):
    return pl.BlockSpec((rows, LANES), lambda p, *_: (0, p))


VMEM_LIMIT = 56 * 1024 * 1024

TABLES = [
    pltpu.VMEM((TOKENS, LANES), F32),
    pltpu.VMEM((TOKENS, LANES), BF16),
    pltpu.VMEM((PAIRS, 2, TOKENS), F32),
    pltpu.VMEM((PAIRS, 2, TOKENS), F32),
    pltpu.VMEM((CHUNKS, CHUNK, CHUNK), F32),
    pltpu.VMEM((TOKENS, 4 * LANES), F32),
    pltpu.VMEM((STATE, TOKENS), BF16),
]

PARAMETERS = [
    whole((TOKENS, 2 * STATE)),
    whole((HEADS, TOKENS)),
    whole((1, LANES)),
    whole((1, LANES)),
    whole((1, CHANNELS)),
    whole((1, CHANNELS)),
]


def scan_forward(x, g, parameters):
    return pl.pallas_call(
        forward_kernel,
        grid=(PAIRS,),
        in_specs=[
            by_pair(TOKENS),
            by_pair(TOKENS),
        ]
        + PARAMETERS,
        out_specs=[
            whole((CHANNELS, TOKENS)),
            by_pair(TOKENS),
            whole((TOKENS, CHANNELS)),
            pl.BlockSpec((1, CHUNKS - 1, STATE, LANES), lambda p: (p, 0, 0, 0)),
            whole((TOKENS, LANES)),
        ],
        out_shape=[
            jax.ShapeDtypeStruct((CHANNELS, TOKENS), BF16),
            jax.ShapeDtypeStruct((TOKENS, CHANNELS), F32),
            jax.ShapeDtypeStruct((TOKENS, CHANNELS), F32),
            jax.ShapeDtypeStruct((PAIRS, CHUNKS - 1, STATE, LANES), F32),
            jax.ShapeDtypeStruct((TOKENS, LANES), F32),
        ],
        scratch_shapes=TABLES + [pltpu.VMEM((TOKENS, LANES), F32)],
        compiler_params=pltpu.CompilerParams(vmem_limit_bytes=VMEM_LIMIT),
        cost_estimate=pl.CostEstimate(flops=16 * 10**9, bytes_accessed=10**7, transcendentals=0),
        name="scan_forward",
    )(x, g, *parameters)


def scan_backward(x, g, cot, scan, states, scale, pull, parameters):
    return pl.pallas_call(
        backward_kernel,
        grid=(PAIRS,),
        in_specs=[
            by_pair(TOKENS),
            by_pair(TOKENS),
            by_pair(TOKENS),
            by_pair(TOKENS),
            pl.BlockSpec((1, CHUNKS - 1, STATE, LANES), lambda p: (p, 0, 0, 0)),
            whole((TOKENS, LANES)),
            whole((TOKENS, LANES)),
        ]
        + PARAMETERS,
        out_specs=[
            by_pair(TOKENS),
            by_pair(TOKENS),
            whole((TOKENS, STATE)),
            whole((TOKENS, STATE)),
            whole((HEADS, TOKENS)),
            whole((8, LANES)),
        ],
        out_shape=[
            jax.ShapeDtypeStruct((TOKENS, CHANNELS), BF16),
            jax.ShapeDtypeStruct((TOKENS, CHANNELS), BF16),
            jax.ShapeDtypeStruct((TOKENS, STATE), BF16),
            jax.ShapeDtypeStruct((TOKENS, STATE), BF16),
            jax.ShapeDtypeStruct((HEADS, TOKENS), F32),
            jax.ShapeDtypeStruct((8, LANES), F32),
        ],
        scratch_shapes=TABLES
        + [
            pltpu.VMEM((CHUNKS, CHUNK, CHUNK), F32),
            pltpu.VMEM((TOKENS, STATE), F32),
            pltpu.VMEM((TOKENS, STATE), F32),
            pltpu.VMEM((TOKENS, LANES), F32),
            pltpu.VMEM((TOKENS, LANES), F32),
            pltpu.VMEM((8, CHANNELS), F32),
        ],
        compiler_params=pltpu.CompilerParams(vmem_limit_bytes=VMEM_LIMIT),
        cost_estimate=pl.CostEstimate(flops=20 * 10**9, bytes_accessed=10**7, transcendentals=0),
        name="scan_backward",
    )(x, g, cot, scan, states, scale, pull, *parameters)


FEATURES = 512
BLOCK = 128
SHARDS = 8


def term_kernel(count, added, placed, places, *refs):
    pieces, low_ref = refs[: 2 * count], refs[2 * count]
    per = 2 * CHANNELS
    copies, arrivals = [], []
    if added:
        out_ref, held, done, sent, come = refs[-5:]
        parts = [
            ref.at[start : start + per]
            for ref in refs[2 * count + 1 : -5]
            for start in range(0, ref.shape[0], per)
        ]
        for k, part in enumerate(parts):
            arrivals.append(pltpu.make_async_copy(part, sent.at[k], come.at[k]))
            arrivals[-1].start()
    else:
        out_ref, held, done = refs[-3:]
    for k in range(count):
        blocks = [piece[...] for piece in pieces[2 * k : 2 * k + 2]]
        term = dot(low_ref[...], jnp.concatenate(blocks, axis=1))
        if added:
            arrivals[k].wait()
        for slot in range(2):
            n = 2 * k + slot
            here = slice(n * CHANNELS, (n + 1) * CHANNELS)
            part = term[:, slot * BLOCK : (slot + 1) * BLOCK]
            if added:
                part = part + sent[k, slot * CHANNELS : (slot + 1) * CHANNELS, :].astype(F32)
            held[here, :] = part.astype(BF16)
            start = n * CHANNELS
            if placed:
                start = pl.multiple_of((places[k] * 2 + slot) * CHANNELS, CHANNELS)
            copies.append(
                pltpu.make_async_copy(
                    held.at[here], out_ref.at[pl.ds(start, CHANNELS)], done.at[n]
                )
            )
            copies[-1].start()
    for copy in copies:
        copy.wait()


def terms(places, blocks, pieces, low, sent=()):
    count = len(pieces)
    added = len(sent) > 0
    rows = 2 * CHANNELS * count
    specs = [pl.BlockSpec(memory_space=pl.ANY) for _ in sent]
    scratch = [
        pltpu.VMEM((2 * count * CHANNELS, BLOCK), BF16),
        pltpu.SemaphoreType.DMA((2 * count,)),
    ]
    if added:
        scratch += [
            pltpu.VMEM((count, 2 * CHANNELS, BLOCK), BF16),
            pltpu.SemaphoreType.DMA((count,)),
        ]

    def kernel(*refs):
        term_kernel(count, added, added, *refs)

    def lanes(slot):
        return pl.BlockSpec((TOKENS, BLOCK), lambda _, at: (0, at[count + slot]))

    return pl.pallas_call(
        kernel,
        grid_spec=pltpu.PrefetchScalarGridSpec(
            num_scalar_prefetch=1,
            grid=(1,),
            in_specs=[lanes(0), lanes(1)] * count + [whole((CHANNELS, TOKENS))] + specs,
            out_specs=pl.BlockSpec(memory_space=pl.ANY),
            scratch_shapes=scratch,
        ),
        out_shape=jax.ShapeDtypeStruct((rows, BLOCK), BF16),
        compiler_params=pltpu.CompilerParams(vmem_limit_bytes=VMEM_LIMIT),
        cost_estimate=pl.CostEstimate(
            flops=(count + 1) * 7 * 10**8, bytes_accessed=2 * 10**6, transcendentals=0
        ),
        name="terms_added" if added else "terms",
    )(
        jnp.stack(list(places) + list(blocks)).astype(jnp.int32),
        *[piece for piece in pieces for _ in range(2)],
        low,
        *sent,
    )


def finish_kernel(scale, kept_ref, given_ref, out_ref):
    total = kept_ref[...].astype(F32) + given_ref[...].astype(F32)
    out_ref[...] = (total * scale).T


def finish(plane, given, scale):
    return pl.pallas_call(
        lambda *refs: finish_kernel(scale, *refs),
        grid=(1,),
        in_specs=[pl.BlockSpec((CHANNELS, BLOCK), lambda _: (1, 0)), whole((CHANNELS, BLOCK))],
        out_specs=whole((BLOCK, CHANNELS)),
        out_shape=jax.ShapeDtypeStruct((BLOCK, CHANNELS), F32),
        cost_estimate=pl.CostEstimate(flops=4 * 10**9, bytes_accessed=10**6, transcendentals=0),
        name="finish",
    )(plane, given)


COLUMNS = 256


def product_kernel(places, *refs):
    pieces = refs[:SHARDS]
    rows_ref, gated_ref, scale_ref, gain_ref = refs[SHARDS : SHARDS + 4]
    cot_ref, gain_grad_ref, pull_ref, sums = refs[SHARDS + 4 :]
    step = pl.program_id(0)
    starts = [pl.multiple_of(places[k] * FEATURES, FEATURES) for k in range(SHARDS)]
    cot_ref[...] = dot(
        jnp.concatenate([piece[...] for piece in pieces], axis=1),
        jnp.concatenate([rows_ref[pl.ds(start, FEATURES), :] for start in starts], axis=0),
    )

    @pl.when(step == 0)
    def _():
        sums[...] = jnp.zeros_like(sums)

    scale = scale_ref[...]
    for half in range(COLUMNS // LANES):
        cols = slice(half * LANES, (half + 1) * LANES)
        with_gated = cot_ref[:, cols] * gated_ref[:, cols]
        gain_grad_ref[:, cols] = jnp.sum(with_gated * scale, axis=0, keepdims=True)
        sums[...] += with_gated * gain_ref[:, cols]

    @pl.when(step == pl.num_programs(0) - 1)
    def _():
        pulled = jnp.sum(sums[...], axis=1, keepdims=True) * (1.0 / CHANNELS)
        pull_ref[...] = scale * scale * scale * pulled


def products(places, pieces, rows, gated, scale, gain):
    depth = SHARDS * FEATURES
    return pl.pallas_call(
        product_kernel,
        grid_spec=pltpu.PrefetchScalarGridSpec(
            num_scalar_prefetch=1,
            grid=(CHANNELS // COLUMNS,),
            in_specs=[whole((TOKENS, FEATURES))] * SHARDS
            + [
                pl.BlockSpec((depth, COLUMNS), lambda n, *_: (0, n)),
                pl.BlockSpec((TOKENS, COLUMNS), lambda n, *_: (0, n)),
                whole((TOKENS, LANES)),
                pl.BlockSpec((1, COLUMNS), lambda n, *_: (0, n)),
            ],
            out_specs=[
                pl.BlockSpec((TOKENS, COLUMNS), lambda n, *_: (0, n)),
                pl.BlockSpec((1, COLUMNS), lambda n, *_: (0, n)),
                whole((TOKENS, LANES)),
            ],
            scratch_shapes=[pltpu.VMEM((TOKENS, LANES), F32)],
        ),
        out_shape=[
            jax.ShapeDtypeStruct((TOKENS, CHANNELS), F32),
            jax.ShapeDtypeStruct((1, CHANNELS), F32),
            jax.ShapeDtypeStruct((TOKENS, LANES), F32),
        ],
        compiler_params=pltpu.CompilerParams(vmem_limit_bytes=VMEM_LIMIT),
        cost_estimate=pl.CostEstimate(
            flops=12 * 10**9, bytes_accessed=16 * 10**6, transcendentals=0
        ),
        name="products",
    )(places, *pieces, rows, gated, scale, gain)


def along_x(step):
    return [(x * 2 + h, (x + step) % 4 * 2 + h) for x in range(4) for h in range(2)]


def beside(shard):
    return lax.ppermute(shard, "tp", along_x(1)), lax.ppermute(shard, "tp", along_x(-1))


def beyond(before, after):
    half = before.shape[0] // 2
    top = lax.ppermute(before[:half], "tp", along_x(1))
    low = lax.ppermute(after[half:], "tp", along_x(-1))
    return top, low


def swap(bit):
    return [(b, b ^ bit) for b in range(32)]


def local_parameters(state_proj, step_raw, log_rate, step_bias, skip_gain, norm_gain):
    def padded(v):
        return jnp.pad(v, (0, LANES - HEADS)).reshape(1, LANES)

    return (
        state_proj.reshape(TOKENS, 2 * STATE),
        step_raw.T,
        padded(step_bias),
        padded(log_rate),
        jnp.repeat(skip_gain, WIDTH).reshape(1, CHANNELS),
        norm_gain.reshape(1, CHANNELS),
    )


def shards(
    scan_input,
    gate_input,
    state_proj,
    step_raw,
    log_rate,
    step_bias,
    skip_gain,
    norm_gain,
    out_proj,
    out_cotangent,
):
    norm_scale = 1.0 / math.sqrt(TOKENS * 32)
    block = lax.axis_index("blk")
    core, y_lo = block % 2, block // 2 % 2
    by_z = [[z * 4 + rest for z in range(8)] for rest in range(4)]
    rows = lax.all_gather(out_proj, "blk", axis=0, tiled=True)
    own = out_cotangent
    partner = lax.ppermute(own, "tp", [(t, t ^ 1) for t in range(8)])
    before, after = beside(own)
    partner, before, after, scan_input = lax.optimization_barrier(
        (partner, before, after, scan_input)
    )
    partner_before, partner_after = beside(partner)
    far_parts = beyond(before, after)

    parameters = local_parameters(
        state_proj, step_raw, log_rate, step_bias, skip_gain, norm_gain
    )
    low, scan, gated, states, scale = scan_forward(scan_input, gate_input, parameters)
    partner_before, partner_after, far_parts, low = lax.optimization_barrier(
        (partner_before, partner_after, far_parts, low)
    )
    far = jnp.concatenate(far_parts, axis=0)
    partner_far = beyond(partner_before, partner_after)
    early = [own, before, after, far, partner, partner_before, partner_after]
    me = lax.axis_index("tp")
    x, h = me // 2, me % 2
    places = [(x + shift) % 4 * 2 + row for row in (h, 1 - h) for shift in (0, 3, 1, 2)]

    mine, mine_y = 2 * y_lo + core, 2 * (1 - y_lo) + core
    theirs, theirs_y = 2 * y_lo + 1 - core, 2 * (1 - y_lo) + 1 - core

    theirs_early = terms(places[:-1], (theirs_y, theirs), early, low)
    theirs_early, partner_far = lax.optimization_barrier((theirs_early, partner_far))
    sent_early = lax.ppermute(theirs_early, "blk", swap(1))
    last = [jnp.concatenate(partner_far, axis=0)]
    sent_last = lax.ppermute(terms(places[-1:], (theirs_y, theirs), last, low), "blk", swap(1))
    both = terms(places, (mine_y, mine), early + last, low, (sent_early, sent_last))
    plane = lax.psum_scatter(
        both, "blk", scatter_dimension=0, tiled=True, axis_index_groups=by_z
    )
    rows, _ = lax.optimization_barrier((rows, both))
    cot, gain_grad, pull = products(
        jnp.stack(places).astype(jnp.int32),
        early + last,
        rows,
        gated,
        scale,
        parameters[-1],
    )
    dx, dg, db, dc, step_grad, small = scan_backward(
        scan_input, gate_input, cot, scan, states, scale, pull, parameters
    )
    summed = jnp.concatenate([small, gain_grad.reshape(8, LANES)], axis=0)
    for bit in (1, 4, 8):
        summed = summed + lax.ppermute(summed, "blk", swap(bit))
    state_grad = jnp.stack([db, dc], axis=1)
    plane, summed, state_grad = lax.optimization_barrier((plane, summed, state_grad))
    given = lax.ppermute(plane[:CHANNELS], "blk", swap(2))
    summed = summed + lax.ppermute(summed, "blk", swap(16))
    given, summed = lax.optimization_barrier((given, summed))
    weight_grad = finish(plane, given, norm_scale)
    summed = (summed + lax.ppermute(summed, "blk", swap(2))) * norm_scale
    return (
        dx,
        dg,
        state_grad,
        step_grad.T,
        weight_grad,
        summed[0, :HEADS],
        summed[1, :HEADS],
        summed[2, :HEADS],
        summed[8:].reshape(CHANNELS),
    )


def solution(mesh):
    placed = (
        P("blk", "tp"),
        P("blk", "tp"),
        P("blk", None, "tp"),
        P("blk", "tp"),
        P("tp"),
        P("tp"),
        P("tp"),
        P("tp"),
        P("blk", "tp"),
        P("blk", "tp"),
    )
    return jax.shard_map(
        shards,
        mesh=mesh,
        in_specs=placed,
        out_specs=(
            P("blk", "tp"),
            P("blk", "tp"),
            P("blk", None, "tp"),
            P("blk", "tp"),
            P("blk", "tp"),
            P("tp"),
            P("tp"),
            P("tp"),
            P("tp"),
        ),
        check_vma=False,
    )
```

```python
import math

import jax
import jax.numpy as jnp
from jax import lax
from jax.experimental import pallas as pl
from jax.experimental.pallas import tpu as pltpu
from jax.sharding import PartitionSpec as P

TOKENS = 512
CHANNELS = 1024
HEADS = 16
WIDTH = 64
STATE = 256
CHUNK = 128
CHUNKS = TOKENS // CHUNK
LANES = 128
PAIRS = HEADS // 2
EPS = 1e-05

F32 = jnp.float32
BF16 = jnp.bfloat16


def dot(a, b, over=(1, 0)):
    return lax.dot_general(
        a, b, (((over[0],), (over[1],)), ((), ())), preferred_element_type=F32
    )


def three_parts(v):
    hi = v.astype(BF16).astype(F32)
    rest = v - hi
    mid = rest.astype(BF16).astype(F32)
    return hi, mid, rest - mid


def packed(v):
    hi, mid, low = three_parts(v)
    return hi + pltpu.roll(mid, HEADS, 1) + pltpu.roll(low, 2 * HEADS, 1)


def halves(v):
    hi = v.astype(BF16)
    return hi, (v - hi.astype(F32)).astype(BF16)


def folded(v):
    middle = v.shape[1] // 2
    return v[:, :middle] + v[:, middle:]


def triangle(lower):
    i = lax.broadcasted_iota(jnp.int32, (CHUNK, CHUNK), 0)
    j = lax.broadcasted_iota(jnp.int32, (CHUNK, CHUNK), 1)
    return i >= j if lower else i <= j


def picker(pair):
    row = lax.broadcasted_iota(jnp.int32, (LANES, 4 * LANES), 0)
    col = lax.broadcasted_iota(jnp.int32, (LANES, 4 * LANES), 1)
    narrow = col < 2 * LANES
    head = 2 * pair + jnp.where(narrow, (col % LANES) // WIDTH, col // CHUNK - 2)
    first = jnp.where(col < LANES, 0, 3 * HEADS)
    hit = (row % HEADS == head) & (row >= first) & (row < first + 3 * HEADS)
    return jnp.where(hit, 1.0, 0.0).astype(BF16)


def softplus(v):
    return jnp.maximum(v, 0.0) + jnp.log1p(jnp.exp(-jnp.abs(v)))


def head_lanes():
    return lax.broadcasted_iota(jnp.int32, (TOKENS, LANES), 1) < HEADS


def steps_of(raw, bias_ref, rate_ref):
    step = jnp.where(head_lanes(), softplus(raw[...] + bias_ref[...]), 0.0)
    return step, -step * jnp.exp(rate_ref[...])


def prepare(raw_t_ref, bias_ref, rate_ref, bc_ref, turned, source,
            raw, pack, run_rows, step_rows, overlap):
    empty = jnp.zeros((CHUNK - HEADS, CHUNK), F32)
    for c in range(CHUNKS):
        rows = slice(c * CHUNK, (c + 1) * CHUNK)
        wide = jnp.concatenate([raw_t_ref[:, rows].astype(F32), empty], axis=0)
        raw[rows, :] = wide.T
        turned[:, rows] = bc_ref[rows, source : source + STATE].astype(F32).T.astype(BF16)
    step, decay = steps_of(raw, bias_ref, rate_ref)
    step_pack = packed(step)
    lower = jnp.where(triangle(True), 1.0, 0.0).astype(BF16)
    upper = jnp.where(triangle(False), 1.0, 0.0).astype(BF16)
    decay_pack = packed(decay).astype(BF16)
    keep = lax.broadcasted_iota(jnp.int32, (CHUNK, LANES), 1) < HEADS
    for c in range(CHUNKS):
        rows = slice(c * CHUNK, (c + 1) * CHUNK)
        total = dot(lower, decay_pack[rows])
        total = total + pltpu.roll(total, LANES - HEADS, 1) + pltpu.roll(total, LANES - 2 * HEADS, 1)
        run_pack = pltpu.roll(packed(jnp.where(keep, total, 0.0)), 3 * HEADS, 1)
        pack[rows, :] = (step_pack[rows] + run_pack).astype(BF16)
        step_t = step[rows].T
        decay_t = three_parts(decay[rows].T[:HEADS])
        across = sum(dot(part.astype(BF16), upper) for part in decay_t)
        for pair in range(PAIRS):
            heads = slice(2 * pair, 2 * pair + 2)
            run_rows[pair, :, rows] = across[heads, :]
            step_rows[pair, :, rows] = step_t[heads, :]
        b, c_low = bc_ref[rows, :STATE], bc_ref[rows, STATE:]
        overlap[c] = jnp.where(triangle(True), dot(c_low, b, (1, 1)), 0.0)


def first_half():
    return lax.broadcasted_iota(jnp.int32, (CHUNK, LANES), 1) < WIDTH


def apart(v):
    first = first_half()
    return jnp.concatenate([jnp.where(first, v, 0.0), jnp.where(first, 0.0, v)], axis=0).astype(BF16)


def decays(columns, run_rows, pair, rows):
    out = []
    for h in range(2):
        across = run_rows[pair, h : h + 1, rows]
        out.append(jnp.exp(jnp.minimum(columns[:, h * CHUNK : (h + 1) * CHUNK] - across, 0.0)))
    return out


def forward_kernel(x_ref, g_ref, bc_ref, raw_t_ref, bias_ref, rate_ref, skip_ref, gain_ref,
                   low_ref, scan_ref, gated_ref, state_ref, scale_ref,
                   raw, pack, run_rows, step_rows, overlap, spread, turned, squares):
    pair = pl.program_id(0)

    @pl.when(pair == 0)
    def _():
        prepare(raw_t_ref, bias_ref, rate_ref, bc_ref, turned, 0,
                raw, pack, run_rows, step_rows, overlap)
        squares[...] = jnp.zeros_like(squares)

    spread[...] = dot(pack[...], picker(pair))
    skip = skip_ref[:, pl.ds(pl.multiple_of(pair * LANES, LANES), LANES)]
    state = None
    for c in range(CHUNKS):
        rows = slice(c * CHUNK, (c + 1) * CHUNK)
        x = x_ref[rows, :].astype(F32)
        step, run = spread[rows, :LANES], spread[rows, LANES : 2 * LANES]
        columns = spread[rows, 2 * LANES :]
        weights = []
        for h, one in enumerate(decays(columns, run_rows, pair, rows)):
            weights.append(halves(one * overlap[c] * step_rows[pair, h : h + 1, rows]))
        y = dot(
            jnp.concatenate(
                [
                    jnp.concatenate([weights[h][part] for h in range(2)], axis=1)
                    for part in range(2)
                ],
                axis=0,
            ),
            apart(x),
        )
        y = y[:CHUNK] + y[CHUNK:]
        if c > 0:
            state_ref[0, c - 1] = state
            held = jnp.concatenate(halves(state), axis=1)
            y = y + jnp.exp(run) * folded(dot(bc_ref[rows, STATE:], held))
        if c < CHUNKS - 1:
            end = run[CHUNK - 1 :, :]
            fresh = jnp.concatenate(halves(x * step * jnp.exp(end - run)), axis=1)
            local = folded(dot(turned[:, rows], fresh))
            state = local if c == 0 else jnp.exp(end) * state + local
        scan_ref[rows, :] = y
        g = g_ref[rows, :].astype(F32)
        gated = (y + skip * x) * (g / (1.0 + jnp.exp(-g)))
        gated_ref[rows, pl.ds(pl.multiple_of(pair * LANES, LANES), LANES)] = gated
        squares[rows, :] += gated * gated

    @pl.when(pair == PAIRS - 1)
    def _():
        for c in range(CHUNKS):
            rows = slice(c * CHUNK, (c + 1) * CHUNK)
            mean = jnp.sum(squares[rows, :], axis=1, keepdims=True) * (1.0 / CHANNELS)
            scale = lax.rsqrt(mean + EPS)
            scale_ref[rows, :] = jnp.broadcast_to(scale, (CHUNK, LANES))
            low_ref[:, rows] = (gated_ref[rows, :] * scale * gain_ref[...]).T.astype(BF16)


def backward_kernel(x_ref, g_ref, cot_ref, scan_ref, state_ref, scale_ref, pull_ref,
                    bc_ref, raw_t_ref, bias_ref, rate_ref, skip_ref, gain_ref,
                    raw, pack, run_rows, step_rows, overlap,
                    dx_ref, dg_ref, db_ref, dc_ref, step_ref, small_ref,
                    spread, turned, d_overlap, d_b, d_c, flow, direct, lanes):
    pair = pl.program_id(0)

    @pl.when(pair == 0)
    def _():
        for c in range(CHUNKS):
            rows = slice(c * CHUNK, (c + 1) * CHUNK)
            turned[:, rows] = bc_ref[rows, STATE:].astype(F32).T.astype(BF16)
        for held in (d_overlap, d_b, d_c, flow, direct, lanes):
            held[...] = jnp.zeros_like(held)

    spread[...] = dot(pack[...], picker(pair))
    here = pl.ds(pl.multiple_of(pair * LANES, LANES), LANES)
    skip, gain = skip_ref[:, here], gain_ref[:, here]
    first = first_half()
    lane = lax.broadcasted_iota(jnp.int32, (CHUNK, LANES), 1)

    def by_head(v):
        one = jnp.sum(jnp.where(first, v, 0.0), axis=1, keepdims=True)
        two = jnp.sum(jnp.where(first, 0.0, v), axis=1, keepdims=True)
        return jnp.where(lane == 2 * pair, one, jnp.where(lane == 2 * pair + 1, two, 0.0))

    d_state = None
    skip_sum = jnp.zeros((1, LANES), F32)
    for c in reversed(range(CHUNKS)):
        rows = slice(c * CHUNK, (c + 1) * CHUNK)
        x = x_ref[rows, :].astype(F32)
        g = g_ref[rows, :].astype(F32)
        scan = scan_ref[rows, :]
        out = scan + skip * x
        sig = 1.0 / (1.0 + jnp.exp(-g))
        silu = g * sig
        d_gated = scale_ref[rows, :] * gain * cot_ref[rows, :] - out * silu * pull_ref[rows, :]
        dy = d_gated * silu
        dg_ref[rows, :] = (d_gated * out * (sig + silu * (1.0 - sig))).astype(BF16)
        skip_sum = skip_sum + jnp.sum(dy * x, axis=0, keepdims=True)

        step, run = spread[rows, :LANES], spread[rows, LANES : 2 * LANES]
        columns = spread[rows, 2 * LANES :]
        driven = x * step
        dy_hi, dy_low = (apart(part.astype(F32)) for part in halves(dy))
        factor = decays(columns, run_rows, pair, rows)
        products = dot(
            jnp.concatenate([dy_hi, dy_low], axis=1),
            jnp.concatenate([x_ref[rows, :], x_ref[rows, :]], axis=1),
            (1, 1),
        )
        step_row = step_rows[pair, :, rows]
        d_overlap[c] += (
            factor[0] * products[:CHUNK] * step_row[:1] + factor[1] * products[CHUNK:] * step_row[1:]
        )
        weights = [halves(one * overlap[c]) for one in factor]
        weights = jnp.concatenate([jnp.concatenate(one, axis=1) for one in weights], axis=0)
        both = dot(weights, jnp.concatenate([dy_hi, dy_low], axis=1), (0, 0))
        d_driven = folded(both[:CHUNK]) + both[CHUNK:, :LANES]
        entering_hi, entering_low = halves(dy * jnp.exp(run))
        entering = jnp.concatenate([entering_hi, entering_low], axis=1)
        end = run[CHUNK - 1 :, :]
        if c > 0:
            held = state_ref[0, c - 1]
            held_hi, held_low = halves(held)
            d_c[rows, :] += dot(
                entering, jnp.concatenate([held_hi, held_hi], axis=1), (1, 1)
            ) + dot(entering_hi, held_low, (1, 1))
        if c < CHUNKS - 1:
            to_end = jnp.exp(end - run)
            d_hi, d_low = halves(d_state)
            from_state = to_end * folded(
                dot(bc_ref[rows, :STATE], jnp.concatenate([d_hi, d_low], axis=1))
            )
            fresh_hi, fresh_low = halves(driven * to_end)
            d_b[rows, :] += dot(
                jnp.concatenate([fresh_hi, fresh_low], axis=1),
                jnp.concatenate([d_hi, d_hi], axis=1),
                (1, 1),
            ) + dot(fresh_hi, d_low, (1, 1))
            crossing = jnp.sum(driven * from_state, axis=0, keepdims=True)
            if c > 0:
                carried = jnp.sum(held * d_state, axis=0, keepdims=True)
                crossing = crossing + jnp.exp(end) * carried
            lanes[c : c + 1, here] = crossing
            d_driven = d_driven + from_state
        if c > 0:
            back = folded(dot(turned[:, rows], entering))
            d_state = back if d_state is None else jnp.exp(end) * d_state + back
        flow[rows, :] += by_head(dy * scan - driven * d_driven)
        direct[rows, :] += by_head(x * d_driven)
        dx_ref[rows, :] = (step * d_driven + skip * dy).astype(BF16)
    lanes[CHUNKS : CHUNKS + 1, here] = skip_sum

    @pl.when(pair == PAIRS - 1)
    def _():
        channel = lax.broadcasted_iota(jnp.int32, (CHANNELS, LANES), 0) // WIDTH
        head = lax.broadcasted_iota(jnp.int32, (CHANNELS, LANES), 1)
        gather = jnp.where(channel == head, 1.0, 0.0).astype(BF16)
        heads = sum(dot(part.astype(BF16), gather) for part in three_parts(lanes[...]))
        step_all, decay_all = steps_of(raw, bias_ref, rate_ref)
        rate = jnp.exp(rate_ref[...])
        upper = jnp.where(triangle(False), 1.0, 0.0).astype(BF16)
        keep = lane < HEADS
        rate_sum = jnp.zeros((1, LANES), F32)
        bias_sum = jnp.zeros((1, LANES), F32)
        for c in range(CHUNKS):
            rows = slice(c * CHUNK, (c + 1) * CHUNK)
            d_decay = sum(dot(upper, part.astype(BF16)) for part in three_parts(flow[rows, :]))
            d_decay = d_decay + heads[c : c + 1, :]
            d_step = direct[rows, :] - d_decay * rate
            before = raw[rows, :] + bias_ref[...]
            d_raw = jnp.where(keep, d_step / (1.0 + jnp.exp(-before)), 0.0)
            step_ref[:, rows] = d_raw.T[:HEADS, :]
            bias_sum = bias_sum + jnp.sum(d_raw, axis=0, keepdims=True)
            rate_sum = rate_sum + jnp.sum(
                jnp.where(keep, d_decay * decay_all[rows], 0.0), axis=0, keepdims=True
            )
            d_hi, d_low = halves(jnp.where(triangle(True), d_overlap[c], 0.0))
            dc_ref[rows, :] = (
                d_c[rows, :] + dot(d_hi, bc_ref[rows, :STATE]) + dot(d_low, bc_ref[rows, :STATE])
            ).astype(BF16)
            db_ref[rows, :] = (
                d_b[rows, :]
                + dot(d_hi, bc_ref[rows, STATE:], (0, 0))
                + dot(d_low, bc_ref[rows, STATE:], (0, 0))
            ).astype(BF16)
        small_ref[...] = jnp.concatenate(
            [rate_sum, bias_sum, heads[CHUNKS : CHUNKS + 1, :], jnp.zeros((5, LANES), F32)], axis=0
        )


def whole(shape):
    return pl.BlockSpec(shape, lambda *_: (0,) * len(shape))


def by_pair(rows):
    return pl.BlockSpec((rows, LANES), lambda p, *_: (0, p))


VMEM_LIMIT = 56 * 1024 * 1024

TABLES = [
    jax.ShapeDtypeStruct((TOKENS, LANES), F32),
    jax.ShapeDtypeStruct((TOKENS, LANES), BF16),
    jax.ShapeDtypeStruct((PAIRS, 2, TOKENS), F32),
    jax.ShapeDtypeStruct((PAIRS, 2, TOKENS), F32),
    jax.ShapeDtypeStruct((CHUNKS, CHUNK, CHUNK), F32),
]

SCRATCH = [
    pltpu.VMEM((TOKENS, 4 * LANES), F32),
    pltpu.VMEM((STATE, TOKENS), BF16),
]

PARAMETERS = [
    whole((TOKENS, 2 * STATE)),
    whole((HEADS, TOKENS)),
    whole((1, LANES)),
    whole((1, LANES)),
    whole((1, CHANNELS)),
    whole((1, CHANNELS)),
]


def scan_forward(x, g, parameters):
    return pl.pallas_call(
        forward_kernel,
        grid=(PAIRS,),
        in_specs=[
            by_pair(TOKENS),
            by_pair(TOKENS),
        ]
        + PARAMETERS,
        out_specs=[
            whole((CHANNELS, TOKENS)),
            by_pair(TOKENS),
            whole((TOKENS, CHANNELS)),
            pl.BlockSpec((1, CHUNKS - 1, STATE, LANES), lambda p: (p, 0, 0, 0)),
            whole((TOKENS, LANES)),
        ]
        + [whole(one.shape) for one in TABLES],
        out_shape=[
            jax.ShapeDtypeStruct((CHANNELS, TOKENS), BF16),
            jax.ShapeDtypeStruct((TOKENS, CHANNELS), F32),
            jax.ShapeDtypeStruct((TOKENS, CHANNELS), F32),
            jax.ShapeDtypeStruct((PAIRS, CHUNKS - 1, STATE, LANES), F32),
            jax.ShapeDtypeStruct((TOKENS, LANES), F32),
        ]
        + TABLES,
        scratch_shapes=SCRATCH + [pltpu.VMEM((TOKENS, LANES), F32)],
        compiler_params=pltpu.CompilerParams(vmem_limit_bytes=VMEM_LIMIT),
        cost_estimate=pl.CostEstimate(flops=16 * 10**9, bytes_accessed=10**7, transcendentals=0),
        name="scan_forward",
    )(x, g, *parameters)


def scan_backward(x, g, cot, scan, states, scale, pull, parameters, tables):
    return pl.pallas_call(
        backward_kernel,
        grid=(PAIRS,),
        in_specs=[
            by_pair(TOKENS),
            by_pair(TOKENS),
            by_pair(TOKENS),
            by_pair(TOKENS),
            pl.BlockSpec((1, CHUNKS - 1, STATE, LANES), lambda p: (p, 0, 0, 0)),
            whole((TOKENS, LANES)),
            whole((TOKENS, LANES)),
        ]
        + PARAMETERS
        + [whole(one.shape) for one in TABLES],
        out_specs=[
            by_pair(TOKENS),
            by_pair(TOKENS),
            whole((TOKENS, STATE)),
            whole((TOKENS, STATE)),
            whole((HEADS, TOKENS)),
            whole((8, LANES)),
        ],
        out_shape=[
            jax.ShapeDtypeStruct((TOKENS, CHANNELS), BF16),
            jax.ShapeDtypeStruct((TOKENS, CHANNELS), BF16),
            jax.ShapeDtypeStruct((TOKENS, STATE), BF16),
            jax.ShapeDtypeStruct((TOKENS, STATE), BF16),
            jax.ShapeDtypeStruct((HEADS, TOKENS), F32),
            jax.ShapeDtypeStruct((8, LANES), F32),
        ],
        scratch_shapes=SCRATCH
        + [
            pltpu.VMEM((CHUNKS, CHUNK, CHUNK), F32),
            pltpu.VMEM((TOKENS, STATE), F32),
            pltpu.VMEM((TOKENS, STATE), F32),
            pltpu.VMEM((TOKENS, LANES), F32),
            pltpu.VMEM((TOKENS, LANES), F32),
            pltpu.VMEM((8, CHANNELS), F32),
        ],
        compiler_params=pltpu.CompilerParams(vmem_limit_bytes=VMEM_LIMIT),
        cost_estimate=pl.CostEstimate(flops=20 * 10**9, bytes_accessed=10**7, transcendentals=0),
        name="scan_backward",
    )(x, g, cot, scan, states, scale, pull, *parameters, *tables)


FEATURES = 512
BLOCK = 128
SHARDS = 8


def term_kernel(count, added, placed, places, *refs):
    pieces, low_ref = refs[: 2 * count], refs[2 * count]
    sent_refs = refs[2 * count + 1 : -3]
    out_ref, held, done = refs[-3:]
    per = 2 * CHANNELS
    sent = [
        ref.at[start : start + per] for ref in sent_refs for start in range(0, ref.shape[0], per)
    ]
    copies = []
    for k in range(count):
        blocks = [piece[...] for piece in pieces[2 * k : 2 * k + 2]]
        term = dot(low_ref[...], jnp.concatenate(blocks, axis=1))
        for slot in range(2):
            n = 2 * k + slot
            here = slice(n * CHANNELS, (n + 1) * CHANNELS)
            part = term[:, slot * BLOCK : (slot + 1) * BLOCK]
            if added:
                part = part + sent[k][slot * CHANNELS : (slot + 1) * CHANNELS, :].astype(F32)
            held[here, :] = part.astype(BF16)
            start = n * CHANNELS
            if placed:
                start = pl.multiple_of((places[k] * 2 + slot) * CHANNELS, CHANNELS)
            copies.append(
                pltpu.make_async_copy(
                    held.at[here], out_ref.at[pl.ds(start, CHANNELS)], done.at[n]
                )
            )
            copies[-1].start()
    for copy in copies:
        copy.wait()


def terms(places, blocks, pieces, low, sent=()):
    count = len(pieces)
    added = len(sent) > 0
    rows = 2 * CHANNELS * count
    specs = [whole(part.shape) for part in sent]

    def kernel(*refs):
        term_kernel(count, added, added, *refs)

    def lanes(slot):
        return pl.BlockSpec((TOKENS, BLOCK), lambda _, at: (0, at[count + slot]))

    return pl.pallas_call(
        kernel,
        grid_spec=pltpu.PrefetchScalarGridSpec(
            num_scalar_prefetch=1,
            grid=(1,),
            in_specs=[lanes(0), lanes(1)] * count + [whole((CHANNELS, TOKENS))] + specs,
            out_specs=pl.BlockSpec(memory_space=pl.ANY),
            scratch_shapes=[
                pltpu.VMEM((2 * count * CHANNELS, BLOCK), BF16),
                pltpu.SemaphoreType.DMA((2 * count,)),
            ],
        ),
        out_shape=jax.ShapeDtypeStruct((rows, BLOCK), BF16),
        compiler_params=pltpu.CompilerParams(vmem_limit_bytes=VMEM_LIMIT),
        cost_estimate=pl.CostEstimate(
            flops=(count + 1) * 7 * 10**8, bytes_accessed=2 * 10**6, transcendentals=0
        ),
        name="terms_added" if added else "terms",
    )(
        jnp.stack(list(places) + list(blocks)).astype(jnp.int32),
        *[piece for piece in pieces for _ in range(2)],
        low,
        *sent,
    )


def finish_kernel(scale, kept_ref, given_ref, out_ref):
    total = kept_ref[...].astype(F32) + given_ref[...].astype(F32)
    out_ref[...] = (total * scale).T


def finish(plane, given, scale):
    return pl.pallas_call(
        lambda *refs: finish_kernel(scale, *refs),
        grid=(1,),
        in_specs=[pl.BlockSpec((CHANNELS, BLOCK), lambda _: (1, 0)), whole((CHANNELS, BLOCK))],
        out_specs=whole((BLOCK, CHANNELS)),
        out_shape=jax.ShapeDtypeStruct((BLOCK, CHANNELS), F32),
        cost_estimate=pl.CostEstimate(flops=4 * 10**9, bytes_accessed=10**6, transcendentals=0),
        name="finish",
    )(plane, given)


COLUMNS = 256


def product_kernel(places, *refs):
    pieces = refs[:SHARDS]
    rows_ref, gated_ref, scale_ref, gain_ref = refs[SHARDS : SHARDS + 4]
    cot_ref, gain_grad_ref, pull_ref, sums = refs[SHARDS + 4 :]
    step = pl.program_id(0)
    starts = [pl.multiple_of(places[k] * FEATURES, FEATURES) for k in range(SHARDS)]
    cot_ref[...] = dot(
        jnp.concatenate([piece[...] for piece in pieces], axis=1),
        jnp.concatenate([rows_ref[pl.ds(start, FEATURES), :] for start in starts], axis=0),
    )

    @pl.when(step == 0)
    def _():
        sums[...] = jnp.zeros_like(sums)

    scale = scale_ref[...]
    for half in range(COLUMNS // LANES):
        cols = slice(half * LANES, (half + 1) * LANES)
        with_gated = cot_ref[:, cols] * gated_ref[:, cols]
        gain_grad_ref[:, cols] = jnp.sum(with_gated * scale, axis=0, keepdims=True)
        sums[...] += with_gated * gain_ref[:, cols]

    @pl.when(step == pl.num_programs(0) - 1)
    def _():
        pulled = jnp.sum(sums[...], axis=1, keepdims=True) * (1.0 / CHANNELS)
        pull_ref[...] = scale * scale * scale * pulled


def products(places, pieces, rows, gated, scale, gain):
    depth = SHARDS * FEATURES
    return pl.pallas_call(
        product_kernel,
        grid_spec=pltpu.PrefetchScalarGridSpec(
            num_scalar_prefetch=1,
            grid=(CHANNELS // COLUMNS,),
            in_specs=[whole((TOKENS, FEATURES))] * SHARDS
            + [
                pl.BlockSpec((depth, COLUMNS), lambda n, *_: (0, n)),
                pl.BlockSpec((TOKENS, COLUMNS), lambda n, *_: (0, n)),
                whole((TOKENS, LANES)),
                pl.BlockSpec((1, COLUMNS), lambda n, *_: (0, n)),
            ],
            out_specs=[
                pl.BlockSpec((TOKENS, COLUMNS), lambda n, *_: (0, n)),
                pl.BlockSpec((1, COLUMNS), lambda n, *_: (0, n)),
                whole((TOKENS, LANES)),
            ],
            scratch_shapes=[pltpu.VMEM((TOKENS, LANES), F32)],
        ),
        out_shape=[
            jax.ShapeDtypeStruct((TOKENS, CHANNELS), F32),
            jax.ShapeDtypeStruct((1, CHANNELS), F32),
            jax.ShapeDtypeStruct((TOKENS, LANES), F32),
        ],
        compiler_params=pltpu.CompilerParams(vmem_limit_bytes=VMEM_LIMIT),
        cost_estimate=pl.CostEstimate(
            flops=12 * 10**9, bytes_accessed=16 * 10**6, transcendentals=0
        ),
        name="products",
    )(places, *pieces, rows, gated, scale, gain)


def along_x(step):
    return [(x * 2 + h, (x + step) % 4 * 2 + h) for x in range(4) for h in range(2)]


def beside(shard):
    return lax.ppermute(shard, "tp", along_x(1)), lax.ppermute(shard, "tp", along_x(-1))


def beyond(before, after):
    half = before.shape[0] // 2
    top = lax.ppermute(before[:half], "tp", along_x(1))
    low = lax.ppermute(after[half:], "tp", along_x(-1))
    return top, low


def swap(bit):
    return [(b, b ^ bit) for b in range(32)]


def local_parameters(state_proj, step_raw, log_rate, step_bias, skip_gain, norm_gain):
    def padded(v):
        return jnp.pad(v, (0, LANES - HEADS)).reshape(1, LANES)

    return (
        state_proj.reshape(TOKENS, 2 * STATE),
        step_raw.T,
        padded(step_bias),
        padded(log_rate),
        jnp.repeat(skip_gain, WIDTH).reshape(1, CHANNELS),
        norm_gain.reshape(1, CHANNELS),
    )


def shards(
    scan_input,
    gate_input,
    state_proj,
    step_raw,
    log_rate,
    step_bias,
    skip_gain,
    norm_gain,
    out_proj,
    out_cotangent,
):
    norm_scale = 1.0 / math.sqrt(TOKENS * 32)
    block = lax.axis_index("blk")
    core, y_lo = block % 2, block // 2 % 2
    by_z = [[z * 4 + rest for z in range(8)] for rest in range(4)]
    rows = lax.all_gather(out_proj, "blk", axis=0, tiled=True)
    own = out_cotangent
    partner = lax.ppermute(own, "tp", [(t, t ^ 1) for t in range(8)])
    before, after = beside(own)
    partner, before, after, scan_input = lax.optimization_barrier(
        (partner, before, after, scan_input)
    )
    partner_before, partner_after = beside(partner)
    far_parts = beyond(before, after)

    parameters = local_parameters(
        state_proj, step_raw, log_rate, step_bias, skip_gain, norm_gain
    )
    low, scan, gated, states, scale, *tables = scan_forward(scan_input, gate_input, parameters)
    partner_before, partner_after, far_parts, low = lax.optimization_barrier(
        (partner_before, partner_after, far_parts, low)
    )
    far = jnp.concatenate(far_parts, axis=0)
    partner_far = beyond(partner_before, partner_after)
    early = [own, before, after, far, partner, partner_before, partner_after]
    me = lax.axis_index("tp")
    x, h = me // 2, me % 2
    places = [(x + shift) % 4 * 2 + row for row in (h, 1 - h) for shift in (0, 3, 1, 2)]

    mine, mine_y = 2 * y_lo + core, 2 * (1 - y_lo) + core
    theirs, theirs_y = 2 * y_lo + 1 - core, 2 * (1 - y_lo) + 1 - core

    theirs_early = terms(places[:-1], (theirs_y, theirs), early, low)
    theirs_early, partner_far = lax.optimization_barrier((theirs_early, partner_far))
    sent_early = lax.ppermute(theirs_early, "blk", swap(1))
    last = [jnp.concatenate(partner_far, axis=0)]
    sent_last = lax.ppermute(terms(places[-1:], (theirs_y, theirs), last, low), "blk", swap(1))
    both = terms(places, (mine_y, mine), early + last, low, (sent_early, sent_last))
    plane = lax.psum_scatter(
        both, "blk", scatter_dimension=0, tiled=True, axis_index_groups=by_z
    )
    rows, _ = lax.optimization_barrier((rows, both))
    cot, gain_grad, pull = products(
        jnp.stack(places).astype(jnp.int32),
        early + last,
        rows,
        gated,
        scale,
        parameters[-1],
    )
    dx, dg, db, dc, step_grad, small = scan_backward(
        scan_input, gate_input, cot, scan, states, scale, pull, parameters, tables
    )
    summed = jnp.concatenate([small, gain_grad.reshape(8, LANES)], axis=0)
    for bit in (1, 4, 8, 16):
        summed = summed + lax.ppermute(summed, "blk", swap(bit))
    state_grad = jnp.stack([db, dc], axis=1)
    plane, summed, state_grad = lax.optimization_barrier((plane, summed, state_grad))
    given = lax.ppermute(plane[:CHANNELS], "blk", swap(2))
    summed = summed + lax.ppermute(summed, "blk", swap(2))
    given, summed = lax.optimization_barrier((given, summed))
    weight_grad = finish(plane, given, norm_scale)
    summed = summed * norm_scale
    return (
        dx,
        dg,
        state_grad,
        step_grad.T,
        weight_grad,
        summed[0, :HEADS],
        summed[1, :HEADS],
        summed[2, :HEADS],
        summed[8:].reshape(CHANNELS),
    )


def solution(mesh):
    placed = (
        P("blk", "tp"),
        P("blk", "tp"),
        P("blk", None, "tp"),
        P("blk", "tp"),
        P("tp"),
        P("tp"),
        P("tp"),
        P("tp"),
        P("blk", "tp"),
        P("blk", "tp"),
    )
    return jax.shard_map(
        shards,
        mesh=mesh,
        in_specs=placed,
        out_specs=(
            P("blk", "tp"),
            P("blk", "tp"),
            P("blk", None, "tp"),
            P("blk", "tp"),
            P("blk", "tp"),
            P("tp"),
            P("tp"),
            P("tp"),
            P("tp"),
        ),
        check_vma=False,
    )
```
